32 devices in a mesh: dp: 16 (over z, y, x), mp: 2 (over core).
Axes of the slice: x: 2, y: 2, z: 4, core: 2. Of those that a mesh axis runs over, the one named last changes fastest.
Arguments:
- pixels: bfloat16 [2, 64, 384, 324], P(None, ('dp', 'mp')), may hold values from -6 to 6
- grid_class: int32 [2, 64], P(None, 'dp'), may hold values from 0 to 2
- extent: int32 [384], P('mp'), may hold values from 1 to 18
- ssm_rate: float32 [2, 384, 64], P(None, 'mp'), may hold values from 0.5 to 20
- ssm_freq: float32 [2, 384, 64], P(None, 'mp'), may hold values from 0 to 8
- ssm_coef: float32 [2, 384, 64], P(None, 'mp'), may hold values from -0.75 to 0.75
- skip_gain: float32 [384], P('mp'), may hold values from -4 to 4
- norm_gain: float32 [384], replicated, may hold values from 0.5 to 1.5
- norm_bias: float32 [384], replicated, may hold values from -3 to 3
- w_in: bfloat16 [384, 1536], P(None, 'mp'), may hold values from -0.3125 to 0.3125
- b_in: float32 [1536], P('mp'), may hold values from -3 to 3
- w_out: bfloat16 [1536, 384], P('mp'), may hold values from -0.15625 to 0.15625
- b_out: float32 [384], replicated, may hold values from -3 to 3
- layer_scale: float32 [384], replicated, may hold values from 0.5 to 1.5
- cotangent: bfloat16 [2, 64, 384, 324], P(None, ('dp', 'mp')), may hold values from -6 to 6
Outputs:
- block_out: bfloat16 [2, 64, 384, 324], P(None, ('dp', 'mp'))
- pixels_grad: bfloat16 [2, 64, 384, 324], P(None, ('dp', 'mp'))
- rate_grad: float32 [2, 384, 64], P(None, 'mp')
- freq_grad: float32 [2, 384, 64], P(None, 'mp')
- coef_grad: float32 [2, 384, 64], P(None, 'mp')
- skip_grad: float32 [384], P('mp')
- gain_grad: float32 [384], replicated
- bias_grad: float32 [384], replicated
- w_in_grad: float32 [384, 1536], P(None, 'mp')
- b_in_grad: float32 [1536], P('mp')
- w_out_grad: float32 [1536, 384], P('mp')
- b_out_grad: float32 [384], replicated
- scale_grad: float32 [384], replicated
The draws below stay inside these ranges and needn't reach their ends.
All inputs are finite; a program needn't handle non-finite values.
Results may differ from the reference program's by a relative error of at most 0.012.
Values may be sent and summed in bfloat16 or wider, within the bound.
A program may use at most 256 MiB of HBM per device.

```python
import math
import jax
import jax.numpy as jnp
import numpy as np
from jax import lax

C = 384
FF = 1536
NSTATE = 64
GRID = 18
MICRO = 2
PIX = 324
IMGS = 64


def touch_ends(array, own_key, least, largest):
    longest = array.shape.index(max(array.shape))
    spots = []
    for shift in (0, 1):
        where = [jax.random.randint(jax.random.fold_in(own_key, axis), (), 0, length) for axis, length in enumerate(array.shape)]
        where[longest] = (where[longest] + shift) % array.shape[longest]
        spots.append(tuple(where))
    return array.at[spots[0]].set(least).at[spots[1]].set(largest)


def level_of(rng, shape, cuts, low, largest):
    gain, own = 1.0, jax.random.fold_in(rng, 6)
    for axis_at, blocks in cuts:
        draws = jnp.exp(jax.random.uniform(jax.random.fold_in(own, axis_at), (blocks,), jnp.float32, low / len(cuts), largest / len(cuts)))
        gain = gain * jnp.repeat(draws, shape[axis_at] // blocks).reshape([-1 if axis == axis_at else 1 for axis in range(len(shape))])
    return gain


def normal_values(stream_key, dims, width, limit, split=(), kind=jnp.bfloat16):
    values = width * jax.random.normal(stream_key, dims, jnp.float32)
    if split:
        values = values * level_of(stream_key, dims, split, -0.22, 0.18)
    return jnp.clip(values, -limit, limit).astype(kind)


def setup_inputs(seed: int = 0) -> dict:
    keys = jax.random.split(jax.random.key(seed), 16)
    return {
        "pixels": normal_values(keys[0], (MICRO, IMGS, C, PIX), 1.0, 6.0, ((1, 32),)),
        "grid_class": touch_ends(jax.random.randint(keys[1], (MICRO, IMGS), 0, 3), jax.random.fold_in(keys[1], 1), 0, 2).astype(jnp.int32),
        "extent": touch_ends(jax.random.randint(keys[2], (C,), 1, GRID + 1), jax.random.fold_in(keys[2], 1), 1, GRID).astype(jnp.int32),
        "ssm_rate": jnp.clip(jnp.exp(math.log(20.0) - 3.6888795 * jax.random.uniform(keys[3], (2, C, NSTATE), jnp.float32) ** level_of(keys[3], (2, C, NSTATE), ((1, 2),), -0.2, 0.2)), 0.5, 20.0),
        "ssm_freq": jnp.clip(8.0 * jax.random.uniform(keys[4], (2, C, NSTATE), jnp.float32) ** level_of(keys[4], (2, C, NSTATE), ((1, 2),), -0.2, 0.2), 0.0, 8.0),
        "ssm_coef": normal_values(keys[5], (2, C, NSTATE), NSTATE ** -0.5, 0.75, ((1, 2),), jnp.float32),
        "skip_gain": normal_values(keys[6], (C,), 1.0, 4.0, ((0, 2),), jnp.float32),
        "norm_gain": jnp.clip(1.0 + 0.1 * jax.random.normal(keys[7], (C,), jnp.float32), 0.5, 1.5),
        "norm_bias": normal_values(keys[8], (C,), 0.5, 3.0, (), jnp.float32),
        "w_in": normal_values(keys[9], (C, FF), C ** -0.5, 0.3125, ((1, 2),)),
        "b_in": normal_values(keys[10], (FF,), 0.5, 3.0, ((0, 2),), jnp.float32),
        "w_out": normal_values(keys[11], (FF, C), FF ** -0.5, 0.15625, ((0, 2),)),
        "b_out": normal_values(keys[12], (C,), 0.5, 3.0, (), jnp.float32),
        "layer_scale": jnp.clip(jax.random.uniform(keys[13], (C,), jnp.float32, 0.5, 1.5), 0.5, 1.5),
        "cotangent": normal_values(keys[14], (MICRO, IMGS, C, PIX), 1.0, 6.0, ((1, 32),)),
    }


HIGH = lax.Precision.HIGHEST

@jax.custom_vjp
def low(v):
    return lax.optimization_barrier(v.astype(jnp.bfloat16)).astype(jnp.float32)

@jax.custom_vjp
def low_back(v):
    return v

def low_keep(v):
    return (low(v), None)

def low_pass(kept, grad):
    return (grad,)

def back_keep(v):
    return (v, None)

def back_low(kept, grad):
    return (low(grad),)
low.defvjp(low_keep, low_pass)
low_back.defvjp(back_keep, back_low)

def lag_selector():
    positions = np.arange(GRID)
    distance = np.abs(positions[:, None] - positions[None, :])
    return (distance[None, :, :] == positions[:, None, None]).astype(np.float32)

def kernel_tables(decay_rate, frequency, coef_in, extent):
    lag_values = jnp.arange(GRID, dtype=jnp.float32)
    lag_whole = jnp.arange(GRID, dtype=jnp.int32)
    selector = jnp.asarray(lag_selector())
    tables = []
    for category in range(3):
        grid_side = 10 + 4 * category
        scaled = lag_values / grid_side
        wave_terms = jnp.exp(-decay_rate[..., None] * scaled) * jnp.cos(frequency[..., None] * scaled)
        kernel_row = lax.optimization_barrier(jnp.sum(coef_in[..., None] * wave_terms, axis=2))
        within = (lag_whole[None, None, :] < extent.astype(jnp.int32)[None, :, None]) & (lag_whole[None, None, :] < grid_side)
        kernel_row = jnp.where(within, kernel_row, 0.0)
        toeplitz = jnp.einsum('acl,lip->acip', kernel_row, selector, precision=HIGH)
        inside = np.arange(GRID) < grid_side
        square_mask = (inside[:, None] & inside[None, :]).astype(np.float32)
        tables.append(toeplitz * jnp.asarray(square_mask))
    return jnp.stack(tables)

def mix_channels(field_in, classes, decay_rate, frequency, coef_in, skip_in, extent):
    tables = kernel_tables(decay_rate, frequency, coef_in, extent)
    onehot = (classes[:, None] == jnp.arange(3, dtype=jnp.int32)[None, :]).astype(jnp.float32)
    rows_op = jnp.einsum('nk,kcip->ncip', onehot, tables[:, 0], precision=HIGH)
    cols_op = jnp.einsum('nk,kcip->ncip', onehot, tables[:, 1], precision=HIGH)
    count = field_in.shape[0]
    channels = field_in.shape[1]
    grid_view = field_in.reshape(count, channels, GRID, GRID)
    partial_rows = jnp.einsum('ncip,ncpq->nciq', rows_op, grid_view, precision=HIGH)
    mixed_out = jnp.einsum('nciq,ncjq->ncij', partial_rows, cols_op, precision=HIGH)
    mixed_out = mixed_out + skip_in[None, :, None, None] * grid_view
    return mixed_out.reshape(count, channels, GRID * GRID)

def layer_norm(field_in, gain_in, bias_in):
    channel_mean = lax.optimization_barrier(jnp.mean(field_in, axis=1, keepdims=True))
    centered = field_in - channel_mean
    variance = lax.optimization_barrier(jnp.mean(centered * centered, axis=1, keepdims=True))
    return centered * lax.rsqrt(variance + 1e-06) * gain_in[None, :, None] + bias_in[None, :, None]

def pixel_mask(classes):
    grid_side = 10 + 4 * classes.astype(jnp.int32)
    pixel_index = jnp.arange(GRID * GRID, dtype=jnp.int32)
    pixel_row = pixel_index // GRID
    pixel_col = pixel_index % GRID
    valid = (pixel_row[None, :] < grid_side[:, None]) & (pixel_col[None, :] < grid_side[:, None])
    return valid.astype(jnp.float32)[:, None, :]

def block_forward(params, field_in, classes, extent):
    decay_rate, frequency, coef_in, skip_in, gain_in, bias_in, w_first, b_first, w_second, b_second, scale_in = params
    source = low_back(field_in)
    mixed_out = mix_channels(source, classes, decay_rate, frequency, coef_in, skip_in, extent)
    mixed_out = low(low_back(mixed_out))
    normed = low(layer_norm(mixed_out, gain_in, bias_in))
    pre_act = jnp.einsum('ncp,cf->nfp', normed, w_first, precision=HIGH) + b_first[None, :, None]
    pre_act = low_back(pre_act)
    activated = low(jax.nn.gelu(pre_act, approximate=False))
    mlp_out = low_back(jnp.einsum('nfp,fc->ncp', activated, w_second, precision=HIGH) + b_second[None, :, None])
    return field_in + scale_in[None, :, None] * mlp_out * pixel_mask(classes)

def reference(pixels, grid_class, extent, ssm_rate, ssm_freq, ssm_coef, skip_gain, norm_gain, norm_bias, w_in, b_in, w_out, b_out, layer_scale, cotangent):
    params = (ssm_rate, ssm_freq, ssm_coef, skip_gain, norm_gain, norm_bias, w_in.astype(jnp.float32), b_in, w_out.astype(jnp.float32), b_out, layer_scale)
    block_images = 8
    fields = pixels.reshape(-1, block_images, C, PIX)
    class_blocks = grid_class.reshape(-1, block_images)
    cot_blocks = cotangent.reshape(-1, block_images, C, PIX)
    zeros_tree = jax.tree.map(jnp.zeros_like, params)

    def scan_step(running, inputs_block):
        field_blk, class_blk, cot_blk = inputs_block

        def forward(param_set, field_in):
            return block_forward(param_set, field_in, class_blk, extent)
        result, backward = jax.vjp(forward, params, field_blk.astype(jnp.float32))
        grad_params, grad_field = backward(cot_blk.astype(jnp.float32))
        running = jax.tree.map(lambda left, right: left + right, running, grad_params)
        return (running, (result.astype(jnp.bfloat16), grad_field.astype(jnp.bfloat16)))
    gradients, (outputs, input_grads) = lax.scan(scan_step, zeros_tree, (fields, class_blocks, cot_blocks))
    return (outputs.reshape(pixels.shape), input_grads.reshape(pixels.shape), gradients[0], gradients[1], gradients[2], gradients[3], gradients[4], gradients[5], gradients[6], gradients[7], gradients[8], gradients[9], gradients[10])
```

```python
import math
from functools import partial

import jax
import jax.numpy as jnp
import numpy as np
from jax import lax
from jax.experimental import pallas as pl
from jax.experimental.pallas import tpu as pltpu
from jax.sharding import PartitionSpec as P

GRID = 18
HALF = 9
SIDES = (10, 14, 18)
LAGS = 3 * GRID
F32 = jnp.float32
BF16 = jnp.bfloat16

ERF_SHIFT = 0.35 / math.sqrt(2.0)
ERF_POLY = (
    0.19396706,
    0.23864529,
    -0.01708609,
    0.69839275,
    -0.6929918,
    0.77818103,
    -0.19910822,
)
VMEM_LIMIT = 60 * 1024 * 1024


def small_sincos(angle):
    sq = angle * angle
    cos = 1.0 + sq * (
        -1 / 2 + sq * (1 / 24 + sq * (-1 / 720 + sq * (1 / 40320 + sq * (-1 / 3628800))))
    )
    sin = angle * (
        1.0
        + sq * (-1 / 6 + sq * (1 / 120 + sq * (-1 / 5040 + sq * (1 / 362880 + sq * (-1 / 39916800)))))
    )
    return sin, cos


def mode_step(rate, freq, side):
    decay = jnp.exp(rate * (-1.0 / side))
    sin, cos = small_sincos(freq * (1.0 / side))
    return decay * cos, decay * sin


def tables_kernel(extent_ref, rate_ref, freq_ref, coef_ref, out_ref):
    for axis in range(2):
        for cat, side in enumerate(SIDES):
            z_re, z_im = mode_step(rate_ref[axis], freq_ref[axis], side)
            w_re = coef_ref[axis]
            w_im = jnp.zeros_like(w_re)
            for lag in range(GRID):
                row = cat * GRID + lag
                if lag >= side:
                    out_ref[axis, row : row + 1, :] = jnp.zeros((1, w_re.shape[1]), F32)
                    continue
                total = jnp.sum(w_re, axis=0, keepdims=True)
                out_ref[axis, row : row + 1, :] = jnp.where(extent_ref[...] > lag, total, 0.0)
                if lag < side - 1:
                    w_re, w_im = w_re * z_re - w_im * z_im, w_re * z_im + w_im * z_re


def modes_grad_kernel(extent_ref, rate_ref, freq_ref, coef_ref, dk_ref, rate_out, freq_out, coef_out):
    for axis in range(2):
        coef = coef_ref[axis]
        g_rate = jnp.zeros_like(coef)
        g_freq = jnp.zeros_like(coef)
        g_coef = jnp.zeros_like(coef)
        for cat, side in enumerate(SIDES):
            z_re, z_im = mode_step(rate_ref[axis], freq_ref[axis], side)
            p_re = jnp.zeros_like(coef)
            p_im = jnp.zeros_like(coef)
            q_re = jnp.zeros_like(coef)
            q_im = jnp.zeros_like(coef)
            for lag in reversed(range(side)):
                row = cat * GRID + lag
                d = jnp.where(extent_ref[...] > lag, dk_ref[axis, row : row + 1, :], 0.0)
                p_re, p_im = p_re * z_re - p_im * z_im + d, p_re * z_im + p_im * z_re
                q_re, q_im = q_re * z_re - q_im * z_im + float(lag) * d, q_re * z_im + q_im * z_re
            g_coef = g_coef + p_re
            g_rate = g_rate - (1.0 / side) * q_re
            g_freq = g_freq - (1.0 / side) * q_im
        coef_out[axis] = g_coef
        rate_out[axis] = g_rate * coef
        freq_out[axis] = g_freq * coef


def tri(a, b):
    low, high = min(a, b), max(a, b)
    return low * HALF - low * (low - 1) // 2 + (high - low)


def rows8(index):
    if isinstance(index, int):
        return pl.ds(index * 8, 8)
    return pl.ds(pl.multiple_of(index * 8, 8), 8)


def lanes(tile):
    if isinstance(tile, int):
        return pl.ds(tile * 128, 128)
    return pl.ds(pl.multiple_of(tile * 128, 128), 128)


def swap(value):
    return pltpu.roll(value, 4, 0)


def sublane_half():
    return lax.broadcasted_iota(jnp.int32, (8, 128), 0) < 4


def side_vreg(class_ref):
    mine = lax.axis_index("mp")
    image = lax.rem(lax.broadcasted_iota(jnp.int32, (8, 128), 0), 4)
    cls = jnp.zeros((8, 128), jnp.int32)
    own = class_ref.shape[1] // 2
    for micro in range(2):
        for img in range(2):
            cls = jnp.where(image == micro * 2 + img, class_ref[micro, mine * own + img], cls)
    return 10 + 4 * cls


def build_masks(class_ref, mask_ref):
    side = side_vreg(class_ref)
    offset = jnp.where(sublane_half(), 0, 1)

    def row(i, carry):
        for pair in range(HALF):
            ok = (i < side) & (2 * pair + offset < side)
            mask_ref[rows8(i * HALF + pair), :] = jnp.where(ok, 1.0, 0.0).astype(F32)
        return carry

    lax.fori_loop(0, GRID, row, 0)


def build_operators(class_ref, table_ref, lag_ref, rowop_ref, colop_ref):
    side = side_vreg(class_ref)
    sign = jnp.where(sublane_half(), 1.0, -1.0).astype(F32)
    tiles = table_ref.shape[2] // 128

    def tile_body(tile, carry):
        at = lanes(tile)
        for axis in range(2):
            for lag in range(GRID):
                by_side = [
                    jnp.broadcast_to(table_ref[axis, cat * GRID + lag : cat * GRID + lag + 1, at], (8, 128))
                    for cat in range(3)
                ]
                lag_ref[axis * GRID + lag, :, at] = 0.5 * jnp.where(
                    side == 10, by_side[0], jnp.where(side == 14, by_side[1], by_side[2])
                )
        for a in range(HALF):
            for b in range(a, HALF):
                near = lag_ref[b - a, :, at]
                far = lag_ref[GRID - 1 - a - b, :, at]
                rowop_ref[tri(a, b), :, at] = near + far
                rowop_ref[45 + tri(a, b), :, at] = near - far
                near = lag_ref[GRID + b - a, :, at]
                far = lag_ref[GRID + GRID - 1 - a - b, :, at]
                colop_ref[tri(a, b), :, at] = near + sign * far
        return carry

    lax.fori_loop(0, tiles, tile_body, 0)


def mirror_in(source_ref, mask_ref, out_ref):
    half = sublane_half()
    sign = jnp.where(half, 1.0, -1.0).astype(F32)
    tiles = source_ref.shape[1] // 128

    def body(i, carry):
        for tile in range(tiles):
            at = lanes(tile)

            def mirrored(row, pair):
                near = source_ref[rows8(row * HALF + pair), at] * mask_ref[rows8(row * HALF + pair), :]
                if pair == 4:
                    return swap(near) + sign * near, None
                other = row * HALF + 8 - pair
                far = source_ref[rows8(other), at] * mask_ref[rows8(other), :]
                even = jnp.where(half, near, far)
                odd = jnp.where(half, far, near)
                return swap(even) + sign * even, odd + sign * swap(odd)

            for pair in range(5):
                top = mirrored(i, pair)
                bottom = mirrored(GRID - 1 - i, pair)
                for step in range(2 if pair < 4 else 1):
                    where = i * HALF + 2 * pair + step
                    out_ref[rows8(where), at] = top[step] + bottom[step]
                    out_ref[rows8(81 + where), at] = top[step] - bottom[step]
        return carry

    lax.fori_loop(0, HALF, body, 0)


def mirror_out(source_ref, mask_ref, out_ref, extra_ref, gain_ref):
    half = sublane_half()
    sign = jnp.where(half, 1.0, -1.0).astype(F32)
    tiles = source_ref.shape[1] // 128

    def body(i, carry):
        for tile in range(tiles):
            at = lanes(tile)
            gain = jnp.broadcast_to(gain_ref[:, at], (8, 128))

            def finish(index, value):
                value = value * mask_ref[rows8(index), :] + gain * extra_ref[rows8(index), at]
                out_ref[rows8(index), at] = value.astype(BF16).astype(F32)

            for pair in range(5):
                both = []
                for step in range(2 if pair < 4 else 1):
                    where = i * HALF + 2 * pair + step
                    plus = source_ref[rows8(where), at]
                    minus = source_ref[rows8(81 + where), at]
                    top, bottom = plus + minus, plus - minus
                    both.append(
                        (swap(top) + sign * top, swap(bottom) + sign * bottom)
                        if step == 0
                        else (top - sign * swap(top), bottom - sign * swap(bottom))
                    )
                for part, row in ((0, i), (1, GRID - 1 - i)):
                    if pair == 4:
                        finish(row * HALF + 4, both[0][part])
                        continue
                    if True:
                        even, odd = both[0][part], both[1][part]
                        finish(row * HALF + pair, jnp.where(half, even, odd))
                        finish(row * HALF + 8 - pair, jnp.where(half, odd, even))
        return carry

    lax.fori_loop(0, HALF, body, 0)


def apply_rows(op_ref, source_ref, out_ref):
    tiles = source_ref.shape[1] // 128

    def body(j, carry):
        for tile in range(tiles):
            at = lanes(tile)
            for rho in range(2):
                values = [source_ref[rows8(rho * 81 + p * HALF + j), at] for p in range(HALF)]
                for i in range(HALF):
                    total = None
                    for p in range(HALF):
                        term = op_ref[rho * 45 + tri(i, p), :, at] * values[p]
                        total = term if total is None else total + term
                    out_ref[rows8(rho * 81 + i * HALF + j), at] = total
        return carry

    lax.fori_loop(0, HALF, body, 0)


def apply_cols(op_ref, source_ref, out_ref):
    tiles = source_ref.shape[1] // 128

    def body(i, carry):
        for tile in range(tiles):
            at = lanes(tile)
            values = [source_ref[rows8(i * HALF + q), at] for q in range(HALF)]
            for j in range(HALF):
                total = None
                for q in range(HALF):
                    term = op_ref[tri(j, q), :, at] * values[q]
                    total = term if total is None else total + term
                out_ref[rows8(i * HALF + j), at] = total
        return carry

    lax.fori_loop(0, 2 * HALF, body, 0)


def front_kernel(
    class_ref,
    table_ref,
    x_ref,
    cot_ref,
    skip_ref,
    gain_ref,
    bias_ref,
    w_in_ref,
    b_in_ref,
    w_out_ref,
    b_out_ref,
    scale_ref,
    block_out,
    gm_out,
    u_out,
    uh_out,
    v_out,
    rowop_out,
    colop_out,
    mask_out,
    dw_in_out,
    dw_out_out,
    db_in_out,
    small_out,
    lag_ref,
    mh_ref,
    mixed_ref,
    normed_ref,
    gmlp_ref,
    act_ref,
    gpre_ref,
    mlp_ref,
    gn_ref,
    stat_ref,
):
    rows, channels = x_ref.shape
    hidden = b_in_ref.shape[1]
    build_masks(class_ref, mask_out)
    build_operators(class_ref, table_ref, lag_ref, rowop_out, colop_out)

    block = 144

    def load(t, carry):
        at = pl.ds(pl.multiple_of(t * block, block), block)
        u_out[at, :] = x_ref[at, :].astype(F32)
        mask = jnp.tile(mask_out[at, :], (1, channels // 128))
        gmlp_ref[at, :] = (cot_ref[at, :].astype(F32) * scale_ref[...] * mask).astype(BF16)
        return carry

    lax.fori_loop(0, rows // block, load, 0)
    mirror_in(u_out, mask_out, uh_out)
    apply_rows(rowop_out, uh_out, v_out)
    apply_cols(colop_out, v_out, mh_ref)
    mirror_out(mh_ref, mask_out, mixed_ref, u_out, skip_ref)

    def norm(t, carry):
        at = pl.ds(pl.multiple_of(t * block, block), block)
        value = mixed_ref[at, :]
        mean = jnp.mean(value, axis=1, keepdims=True)
        centered = value - mean
        variance = jnp.mean(centered * centered, axis=1, keepdims=True)
        rstd = lax.rsqrt(variance + 1e-06)
        hat = centered * rstd
        mixed_ref[at, :] = hat
        stat_ref[at, :] = jnp.broadcast_to(rstd, (block, 128))
        normed_ref[at, :] = (hat * gain_ref[...] + bias_ref[...]).astype(BF16)
        return carry

    lax.fori_loop(0, rows // block, norm, 0)

    chunk = 256
    tile_rows = 432
    mlp_ref[...] = jnp.broadcast_to(b_out_ref[...], mlp_ref.shape)
    gn_ref[...] = jnp.zeros_like(gn_ref)

    def feed(f, carry):
        cols = pl.ds(pl.multiple_of(f * chunk, chunk), chunk)
        w_first = w_in_ref[:, cols]
        w_second = w_out_ref[cols, :]
        bias = b_in_ref[:, cols]
        db = jnp.zeros((1, chunk), F32)
        for t in range(rows // tile_rows):
            at = pl.ds(t * tile_rows, tile_rows)
            pre = jnp.dot(normed_ref[at, :], w_first, preferred_element_type=F32) + bias
            size = jnp.abs(pre)
            inv = 1.0 / (1.0 + ERF_SHIFT * size)
            poly = jnp.full_like(inv, 0.5 * ERF_POLY[-1])
            for value in reversed(ERF_POLY[:-1]):
                poly = poly * inv + 0.5 * value
            bell = jnp.exp(-0.5 * pre * pre)
            tail = poly * inv * bell
            cdf = jnp.where(pre >= 0.0, 1.0 - tail, tail)
            act = (pre * cdf).astype(BF16)
            slope = cdf + pre * bell * (1.0 / math.sqrt(2.0 * math.pi))
            g_act = lax.dot_general(
                gmlp_ref[at, :], w_second, (((1,), (1,)), ((), ())), preferred_element_type=F32
            )
            g_pre = (g_act * slope).astype(BF16)
            db = db + jnp.sum(g_pre.astype(F32), axis=0, keepdims=True)
            act_ref[at, :] = act
            gpre_ref[at, :] = g_pre
            mlp_ref[at, :] += jnp.dot(act, w_second, preferred_element_type=F32)
            gn_ref[at, :] += lax.dot_general(
                g_pre, w_first, (((1,), (1,)), ((), ())), preferred_element_type=F32
            )
        db_in_out[:, cols] = db
        dw_in_out[:, cols] = lax.dot_general(
            normed_ref[...], gpre_ref[...], (((0,), (0,)), ((), ())), preferred_element_type=F32
        )
        dw_out_out[cols, :] = lax.dot_general(
            act_ref[...], gmlp_ref[...], (((0,), (0,)), ((), ())), preferred_element_type=F32
        )
        return carry

    lax.fori_loop(0, hidden // chunk, feed, 0)

    def back(t, carry):
        d_gain, d_bias, d_scale, d_b_out = carry
        at = pl.ds(pl.multiple_of(t * block, block), block)
        mask = jnp.tile(mask_out[at, :], (1, channels // 128))
        branch = mlp_ref[at, :] * mask
        block_out[at, :] = (u_out[at, :] + scale_ref[...] * branch).astype(BF16)
        d_scale = d_scale + jnp.sum(cot_ref[at, :].astype(F32) * branch, axis=0, keepdims=True)
        d_b_out = d_b_out + jnp.sum(gmlp_ref[at, :].astype(F32), axis=0, keepdims=True)
        grad = gn_ref[at, :]
        hat = mixed_ref[at, :]
        d_gain = d_gain + jnp.sum(grad * hat, axis=0, keepdims=True)
        d_bias = d_bias + jnp.sum(grad, axis=0, keepdims=True)
        grad = grad * gain_ref[...]
        mean_g = jnp.mean(grad, axis=1, keepdims=True)
        mean_gh = jnp.mean(grad * hat, axis=1, keepdims=True)
        rstd = jnp.tile(stat_ref[at, :], (1, channels // 128))
        gm_out[at, :] = (rstd * (grad - mean_g - hat * mean_gh)).astype(BF16).astype(F32)
        return d_gain, d_bias, d_scale, d_b_out

    zero = jnp.zeros((1, channels), F32)
    sums = lax.fori_loop(0, rows // block, back, (zero, zero, zero, zero))
    for index, value in enumerate(sums):
        small_out[index : index + 1, :] = value


def back_kernel(
    class_ref,
    gm_ref,
    cot_ref,
    u_ref,
    uh_ref,
    v_ref,
    rowop_ref,
    colop_ref,
    mask_ref,
    skip_ref,
    dx_out,
    dk_out,
    dskip_out,
    gh_ref,
    x_ref,
    row_acc,
    col_acc,
    gu_ref,
):
    rows, channels = gm_ref.shape
    tiles = channels // 128
    mirror_in(gm_ref, mask_ref, gh_ref)
    apply_cols(colop_ref, gh_ref, x_ref)
    cut = 3

    def row_corr(step, carry):
        tile = step // (2 * (HALF // cut))
        rest = lax.rem(step, 2 * (HALF // cut))
        rho = rest // (HALF // cut)
        first = lax.rem(rest, HALF // cut) * cut
        at = lanes(tile)
        sums = [[None] * HALF for _ in range(cut)]
        for j in range(HALF):
            left = [x_ref[rows8(rho * 81 + (first + k) * HALF + j), at] for k in range(cut)]
            for p in range(HALF):
                right = uh_ref[rows8(rho * 81 + p * HALF + j), at]
                for k in range(cut):
                    term = left[k] * right
                    sums[k][p] = term if sums[k][p] is None else sums[k][p] + term
        for k in range(cut):
            for p in range(HALF):
                row_acc[rows8(rho * 81 + (first + k) * HALF + p), at] = sums[k][p]
        return carry

    lax.fori_loop(0, tiles * 2 * (HALF // cut), row_corr, 0)

    def col_corr(step, carry):
        tile = step // (HALF // cut)
        first = lax.rem(step, HALF // cut) * cut
        at = lanes(tile)
        sums = [[None] * HALF for _ in range(cut)]
        for i in range(2 * HALF):
            left = [gh_ref[rows8(i * HALF + first + k), at] for k in range(cut)]
            for q in range(HALF):
                right = v_ref[rows8(i * HALF + q), at]
                for k in range(cut):
                    term = left[k] * right
                    sums[k][q] = term if sums[k][q] is None else sums[k][q] + term
        for k in range(cut):
            for q in range(HALF):
                col_acc[rows8((first + k) * HALF + q), at] = sums[k][q]
        return carry

    lax.fori_loop(0, tiles * (HALF // cut), col_corr, 0)

    side = side_vreg(class_ref)
    sign = jnp.where(sublane_half(), 1.0, -1.0).astype(F32)

    def lag_body(tile, carry):
        at = lanes(tile)
        for axis in range(2):
            near = [None] * HALF
            far = [None] * (GRID)
            for a in range(HALF):
                for b in range(HALF):
                    if axis == 0:
                        plus = row_acc[rows8(a * HALF + b), at]
                        minus = row_acc[rows8(81 + a * HALF + b), at]
                        direct, cross = plus + minus, plus - minus
                    else:
                        direct = col_acc[rows8(a * HALF + b), at]
                        cross = sign * direct
                    d, s = abs(a - b), GRID - 1 - a - b
                    near[d] = direct if near[d] is None else near[d] + direct
                    far[s] = cross if far[s] is None else far[s] + cross
            for lag in range(GRID):
                total = None
                for part in ([near[lag]] if lag < HALF else []) + ([far[lag]] if lag else []):
                    total = part if total is None else total + part
                total = 0.5 * total
                for cat, length in enumerate(SIDES):
                    row = cat * GRID + lag
                    value = jnp.where(side == length, total, 0.0)
                    dk_out[axis, row : row + 1, at] = jnp.sum(value, axis=0, keepdims=True)
        return carry

    lax.fori_loop(0, tiles, lag_body, 0)

    apply_rows(rowop_ref, x_ref, gh_ref)
    mirror_out(gh_ref, mask_ref, gu_ref, gm_ref, skip_ref)
    block = 144

    def finish(t, total):
        at = pl.ds(pl.multiple_of(t * block, block), block)
        dx_out[at, :] = (cot_ref[at, :].astype(F32) + gu_ref[at, :]).astype(BF16)
        return total + jnp.sum(gm_ref[at, :] * u_ref[at, :], axis=0, keepdims=True)

    dskip_out[...] = lax.fori_loop(0, rows // block, finish, jnp.zeros((1, channels), F32))


VM = pl.BlockSpec(memory_space=pltpu.VMEM)
SM = pl.BlockSpec(memory_space=pltpu.SMEM)


def shape(dims, kind=F32):
    return jax.ShapeDtypeStruct(dims, kind)


def call(kernel, outs, ins, scratch=(), name=None):
    return pl.pallas_call(
        kernel,
        out_shape=tuple(outs),
        in_specs=ins,
        out_specs=tuple(VM for _ in outs),
        scratch_shapes=list(scratch),
        compiler_params=pltpu.CompilerParams(vmem_limit_bytes=VMEM_LIMIT),
        name=name,
    )


def to_rows(images):
    micro, count, channels, cells = images.shape
    return images.transpose(3, 0, 1, 2).reshape(cells * micro * count, channels)


def from_rows(rows, like):
    micro, count, channels, cells = like.shape
    return rows.reshape(cells, micro, count, channels).transpose(1, 2, 3, 0)


def on_device(
    pixels,
    grid_class,
    extent,
    ssm_rate,
    ssm_freq,
    ssm_coef,
    skip_gain,
    norm_gain,
    norm_bias,
    w_in,
    b_in,
    w_out,
    b_out,
    layer_scale,
    cotangent,
):
    micro, count, channels, cells = pixels.shape
    rows = micro * count * cells
    own = ssm_rate.shape[1]
    modes = ssm_rate.shape[2]
    hidden = b_in.shape[0] * 2
    x = to_rows(pixels)
    cot = to_rows(cotangent)
    extent_row = extent.reshape(1, own)
    rate = ssm_rate.transpose(0, 2, 1)
    freq = ssm_freq.transpose(0, 2, 1)
    coef = ssm_coef.transpose(0, 2, 1)
    (table,) = call(tables_kernel, [shape((2, LAGS, own))], [VM] * 4, name="tables")(
        extent_row, rate, freq, coef
    )
    table = lax.all_gather(table, "mp", axis=2, tiled=True)
    w_in_all = lax.all_gather(w_in, "mp", axis=1, tiled=True)
    w_out_all = lax.all_gather(w_out, "mp", axis=0, tiled=True)
    vectors = lax.all_gather(jnp.concatenate([b_in, skip_gain]), "mp", axis=0)
    b_in_all = vectors[:, : b_in.shape[0]].reshape(1, hidden)
    skip_all = vectors[:, b_in.shape[0] :].reshape(1, channels)

    def row(v):
        return v.reshape(1, channels)

    field = (rows, channels)
    (
        block_out,
        gm,
        u,
        uh,
        v,
        rowop,
        colop,
        mask,
        dw_in,
        dw_out,
        db_in,
        small,
    ) = call(
        front_kernel,
        [
            shape(field, BF16),
            shape(field),
            shape(field),
            shape(field),
            shape(field),
            shape((90, 8, channels)),
            shape((45, 8, channels)),
            shape((rows, 128)),
            shape((channels, hidden)),
            shape((hidden, channels)),
            shape((1, hidden)),
            shape((4, channels)),
        ],
        [SM] + [VM] * 11,
        [
            pltpu.VMEM((2 * GRID, 8, channels), F32),
            pltpu.VMEM(field, F32),
            pltpu.VMEM(field, F32),
            pltpu.VMEM(field, BF16),
            pltpu.VMEM(field, BF16),
            pltpu.VMEM((rows, 256), BF16),
            pltpu.VMEM((rows, 256), BF16),
            pltpu.VMEM(field, F32),
            pltpu.VMEM(field, F32),
            pltpu.VMEM((rows, 128), F32),
        ],
        name="front",
    )(
        grid_class,
        table,
        x,
        cot,
        skip_all,
        row(norm_gain),
        row(norm_bias),
        w_in_all,
        b_in_all,
        w_out_all,
        row(b_out),
        row(layer_scale),
    )
    dx, dk, dskip = call(
        back_kernel,
        [shape(field, BF16), shape((2, LAGS, channels)), shape((1, channels))],
        [SM] + [VM] * 9,
        [
            pltpu.VMEM(field, F32),
            pltpu.VMEM(field, F32),
            pltpu.VMEM((162 * 8, channels), F32),
            pltpu.VMEM((81 * 8, channels), F32),
            pltpu.VMEM(field, F32),
        ],
        name="back",
    )(grid_class, gm, cot, u, uh, v, rowop, colop, mask, skip_all)

    dw_in = lax.psum(
        lax.psum_scatter(dw_in, "mp", scatter_dimension=1, tiled=True), "dp"
    )
    dw_out = lax.psum(
        lax.psum_scatter(dw_out, "mp", scatter_dimension=0, tiled=True), "dp"
    )
    mine = lax.axis_index("mp")
    db_in, dk, dskip, small = lax.psum((db_in, dk, dskip, small), ("dp", "mp"))
    db_in = lax.dynamic_slice_in_dim(db_in[0], mine * (hidden // 2), hidden // 2)
    dk = lax.dynamic_slice_in_dim(dk, mine * own, own, axis=2)
    dskip = lax.dynamic_slice_in_dim(dskip[0], mine * own, own)
    g_rate, g_freq, g_coef = call(
        modes_grad_kernel, [shape((2, modes, own))] * 3, [VM] * 5, name="modes"
    )(extent_row, rate, freq, coef, dk)
    return (
        from_rows(block_out, pixels),
        from_rows(dx, pixels),
        g_rate.transpose(0, 2, 1),
        g_freq.transpose(0, 2, 1),
        g_coef.transpose(0, 2, 1),
        dskip,
        small[0],
        small[1],
        dw_in,
        db_in,
        dw_out,
        small[3],
        small[2],
    )


def solution(mesh):
    placed = (
        P(None, ("dp", "mp"), None, None),
        P(None, "dp"),
        P("mp"),
        P(None, "mp", None),
        P(None, "mp", None),
        P(None, "mp", None),
        P("mp"),
        P(),
        P(),
        P(None, "mp"),
        P("mp"),
        P("mp", None),
        P(),
        P(),
        P(None, ("dp", "mp"), None, None),
    )
    return jax.shard_map(
        on_device,
        mesh=mesh,
        in_specs=placed,
        out_specs=(
            P(None, ("dp", "mp"), None, None),
            P(None, ("dp", "mp"), None, None),
            P(None, "mp", None),
            P(None, "mp", None),
            P(None, "mp", None),
            P("mp"),
            P(),
            P(),
            P(None, "mp"),
            P("mp"),
            P("mp", None),
            P(),
            P(),
        ),
        check_vma=False,
    )
```

```python
import math
from functools import partial

import jax
import jax.numpy as jnp
import numpy as np
from jax import lax
from jax.experimental import pallas as pl
from jax.experimental.pallas import tpu as pltpu
from jax.sharding import PartitionSpec as P

GRID = 18
HALF = 9
SIDES = (10, 14, 18)
LAGS = 3 * GRID
F32 = jnp.float32
BF16 = jnp.bfloat16

ERF_SHIFT = 0.35 / math.sqrt(2.0)
ERF_POLY = (
    0.19396706,
    0.23864529,
    -0.01708609,
    0.69839275,
    -0.6929918,
    0.77818103,
    -0.19910822,
)
VMEM_LIMIT = 60 * 1024 * 1024


def small_sincos(angle):
    sq = angle * angle
    cos = 1.0 + sq * (
        -1 / 2 + sq * (1 / 24 + sq * (-1 / 720 + sq * (1 / 40320 + sq * (-1 / 3628800))))
    )
    sin = angle * (
        1.0
        + sq * (-1 / 6 + sq * (1 / 120 + sq * (-1 / 5040 + sq * (1 / 362880 + sq * (-1 / 39916800)))))
    )
    return sin, cos


def mode_step(rate, freq, side):
    decay = jnp.exp(rate * (-1.0 / side))
    sin, cos = small_sincos(freq * (1.0 / side))
    return decay * cos, decay * sin


PACK_ROWS = 120
SMALL_ROWS = 121

def write_tables(extent_ref, rate_ref, freq_ref, coef_ref, out_ref):
    for axis in range(2):
        for cat, side in enumerate(SIDES):
            z_re, z_im = mode_step(rate_ref[axis], freq_ref[axis], side)
            w_re = coef_ref[axis]
            w_im = jnp.zeros_like(w_re)
            for lag in range(GRID):
                row = axis * LAGS + cat * GRID + lag
                if lag >= side:
                    out_ref[row : row + 1, :] = jnp.zeros((1, w_re.shape[1]), F32)
                    continue
                total = jnp.sum(w_re, axis=0, keepdims=True)
                out_ref[row : row + 1, :] = jnp.where(extent_ref[...] > lag, total, 0.0)
                if lag < side - 1:
                    w_re, w_im = w_re * z_re - w_im * z_im, w_re * z_im + w_im * z_re


def modes_grad(extent_ref, rate_ref, freq_ref, coef_ref, dk_ref, rate_out, freq_out, coef_out):
    for axis in range(2):
        coef = coef_ref[axis]
        g_rate = jnp.zeros_like(coef)
        g_freq = jnp.zeros_like(coef)
        g_coef = jnp.zeros_like(coef)
        for cat, side in enumerate(SIDES):
            z_re, z_im = mode_step(rate_ref[axis], freq_ref[axis], side)
            p_re = jnp.zeros_like(coef)
            p_im = jnp.zeros_like(coef)
            q_re = jnp.zeros_like(coef)
            q_im = jnp.zeros_like(coef)
            for lag in reversed(range(side)):
                row = axis * LAGS + cat * GRID + lag
                d = jnp.where(extent_ref[...] > lag, dk_ref[row : row + 1, :], 0.0)
                p_re, p_im = p_re * z_re - p_im * z_im + d, p_re * z_im + p_im * z_re
                q_re, q_im = q_re * z_re - q_im * z_im + float(lag) * d, q_re * z_im + q_im * z_re
            g_coef = g_coef + p_re
            g_rate = g_rate - (1.0 / side) * q_re
            g_freq = g_freq - (1.0 / side) * q_im
        coef_out[axis] = g_coef
        rate_out[axis] = g_rate * coef
        freq_out[axis] = g_freq * coef

def tri(a, b):
    low, high = min(a, b), max(a, b)
    return low * HALF - low * (low - 1) // 2 + (high - low)


def rows8(index):
    if isinstance(index, int):
        return pl.ds(index * 8, 8)
    return pl.ds(pl.multiple_of(index * 8, 8), 8)


def lanes(tile):
    if isinstance(tile, int):
        return pl.ds(tile * 128, 128)
    return pl.ds(pl.multiple_of(tile * 128, 128), 128)


def swap(value):
    return pltpu.roll(value, 4, 0)


def sublane_half():
    return lax.broadcasted_iota(jnp.int32, (8, 128), 0) < 4


def side_vreg(class_ref):
    mine = lax.axis_index("mp")
    image = lax.rem(lax.broadcasted_iota(jnp.int32, (8, 128), 0), 4)
    cls = jnp.zeros((8, 128), jnp.int32)
    own = class_ref.shape[1] // 2
    for micro in range(2):
        for img in range(2):
            cls = jnp.where(image == micro * 2 + img, class_ref[micro, mine * own + img], cls)
    return 10 + 4 * cls


def build_masks(class_ref, mask_ref):
    side = side_vreg(class_ref)
    offset = jnp.where(sublane_half(), 0, 1)

    def row(i, carry):
        for pair in range(HALF):
            ok = (i < side) & (2 * pair + offset < side)
            mask_ref[rows8(i * HALF + pair), :] = jnp.where(ok, 1.0, 0.0).astype(F32)
        return carry

    lax.fori_loop(0, GRID, row, 0)


def build_operators(class_ref, table_ref, lag_ref, rowop_ref, colop_ref):
    side = side_vreg(class_ref)
    sign = jnp.where(sublane_half(), 1.0, -1.0).astype(F32)
    tiles = table_ref.shape[1] // 128

    def tile_body(tile, carry):
        at = lanes(tile)
        for axis in range(2):
            for lag in range(GRID):
                by_side = [
                    jnp.broadcast_to(table_ref[axis * LAGS + cat * GRID + lag : axis * LAGS + cat * GRID + lag + 1, at], (8, 128))
                    for cat in range(3)
                ]
                lag_ref[axis * GRID + lag, :, at] = 0.5 * jnp.where(
                    side == 10, by_side[0], jnp.where(side == 14, by_side[1], by_side[2])
                )
        for a in range(HALF):
            for b in range(a, HALF):
                near = lag_ref[b - a, :, at]
                far = lag_ref[GRID - 1 - a - b, :, at]
                rowop_ref[tri(a, b), :, at] = near + far
                rowop_ref[45 + tri(a, b), :, at] = near - far
                near = lag_ref[GRID + b - a, :, at]
                far = lag_ref[GRID + GRID - 1 - a - b, :, at]
                colop_ref[tri(a, b), :, at] = near + sign * far
        return carry

    lax.fori_loop(0, tiles, tile_body, 0)


def mirror_in(source_ref, mask_ref, out_ref):
    half = sublane_half()
    sign = jnp.where(half, 1.0, -1.0).astype(F32)
    tiles = source_ref.shape[1] // 128

    def body(i, carry):
        for tile in range(tiles):
            at = lanes(tile)

            def mirrored(row, pair):
                near = source_ref[rows8(row * HALF + pair), at] * mask_ref[rows8(row * HALF + pair), :]
                if pair == 4:
                    return swap(near) + sign * near, None
                other = row * HALF + 8 - pair
                far = source_ref[rows8(other), at] * mask_ref[rows8(other), :]
                even = jnp.where(half, near, far)
                odd = jnp.where(half, far, near)
                return swap(even) + sign * even, odd + sign * swap(odd)

            for pair in range(5):
                top = mirrored(i, pair)
                bottom = mirrored(GRID - 1 - i, pair)
                for step in range(2 if pair < 4 else 1):
                    where = i * HALF + 2 * pair + step
                    out_ref[rows8(where), at] = top[step] + bottom[step]
                    out_ref[rows8(81 + where), at] = top[step] - bottom[step]
        return carry

    lax.fori_loop(0, HALF, body, 0)


def mirror_out(source_ref, mask_ref, out_ref, extra_ref, gain_ref):
    half = sublane_half()
    sign = jnp.where(half, 1.0, -1.0).astype(F32)
    tiles = source_ref.shape[1] // 128

    def body(i, carry):
        for tile in range(tiles):
            at = lanes(tile)
            gain = jnp.broadcast_to(gain_ref[:, at], (8, 128))

            def finish(index, value):
                value = value * mask_ref[rows8(index), :] + gain * extra_ref[rows8(index), at]
                out_ref[rows8(index), at] = value.astype(BF16).astype(F32)

            for pair in range(5):
                both = []
                for step in range(2 if pair < 4 else 1):
                    where = i * HALF + 2 * pair + step
                    plus = source_ref[rows8(where), at]
                    minus = source_ref[rows8(81 + where), at]
                    top, bottom = plus + minus, plus - minus
                    both.append(
                        (swap(top) + sign * top, swap(bottom) + sign * bottom)
                        if step == 0
                        else (top - sign * swap(top), bottom - sign * swap(bottom))
                    )
                for part, row in ((0, i), (1, GRID - 1 - i)):
                    if pair == 4:
                        finish(row * HALF + 4, both[0][part])
                        continue
                    if True:
                        even, odd = both[0][part], both[1][part]
                        finish(row * HALF + pair, jnp.where(half, even, odd))
                        finish(row * HALF + 8 - pair, jnp.where(half, odd, even))
        return carry

    lax.fori_loop(0, HALF, body, 0)


def apply_rows(op_ref, source_ref, out_ref):
    tiles = source_ref.shape[1] // 128

    def body(j, carry):
        for tile in range(tiles):
            at = lanes(tile)
            for rho in range(2):
                values = [source_ref[rows8(rho * 81 + p * HALF + j), at] for p in range(HALF)]
                for i in range(HALF):
                    total = None
                    for p in range(HALF):
                        term = op_ref[rho * 45 + tri(i, p), :, at] * values[p]
                        total = term if total is None else total + term
                    out_ref[rows8(rho * 81 + i * HALF + j), at] = total
        return carry

    lax.fori_loop(0, HALF, body, 0)


def apply_cols(op_ref, source_ref, out_ref):
    tiles = source_ref.shape[1] // 128

    def body(i, carry):
        for tile in range(tiles):
            at = lanes(tile)
            values = [source_ref[rows8(i * HALF + q), at] for q in range(HALF)]
            for j in range(HALF):
                total = None
                for q in range(HALF):
                    term = op_ref[tri(j, q), :, at] * values[q]
                    total = term if total is None else total + term
                out_ref[rows8(i * HALF + j), at] = total
        return carry

    lax.fori_loop(0, 2 * HALF, body, 0)


def row_correlate(left_ref, right_ref, acc_ref, cut=3):
    tiles = left_ref.shape[1] // 128
    blocks = HALF // cut

    def body(step, carry):
        tile = step // (2 * blocks)
        rest = lax.rem(step, 2 * blocks)
        rho = rest // blocks
        first = lax.rem(rest, blocks) * cut
        at = lanes(tile)
        sums = [[None] * HALF for _ in range(cut)]
        for j in range(HALF):
            left = [left_ref[rows8(rho * 81 + (first + k) * HALF + j), at] for k in range(cut)]
            for p in range(HALF):
                right = right_ref[rows8(rho * 81 + p * HALF + j), at]
                for k in range(cut):
                    term = left[k] * right
                    sums[k][p] = term if sums[k][p] is None else sums[k][p] + term
        for k in range(cut):
            for p in range(HALF):
                acc_ref[rows8(rho * 81 + (first + k) * HALF + p), at] = sums[k][p]
        return carry

    lax.fori_loop(0, tiles * 2 * blocks, body, 0)


def col_correlate(left_ref, right_ref, acc_ref, cut=3):
    tiles = left_ref.shape[1] // 128
    blocks = HALF // cut

    def body(step, carry):
        tile = step // blocks
        first = lax.rem(step, blocks) * cut
        at = lanes(tile)
        sums = [[None] * HALF for _ in range(cut)]
        for i in range(2 * HALF):
            left = [left_ref[rows8(i * HALF + first + k), at] for k in range(cut)]
            for q in range(HALF):
                right = right_ref[rows8(i * HALF + q), at]
                for k in range(cut):
                    term = left[k] * right
                    sums[k][q] = term if sums[k][q] is None else sums[k][q] + term
        for k in range(cut):
            for q in range(HALF):
                acc_ref[rows8((first + k) * HALF + q), at] = sums[k][q]
        return carry

    lax.fori_loop(0, tiles * blocks, body, 0)


def gather_lags(class_ref, row_acc, col_acc, dk_ref):
    side = side_vreg(class_ref)
    sign = jnp.where(sublane_half(), 1.0, -1.0).astype(F32)
    tiles = row_acc.shape[1] // 128

    def body(tile, carry):
        at = lanes(tile)
        for axis in range(2):
            near = [None] * HALF
            far = [None] * GRID
            for a in range(HALF):
                for b in range(HALF):
                    if axis == 0:
                        plus = row_acc[rows8(a * HALF + b), at]
                        minus = row_acc[rows8(81 + a * HALF + b), at]
                        direct, cross = plus + minus, plus - minus
                    else:
                        direct = col_acc[rows8(a * HALF + b), at]
                        cross = sign * direct
                    d, s = abs(a - b), GRID - 1 - a - b
                    near[d] = direct if near[d] is None else near[d] + direct
                    far[s] = cross if far[s] is None else far[s] + cross
            for lag in range(GRID):
                total = None
                for part in ([near[lag]] if lag < HALF else []) + ([far[lag]] if lag else []):
                    total = part if total is None else total + part
                total = 0.5 * total
                for cat, length in enumerate(SIDES):
                    row = axis * LAGS + cat * GRID + lag
                    value = jnp.where(side == length, total, 0.0)
                    dk_ref[row : row + 1, at] = jnp.sum(value, axis=0, keepdims=True)
        return carry

    lax.fori_loop(0, tiles, body, 0)


def bit_orders(size):
    bits = size.bit_length() - 1
    turn = min(3, max(bits, 1))
    base = list(range(bits))
    return [
        [base[(k + part) % turn] if k < turn else base[k] for k in range(bits)] for part in range(3)
    ]


def chunk_rows(total, size):
    per = -(-total // (3 * size))
    return -(-per // 16) * 16


class Ring:
    def __init__(self, size, rows, acc, send, recv, full, sems):
        self.size, self.rows = size, rows
        self.acc, self.send, self.recv, self.full = acc, send, recv, full
        self.send_sem, self.recv_sem, self.back_send, self.back_recv = sems
        self.orders = bit_orders(size)
        self.bits = size.bit_length() - 1
        self.me = lax.axis_index("dp")
        self.place = []
        for order in self.orders:
            place = 0
            for bit in order:
                place = place * 2 + lax.rem(self.me // (1 << bit), 2)
            self.place.append(place)

    def peer(self, bit):
        mine = lax.rem(self.me // (1 << bit), 2)
        return self.me + (1 - 2 * mine) * (1 << bit)

    def span(self, part, step):
        half = self.size >> (step + 1)
        index = self.place[part] // half
        mine = lax.rem(index, 2)
        base = part * self.size * self.rows
        keep = base + index * half * self.rows
        away = base + (index + 1 - 2 * mine) * half * self.rows
        return pl.multiple_of(keep, 16), pl.multiple_of(away, 16), half * self.rows

    def slot(self, part, step):
        done = self.size - (self.size >> step)
        return (part * self.size + done) * self.rows

    def reduce_copy(self, part, step):
        _, away, length = self.span(part, step)
        return pltpu.make_async_remote_copy(
            src_ref=self.send.at[pl.ds(away, length), :],
            dst_ref=self.recv.at[pl.ds(self.slot(part, step), length), :],
            send_sem=self.send_sem.at[part, step],
            recv_sem=self.recv_sem.at[part, step],
            device_id={"dp": self.peer(self.orders[part][step])},
            device_id_type=pl.DeviceIdType.MESH,
        )

    def gather_copy(self, part, step):
        keep, _, length = self.span(part, step)
        return pltpu.make_async_remote_copy(
            src_ref=self.full.at[pl.ds(keep, length), :],
            dst_ref=self.full.at[pl.ds(keep, length), :],
            send_sem=self.back_send.at[part, step],
            recv_sem=self.back_recv.at[part, step],
            device_id={"dp": self.peer(self.orders[part][step])},
            device_id_type=pl.DeviceIdType.MESH,
        )

    def reduce_start(self, step):
        for part in range(3):
            _, away, length = self.span(part, step)
            copy_rows(self.acc, away, self.send, away, length, lambda v: v.astype(BF16))
            self.reduce_copy(part, step).start()

    def reduce_finish(self, step):
        for part in range(3):
            self.reduce_copy(part, step).wait_recv()
            keep, _, length = self.span(part, step)
            slot = self.slot(part, step)

            def body(t, carry, keep=keep, slot=slot):
                at = pl.ds(pl.multiple_of(keep + t * 48, 16), 48)
                other = pl.ds(pl.multiple_of(slot + t * 48, 16), 48)
                self.acc[at, :] += self.recv[other, :].astype(F32)
                return carry

            if length % 48 == 0:
                lax.fori_loop(0, length // 48, body, 0)
            else:
                self.acc[pl.ds(keep, length), :] += self.recv[pl.ds(slot, length), :].astype(F32)

    def gather_first(self):
        for part in range(3):
            own = pl.multiple_of((part * self.size + self.place[part]) * self.rows, 16)
            copy_rows(self.acc, own, self.full, own, self.rows, lambda v: v.astype(BF16))

    def gather_start(self, step):
        for part in range(3):
            self.gather_copy(part, step).start()

    def gather_finish(self, step):
        for part in range(3):
            self.gather_copy(part, step).wait_recv()

    def close(self):
        for part in range(3):
            for step in range(self.bits):
                self.reduce_copy(part, step).wait_send()
                self.gather_copy(part, step).wait_send()


def copy_rows(source, first, target, where, length, change, block=48):
    if length % block:
        block = 16

    def body(t, carry):
        here = pl.ds(pl.multiple_of(first + t * block, 16), block)
        there = pl.ds(pl.multiple_of(where + t * block, 16), block)
        target[there, :] = change(source[here, :])
        return carry

    lax.fori_loop(0, length // block, body, 0)


def wide(ref, first, count):
    return jnp.concatenate([ref[first + k : first + k + 1, :] for k in range(count)], axis=1)


def mega_kernel(
    size,
    class_ref,
    extent_ref,
    rate_ref,
    freq_ref,
    coef_ref,
    skip_ref,
    b_in_ref,
    vec_ref,
    w_in_ref,
    w_out_ref,
    x_ref,
    cot_ref,
    block_out,
    dx_out,
    full_out,
    small_out,
    pack_own,
    pack_oth,
    w_in_oth,
    w_out_oth,
    table_ref,
    skip_all,
    mask_ref,
    lag_ref,
    rowop_ref,
    colop_ref,
    u_ref,
    uh_ref,
    v_ref,
    mh_ref,
    mixed_ref,
    normed_ref,
    gmlp_ref,
    act_ref,
    gpre_ref,
    mlp_ref,
    gn_ref,
    stat_ref,
    gm_ref,
    row_acc,
    col_acc,
    dk_ref,
    db_ref,
    sums_ref,
    acc_ref,
    away_ref,
    landed_ref,
    send_ref,
    recv_ref,
    small_keep,
    small_send,
    small_land,
    small_recv,
    pair_send,
    pair_recv,
    red_send,
    red_recv,
    gat_send,
    gat_recv,
    sc_send,
    sc_recv,
    bc_send,
    bc_recv,
):
    rows, channels = x_ref.shape
    own = pack_own.shape[1]
    half_hidden = w_in_ref.shape[1]
    me = lax.axis_index("dp")
    core = lax.axis_index("mp")
    partner = {"mp": 1 - core}

    barrier = pltpu.get_barrier_semaphore()
    pl.semaphore_signal(barrier, inc=1, device_id=partner, device_id_type=pl.DeviceIdType.MESH)
    for offset in range(1, size):
        pl.semaphore_signal(
            barrier,
            inc=1,
            device_id={"dp": lax.rem(me + offset, size)},
            device_id_type=pl.DeviceIdType.MESH,
        )

    def pair_copy(index, source, target):
        return pltpu.make_async_remote_copy(
            src_ref=source,
            dst_ref=target,
            send_sem=pair_send.at[index],
            recv_sem=pair_recv.at[index],
            device_id=partner,
            device_id_type=pl.DeviceIdType.MESH,
        )

    write_tables(extent_ref, rate_ref, freq_ref, coef_ref, pack_own)
    pack_own[108:109, :] = skip_ref[...]
    for k in range(4):
        pack_own[109 + k : 110 + k, :] = b_in_ref[:, k * own : (k + 1) * own]
    pack_own[113:PACK_ROWS, :] = jnp.zeros((PACK_ROWS - 113, own), F32)
    pl.semaphore_wait(barrier, size)
    pack_copy = pair_copy(0, pack_own, pack_oth)
    first_copy = pair_copy(1, w_in_ref, w_in_oth)
    second_copy = pair_copy(2, w_out_ref, w_out_oth)
    pack_copy.start()
    first_copy.start()
    second_copy.start()

    build_masks(class_ref, mask_ref)
    block = 144
    scale = vec_ref[3:4, :]

    def load(t, carry):
        at = pl.ds(pl.multiple_of(t * block, block), block)
        u_ref[at, :] = x_ref[at, :].astype(F32)
        mask = jnp.tile(mask_ref[at, :], (1, channels // 128))
        gmlp_ref[at, :] = (cot_ref[at, :].astype(F32) * scale * mask).astype(BF16)
        return carry

    lax.fori_loop(0, rows // block, load, 0)
    mirror_in(u_ref, mask_ref, uh_ref)

    pack_copy.wait_recv()
    first = core == 0
    low = jnp.where(first, pack_own[...], pack_oth[...])
    high = jnp.where(first, pack_oth[...], pack_own[...])
    table_ref[...] = jnp.concatenate([low, high], axis=1)
    skip_all[...] = table_ref[108:109, :]
    build_operators(class_ref, table_ref, lag_ref, rowop_ref, colop_ref)
    apply_rows(rowop_ref, uh_ref, v_ref)
    apply_cols(colop_ref, v_ref, mh_ref)
    mirror_out(mh_ref, mask_ref, mixed_ref, u_ref, skip_all)

    gain = vec_ref[0:1, :]
    shift = vec_ref[1:2, :]

    def norm(t, carry):
        at = pl.ds(pl.multiple_of(t * block, block), block)
        value = mixed_ref[at, :]
        mean = jnp.mean(value, axis=1, keepdims=True)
        centered = value - mean
        variance = jnp.mean(centered * centered, axis=1, keepdims=True)
        rstd = lax.rsqrt(variance + 1e-06)
        hat = centered * rstd
        mixed_ref[at, :] = hat
        stat_ref[at, :] = jnp.broadcast_to(rstd, (block, 128))
        normed_ref[at, :] = (hat * gain + shift).astype(BF16)
        return carry

    lax.fori_loop(0, rows // block, norm, 0)

    chunk = 256
    tile_rows = 432
    mlp_ref[...] = jnp.broadcast_to(vec_ref[2:3, :], mlp_ref.shape)
    gn_ref[...] = jnp.zeros_like(gn_ref)
    first_copy.wait_recv()
    second_copy.wait_recv()

    def feed(w_first_ref, w_second_ref, bias_row, target_ref, db_row):
        db_ref[2:3, :] = bias_row

        def body(f, carry):
            cols = pl.ds(pl.multiple_of(f * chunk, chunk), chunk)
            w_first = w_first_ref[:, cols]
            w_second = w_second_ref[cols, :]
            bias = db_ref[2:3, cols]
            db = jnp.zeros((1, chunk), F32)
            for t in range(rows // tile_rows):
                at = pl.ds(t * tile_rows, tile_rows)
                pre = jnp.dot(normed_ref[at, :], w_first, preferred_element_type=F32) + bias
                size_of = jnp.abs(pre)
                inv = 1.0 / (1.0 + ERF_SHIFT * size_of)
                poly = jnp.full_like(inv, 0.5 * ERF_POLY[-1])
                for value in reversed(ERF_POLY[:-1]):
                    poly = poly * inv + 0.5 * value
                bell = jnp.exp(-0.5 * pre * pre)
                tail = poly * inv * bell
                cdf = jnp.where(pre >= 0.0, 1.0 - tail, tail)
                act = (pre * cdf).astype(BF16)
                slope = cdf + pre * bell * (1.0 / math.sqrt(2.0 * math.pi))
                g_act = lax.dot_general(
                    gmlp_ref[at, :], w_second, (((1,), (1,)), ((), ())), preferred_element_type=F32
                )
                g_pre = (g_act * slope).astype(BF16)
                db = db + jnp.sum(g_pre.astype(F32), axis=0, keepdims=True)
                act_ref[at, :] = act
                gpre_ref[at, :] = g_pre
                mlp_ref[at, :] += jnp.dot(act, w_second, preferred_element_type=F32)
                gn_ref[at, :] += lax.dot_general(
                    g_pre, w_first, (((1,), (1,)), ((), ())), preferred_element_type=F32
                )
            db_ref[db_row : db_row + 1, cols] = db
            d_first = lax.dot_general(
                normed_ref[...], gpre_ref[...], (((0,), (0,)), ((), ())), preferred_element_type=F32
            )
            for k in range(chunk // 128):
                at = pl.ds(pl.multiple_of((f * (chunk // 128) + k) * channels, channels), channels)
                target_ref[at, :] = d_first[:, k * 128 : (k + 1) * 128].astype(target_ref.dtype)
            d_second = lax.dot_general(
                act_ref[...], gmlp_ref[...], (((0,), (0,)), ((), ())), preferred_element_type=F32
            )
            base = channels * (half_hidden // 128)
            for k in range(channels // 128):
                at = pl.ds(pl.multiple_of(base + k * half_hidden + f * chunk, chunk), chunk)
                target_ref[at, :] = d_second[:, k * 128 : (k + 1) * 128].astype(target_ref.dtype)
            return carry

        lax.fori_loop(0, half_hidden // chunk, body, 0)

    feed(w_in_oth, w_out_oth, wide(pack_oth, 109, 4), away_ref, 1)
    grads_copy = pair_copy(3, away_ref, landed_ref)
    grads_copy.start()
    feed(w_in_ref, w_out_ref, b_in_ref[...], acc_ref, 0)

    ring = Ring(size, chunk_rows(away_ref.shape[0], size), acc_ref, send_ref, recv_ref, full_out,
                (red_send, red_recv, gat_send, gat_recv))
    grads_copy.wait_recv()

    def add_pair(t, carry):
        at = pl.ds(pl.multiple_of(t * 96, 96), 96)
        acc_ref[at, :] += landed_ref[at, :].astype(F32)
        return carry

    lax.fori_loop(0, away_ref.shape[0] // 96, add_pair, 0)
    pad = acc_ref.shape[0] - away_ref.shape[0]
    if pad:
        acc_ref[away_ref.shape[0] :, :] = jnp.zeros((pad, 128), F32)

    def advance(step):
        if step > 2 * ring.bits:
            return
        if 0 < step <= ring.bits:
            ring.reduce_finish(step - 1)
        if step > ring.bits:
            ring.gather_finish(2 * ring.bits - step)
        if step < ring.bits:
            ring.reduce_start(step)
        if step == ring.bits:
            ring.gather_first()
        if ring.bits <= step < 2 * ring.bits:
            ring.gather_start(2 * ring.bits - 1 - step)

    advance(0)

    def back(t, carry):
        d_gain, d_bias, d_scale, d_b_out = carry
        at = pl.ds(pl.multiple_of(t * block, block), block)
        mask = jnp.tile(mask_ref[at, :], (1, channels // 128))
        branch = mlp_ref[at, :] * mask
        block_out[at, :] = (u_ref[at, :] + scale * branch).astype(BF16)
        d_scale = d_scale + jnp.sum(cot_ref[at, :].astype(F32) * branch, axis=0, keepdims=True)
        d_b_out = d_b_out + jnp.sum(gmlp_ref[at, :].astype(F32), axis=0, keepdims=True)
        grad = gn_ref[at, :]
        hat = mixed_ref[at, :]
        d_gain = d_gain + jnp.sum(grad * hat, axis=0, keepdims=True)
        d_bias = d_bias + jnp.sum(grad, axis=0, keepdims=True)
        grad = grad * gain
        mean_g = jnp.mean(grad, axis=1, keepdims=True)
        mean_gh = jnp.mean(grad * hat, axis=1, keepdims=True)
        rstd = jnp.tile(stat_ref[at, :], (1, channels // 128))
        gm_ref[at, :] = (rstd * (grad - mean_g - hat * mean_gh)).astype(BF16).astype(F32)
        return d_gain, d_bias, d_scale, d_b_out

    zero = jnp.zeros((1, channels), F32)
    sums = lax.fori_loop(0, rows // block, back, (zero, zero, zero, zero))
    for index, value in enumerate(sums):
        sums_ref[index : index + 1, :] = value

    gh_ref, xh_ref = mh_ref, mlp_ref
    mirror_in(gm_ref, mask_ref, gh_ref)
    advance(1)
    apply_cols(colop_ref, gh_ref, xh_ref)
    advance(2)
    row_correlate(xh_ref, uh_ref, row_acc)
    advance(3)
    col_correlate(gh_ref, v_ref, col_acc)
    advance(4)
    gather_lags(class_ref, row_acc, col_acc, dk_ref)

    def skip_sum(t, total):
        at = pl.ds(pl.multiple_of(t * block, block), block)
        return total + jnp.sum(gm_ref[at, :] * u_ref[at, :], axis=0, keepdims=True)

    dk_ref[108:109, :] = lax.fori_loop(0, rows // block, skip_sum, zero)
    dk_ref[109:112, :] = jnp.zeros((3, channels), F32)
    low = dk_ref[:, :own]
    high = dk_ref[:, own:]
    small_keep[...] = jnp.zeros_like(small_keep)
    small_keep[0:112, :] = jnp.where(first, low, high)
    small_send[0:112, :] = jnp.where(first, high, low)
    for k in range(4):
        small_keep[109 + k : 110 + k, :] = db_ref[0:1, k * own : (k + 1) * own]
        small_send[109 + k : 110 + k, :] = db_ref[1:2, k * own : (k + 1) * own]
    for k in range(8):
        value = sums_ref[k // 2 : k // 2 + 1, (k % 2) * own : (k % 2 + 1) * own]
        small_keep[113 + k : 114 + k, :] = value
        small_send[113 + k : 114 + k, :] = value
    small_send[SMALL_ROWS:128, :] = jnp.zeros((128 - SMALL_ROWS, own), F32)
    small_pair = pair_copy(4, small_send, small_land)
    small_pair.start()
    apply_rows(rowop_ref, xh_ref, gh_ref)
    small_pair.wait_recv()
    small_keep[0:128, :] += small_land[...]

    per = small_keep.shape[0] // size
    mine = pl.ds(pl.multiple_of(me * per, 8), per)

    def scatter_copy(offset):
        target = lax.rem(me + offset, size)
        return pltpu.make_async_remote_copy(
            src_ref=small_keep.at[pl.ds(pl.multiple_of(target * per, 8), per), :],
            dst_ref=small_recv.at[offset - 1],
            send_sem=sc_send.at[offset - 1],
            recv_sem=sc_recv.at[offset - 1],
            device_id={"dp": target},
            device_id_type=pl.DeviceIdType.MESH,
        )

    def spread_copy(offset):
        target = lax.rem(me + offset, size)
        return pltpu.make_async_remote_copy(
            src_ref=small_out.at[mine, :],
            dst_ref=small_out.at[mine, :],
            send_sem=bc_send.at[offset - 1],
            recv_sem=bc_recv.at[offset - 1],
            device_id={"dp": target},
            device_id_type=pl.DeviceIdType.MESH,
        )

    for offset in range(1, size):
        scatter_copy(offset).start()
    mirror_out(gh_ref, mask_ref, gn_ref, gm_ref, skip_all)
    total = small_keep[mine, :]
    for offset in range(1, size):
        scatter_copy(offset).wait_recv()
        total = total + small_recv[offset - 1]
    small_out[mine, :] = total
    for offset in range(1, size):
        spread_copy(offset).start()

    def finish(t, carry):
        at = pl.ds(pl.multiple_of(t * block, block), block)
        dx_out[at, :] = (cot_ref[at, :].astype(F32) + gn_ref[at, :]).astype(BF16)
        return carry

    lax.fori_loop(0, rows // block, finish, 0)
    for step in range(5, 2 * ring.bits + 1):
        advance(step)
    if ring.bits == 0:
        pass
    for offset in range(1, size):
        spread_copy(offset).wait_recv()
    for offset in range(1, size):
        scatter_copy(offset).wait_send()
        spread_copy(offset).wait_send()
    ring.close()
    for copy in (pack_copy, first_copy, second_copy, grads_copy, small_pair):
        copy.wait_send()


def final_kernel(
    extent_ref, rate_ref, freq_ref, coef_ref, full_ref, small_ref, rate_out, freq_out, coef_out,
    skip_out, vec_out, dw_in_out, db_in_out, dw_out_out,
):
    channels, half_hidden = dw_in_out.shape
    for k in range(half_hidden // 128):
        dw_in_out[:, k * 128 : (k + 1) * 128] = full_ref[k * channels : (k + 1) * channels, :].astype(F32)
    base = channels * (half_hidden // 128)
    for k in range(channels // 128):
        dw_out_out[:, k * 128 : (k + 1) * 128] = full_ref[
            base + k * half_hidden : base + (k + 1) * half_hidden, :
        ].astype(F32)
    modes_grad(extent_ref, rate_ref, freq_ref, coef_ref, small_ref, rate_out, freq_out, coef_out)
    skip_out[...] = small_ref[108:109, :]
    db_in_out[...] = wide(small_ref, 109, 4)
    for k in range(4):
        vec_out[k : k + 1, :] = wide(small_ref, 113 + 2 * k, 2)


VM = pl.BlockSpec(memory_space=pltpu.VMEM)
SM = pl.BlockSpec(memory_space=pltpu.SMEM)


def shape(dims, kind=F32):
    return jax.ShapeDtypeStruct(dims, kind)


def to_rows(images):
    micro, count, channels, cells = images.shape
    return images.transpose(3, 0, 1, 2).reshape(cells * micro * count, channels)


def from_rows(rows, like):
    micro, count, channels, cells = like.shape
    return rows.reshape(cells, micro, count, channels).transpose(1, 2, 3, 0)


def on_device(
    size,
    pixels,
    grid_class,
    extent,
    ssm_rate,
    ssm_freq,
    ssm_coef,
    skip_gain,
    norm_gain,
    norm_bias,
    w_in,
    b_in,
    w_out,
    b_out,
    layer_scale,
    cotangent,
):
    micro, count, channels, cells = pixels.shape
    rows = micro * count * cells
    own = ssm_rate.shape[1]
    modes = ssm_rate.shape[2]
    half_hidden = b_in.shape[0]
    x = to_rows(pixels)
    cot = to_rows(cotangent)
    extent_row = extent.reshape(1, own)
    rate = ssm_rate.transpose(0, 2, 1)
    freq = ssm_freq.transpose(0, 2, 1)
    coef = ssm_coef.transpose(0, 2, 1)
    vec = jnp.stack([norm_gain, norm_bias, b_out, layer_scale])
    field = (rows, channels)
    grad_rows = 2 * channels * half_hidden // 128
    all_rows = 3 * size * chunk_rows(grad_rows, size)
    small_rows = max(128, 8 * size)
    bits = max(size.bit_length() - 1, 1)
    peers = max(size - 1, 1)
    DMA = pltpu.SemaphoreType.DMA
    block_out, dx, full, small = pl.pallas_call(
        partial(mega_kernel, size),
        out_shape=(
            shape(field, BF16),
            shape(field, BF16),
            shape((all_rows, 128), BF16),
            shape((small_rows, own)),
        ),
        in_specs=[SM] + [VM] * 11,
        out_specs=(VM,) * 4,
        scratch_shapes=[
            pltpu.VMEM((PACK_ROWS, own), F32),
            pltpu.VMEM((PACK_ROWS, own), F32),
            pltpu.VMEM(w_in.shape, BF16),
            pltpu.VMEM(w_out.shape, BF16),
            pltpu.VMEM((PACK_ROWS, channels), F32),
            pltpu.VMEM((1, channels), F32),
            pltpu.VMEM((rows, 128), F32),
            pltpu.VMEM((2 * GRID, 8, channels), F32),
            pltpu.VMEM((90, 8, channels), F32),
            pltpu.VMEM((45, 8, channels), F32),
            pltpu.VMEM(field, F32),
            pltpu.VMEM(field, F32),
            pltpu.VMEM(field, F32),
            pltpu.VMEM(field, F32),
            pltpu.VMEM(field, F32),
            pltpu.VMEM(field, BF16),
            pltpu.VMEM(field, BF16),
            pltpu.VMEM((rows, 256), BF16),
            pltpu.VMEM((rows, 256), BF16),
            pltpu.VMEM(field, F32),
            pltpu.VMEM(field, F32),
            pltpu.VMEM((rows, 128), F32),
            pltpu.VMEM(field, F32),
            pltpu.VMEM((162 * 8, channels), F32),
            pltpu.VMEM((81 * 8, channels), F32),
            pltpu.VMEM((112, channels), F32),
            pltpu.VMEM((3, half_hidden), F32),
            pltpu.VMEM((4, channels), F32),
            pltpu.VMEM((all_rows, 128), F32),
            pltpu.VMEM((grad_rows, 128), BF16),
            pltpu.VMEM((grad_rows, 128), BF16),
            pltpu.VMEM((all_rows, 128), BF16),
            pltpu.VMEM((all_rows, 128), BF16),
            pltpu.VMEM((small_rows, own), F32),
            pltpu.VMEM((128, own), F32),
            pltpu.VMEM((128, own), F32),
            pltpu.VMEM((peers, small_rows // size, own), F32),
            DMA((5,)),
            DMA((5,)),
            DMA((3, bits)),
            DMA((3, bits)),
            DMA((3, bits)),
            DMA((3, bits)),
            DMA((peers,)),
            DMA((peers,)),
            DMA((peers,)),
            DMA((peers,)),
        ],
        compiler_params=pltpu.CompilerParams(
            vmem_limit_bytes=VMEM_LIMIT, collective_id=0, has_side_effects=True
        ),
        name="block",
    )(
        grid_class,
        extent_row,
        rate,
        freq,
        coef,
        skip_gain.reshape(1, own),
        b_in.reshape(1, half_hidden),
        vec,
        w_in,
        w_out,
        x,
        cot,
    )
    g_rate, g_freq, g_coef, g_skip, g_vec, dw_in, db_in, dw_out = pl.pallas_call(
        final_kernel,
        out_shape=(
            shape((2, modes, own)),
            shape((2, modes, own)),
            shape((2, modes, own)),
            shape((1, own)),
            shape((4, channels)),
            shape(w_in.shape),
            shape((1, half_hidden)),
            shape(w_out.shape),
        ),
        in_specs=[VM] * 6,
        out_specs=(VM,) * 8,
        compiler_params=pltpu.CompilerParams(vmem_limit_bytes=VMEM_LIMIT),
        name="final",
    )(extent_row, rate, freq, coef, full, small)
    return (
        from_rows(block_out, pixels),
        from_rows(dx, pixels),
        g_rate.transpose(0, 2, 1),
        g_freq.transpose(0, 2, 1),
        g_coef.transpose(0, 2, 1),
        g_skip[0],
        g_vec[0],
        g_vec[1],
        dw_in,
        db_in[0],
        dw_out,
        g_vec[3],
        g_vec[2],
    )


def solution(mesh):
    placed = (
        P(None, ("dp", "mp"), None, None),
        P(None, "dp"),
        P("mp"),
        P(None, "mp", None),
        P(None, "mp", None),
        P(None, "mp", None),
        P("mp"),
        P(),
        P(),
        P(None, "mp"),
        P("mp"),
        P("mp", None),
        P(),
        P(),
        P(None, ("dp", "mp"), None, None),
    )
    return jax.shard_map(
        partial(on_device, mesh.shape["dp"]),
        mesh=mesh,
        in_specs=placed,
        out_specs=(
            P(None, ("dp", "mp"), None, None),
            P(None, ("dp", "mp"), None, None),
            P(None, "mp", None),
            P(None, "mp", None),
            P(None, "mp", None),
            P("mp"),
            P(),
            P(),
            P(None, "mp"),
            P("mp"),
            P("mp", None),
            P(),
            P(),
        ),
        check_vma=False,
    )
```

```python
import math
from functools import partial

import jax
import jax.numpy as jnp
import numpy as np
from jax import lax
from jax.experimental import pallas as pl
from jax.experimental.pallas import tpu as pltpu
from jax.sharding import PartitionSpec as P

GRID = 18
HALF = 9
SIDES = (10, 14, 18)
LAGS = 3 * GRID
F32 = jnp.float32
BF16 = jnp.bfloat16

ERF_SHIFT = 0.35 / math.sqrt(2.0)
ERF_POLY = (
    0.19396706,
    0.23864529,
    -0.01708609,
    0.69839275,
    -0.6929918,
    0.77818103,
    -0.19910822,
)
CHUNK = 256
VMEM_LIMIT = 60 * 1024 * 1024


def small_sincos(angle):
    sq = angle * angle
    cos = 1.0 + sq * (
        -1 / 2 + sq * (1 / 24 + sq * (-1 / 720 + sq * (1 / 40320 + sq * (-1 / 3628800))))
    )
    sin = angle * (
        1.0
        + sq * (-1 / 6 + sq * (1 / 120 + sq * (-1 / 5040 + sq * (1 / 362880 + sq * (-1 / 39916800)))))
    )
    return sin, cos


def mode_step(rate, freq, side):
    decay = jnp.exp(rate * (-1.0 / side))
    sin, cos = small_sincos(freq * (1.0 / side))
    return decay * cos, decay * sin


PACK_ROWS = 120
SMALL_ROWS = 121

def write_tables(extent_ref, rate_ref, freq_ref, coef_ref, out_ref):
    extent = extent_ref[...].reshape(1, extent_ref.shape[0])
    for axis in range(2):
        for cat, side in enumerate(SIDES):
            z_re, z_im = mode_step(rate_ref[axis], freq_ref[axis], side)
            w_re = coef_ref[axis]
            w_im = jnp.zeros_like(w_re)
            for lag in range(GRID):
                row = axis * LAGS + cat * GRID + lag
                if lag >= side:
                    out_ref[row : row + 1, :] = jnp.zeros((1, w_re.shape[1]), F32)
                    continue
                total = jnp.sum(w_re, axis=0, keepdims=True)
                out_ref[row : row + 1, :] = jnp.where(extent > lag, total, 0.0)
                if lag < side - 1:
                    w_re, w_im = w_re * z_re - w_im * z_im, w_re * z_im + w_im * z_re


def modes_grad(extent_ref, rate_ref, freq_ref, coef_ref, dk_ref, rate_out, freq_out, coef_out):
    extent = extent_ref[...].reshape(1, extent_ref.shape[0])
    for axis in range(2):
        coef = coef_ref[axis]
        g_rate = jnp.zeros_like(coef)
        g_freq = jnp.zeros_like(coef)
        g_coef = jnp.zeros_like(coef)
        for cat, side in enumerate(SIDES):
            z_re, z_im = mode_step(rate_ref[axis], freq_ref[axis], side)
            p_re = jnp.zeros_like(coef)
            p_im = jnp.zeros_like(coef)
            q_re = jnp.zeros_like(coef)
            q_im = jnp.zeros_like(coef)
            for lag in reversed(range(side)):
                row = axis * LAGS + cat * GRID + lag
                d = jnp.where(extent > lag, dk_ref[row : row + 1, :], 0.0)
                p_re, p_im = p_re * z_re - p_im * z_im + d, p_re * z_im + p_im * z_re
                q_re, q_im = q_re * z_re - q_im * z_im + float(lag) * d, q_re * z_im + q_im * z_re
            g_coef = g_coef + p_re
            g_rate = g_rate - (1.0 / side) * q_re
            g_freq = g_freq - (1.0 / side) * q_im
        coef_out[axis] = g_coef
        rate_out[axis] = g_rate * coef
        freq_out[axis] = g_freq * coef

def tri(a, b):
    low, high = min(a, b), max(a, b)
    return low * HALF - low * (low - 1) // 2 + (high - low)


def rows8(index):
    if isinstance(index, int):
        return pl.ds(index * 8, 8)
    return pl.ds(pl.multiple_of(index * 8, 8), 8)


def lanes(tile):
    if isinstance(tile, int):
        return pl.ds(tile * 128, 128)
    return pl.ds(pl.multiple_of(tile * 128, 128), 128)


def swap(value):
    return pltpu.roll(value, 4, 0)


def sublane_half():
    return lax.broadcasted_iota(jnp.int32, (8, 128), 0) < 4


def side_vreg(class_ref):
    mine = lax.axis_index("mp")
    image = lax.rem(lax.broadcasted_iota(jnp.int32, (8, 128), 0), 4)
    cls = jnp.zeros((8, 128), jnp.int32)
    own = class_ref.shape[1] // 2
    for micro in range(2):
        for img in range(2):
            cls = jnp.where(image == micro * 2 + img, class_ref[micro, mine * own + img], cls)
    return 10 + 4 * cls


def build_masks(class_ref, mask_ref):
    side = side_vreg(class_ref)
    offset = jnp.where(sublane_half(), 0, 1)

    def row(i, carry):
        for pair in range(HALF):
            ok = (i < side) & (2 * pair + offset < side)
            mask_ref[rows8(i * HALF + pair), :] = jnp.where(ok, 1.0, 0.0).astype(F32)
        return carry

    lax.fori_loop(0, GRID, row, 0)


def build_operators(class_ref, table_ref, lag_ref, rowop_ref, colop_ref):
    side = side_vreg(class_ref)
    sign = jnp.where(sublane_half(), 1.0, -1.0).astype(F32)
    tiles = table_ref.shape[1] // 128

    def tile_body(tile, carry):
        at = lanes(tile)
        for axis in range(2):
            for lag in range(GRID):
                by_side = [
                    jnp.broadcast_to(table_ref[axis * LAGS + cat * GRID + lag : axis * LAGS + cat * GRID + lag + 1, at], (8, 128))
                    for cat in range(3)
                ]
                lag_ref[axis * GRID + lag, :, at] = 0.5 * jnp.where(
                    side == 10, by_side[0], jnp.where(side == 14, by_side[1], by_side[2])
                )
        for a in range(HALF):
            for b in range(a, HALF):
                near = lag_ref[b - a, :, at]
                far = lag_ref[GRID - 1 - a - b, :, at]
                rowop_ref[tri(a, b), :, at] = near + far
                rowop_ref[45 + tri(a, b), :, at] = near - far
                near = lag_ref[GRID + b - a, :, at]
                far = lag_ref[GRID + GRID - 1 - a - b, :, at]
                colop_ref[tri(a, b), :, at] = near + sign * far
        return carry

    lax.fori_loop(0, tiles, tile_body, 0)


def mirror_in(source_ref, mask_ref, out_ref):
    half = sublane_half()
    sign = jnp.where(half, 1.0, -1.0).astype(F32)
    tiles = source_ref.shape[1] // 128

    def body(i, carry):
        for tile in range(tiles):
            at = lanes(tile)

            def mirrored(row, pair):
                near = source_ref[rows8(row * HALF + pair), at] * mask_ref[rows8(row * HALF + pair), :]
                if pair == 4:
                    return swap(near) + sign * near, None
                other = row * HALF + 8 - pair
                far = source_ref[rows8(other), at] * mask_ref[rows8(other), :]
                even = jnp.where(half, near, far)
                odd = jnp.where(half, far, near)
                return swap(even) + sign * even, odd + sign * swap(odd)

            for pair in range(5):
                top = mirrored(i, pair)
                bottom = mirrored(GRID - 1 - i, pair)
                for step in range(2 if pair < 4 else 1):
                    where = i * HALF + 2 * pair + step
                    out_ref[rows8(where), at] = top[step] + bottom[step]
                    out_ref[rows8(81 + where), at] = top[step] - bottom[step]
        return carry

    lax.fori_loop(0, HALF, body, 0)


def mirror_out(source_ref, mask_ref, out_ref, extra_ref, gain_ref):
    half = sublane_half()
    sign = jnp.where(half, 1.0, -1.0).astype(F32)
    tiles = source_ref.shape[1] // 128

    def body(i, carry):
        for tile in range(tiles):
            at = lanes(tile)
            gain = jnp.broadcast_to(gain_ref[:, at], (8, 128))

            def finish(index, value):
                value = value * mask_ref[rows8(index), :] + gain * extra_ref[rows8(index), at]
                out_ref[rows8(index), at] = value.astype(BF16).astype(F32)

            for pair in range(5):
                both = []
                for step in range(2 if pair < 4 else 1):
                    where = i * HALF + 2 * pair + step
                    plus = source_ref[rows8(where), at]
                    minus = source_ref[rows8(81 + where), at]
                    top, bottom = plus + minus, plus - minus
                    both.append(
                        (swap(top) + sign * top, swap(bottom) + sign * bottom)
                        if step == 0
                        else (top - sign * swap(top), bottom - sign * swap(bottom))
                    )
                for part, row in ((0, i), (1, GRID - 1 - i)):
                    if pair == 4:
                        finish(row * HALF + 4, both[0][part])
                        continue
                    if True:
                        even, odd = both[0][part], both[1][part]
                        finish(row * HALF + pair, jnp.where(half, even, odd))
                        finish(row * HALF + 8 - pair, jnp.where(half, odd, even))
        return carry

    lax.fori_loop(0, HALF, body, 0)


def apply_rows(op_ref, source_ref, out_ref):
    tiles = source_ref.shape[1] // 128

    def body(j, carry):
        for tile in range(tiles):
            at = lanes(tile)
            for rho in range(2):
                values = [source_ref[rows8(rho * 81 + p * HALF + j), at] for p in range(HALF)]
                for i in range(HALF):
                    total = None
                    for p in range(HALF):
                        term = op_ref[rho * 45 + tri(i, p), :, at] * values[p]
                        total = term if total is None else total + term
                    out_ref[rows8(rho * 81 + i * HALF + j), at] = total
        return carry

    lax.fori_loop(0, HALF, body, 0)


def apply_cols(op_ref, source_ref, out_ref):
    tiles = source_ref.shape[1] // 128

    def body(i, carry):
        for tile in range(tiles):
            at = lanes(tile)
            values = [source_ref[rows8(i * HALF + q), at] for q in range(HALF)]
            for j in range(HALF):
                total = None
                for q in range(HALF):
                    term = op_ref[tri(j, q), :, at] * values[q]
                    total = term if total is None else total + term
                out_ref[rows8(i * HALF + j), at] = total
        return carry

    lax.fori_loop(0, 2 * HALF, body, 0)


def row_correlate(left_ref, right_ref, acc_ref, cut=3):
    for tile in range(left_ref.shape[1] // 128):
        for rho in range(2):

            def body(step, carry, at=lanes(tile), rho=rho):
                first = step * cut
                sums = [[None] * HALF for _ in range(cut)]
                for j in range(HALF):
                    left = [
                        left_ref[rows8(rho * 81 + (first + k) * HALF + j), at] for k in range(cut)
                    ]
                    for p in range(HALF):
                        right = right_ref[rows8(rho * 81 + p * HALF + j), at]
                        for k in range(cut):
                            term = left[k] * right
                            sums[k][p] = term if sums[k][p] is None else sums[k][p] + term
                for k in range(cut):
                    for p in range(HALF):
                        acc_ref[rows8(rho * 81 + (first + k) * HALF + p), at] = sums[k][p]
                return carry

            lax.fori_loop(0, HALF // cut, body, 0)


def col_correlate(left_ref, right_ref, acc_ref, cut=3):
    for tile in range(left_ref.shape[1] // 128):

        def body(step, carry, at=lanes(tile)):
            first = step * cut
            sums = [[None] * HALF for _ in range(cut)]
            for i in range(2 * HALF):
                left = [left_ref[rows8(i * HALF + first + k), at] for k in range(cut)]
                for q in range(HALF):
                    right = right_ref[rows8(i * HALF + q), at]
                    for k in range(cut):
                        term = left[k] * right
                        sums[k][q] = term if sums[k][q] is None else sums[k][q] + term
            for k in range(cut):
                for q in range(HALF):
                    acc_ref[rows8((first + k) * HALF + q), at] = sums[k][q]
            return carry

        lax.fori_loop(0, HALF // cut, body, 0)


def gather_lags(class_ref, row_acc, col_acc, dk_ref):
    side = side_vreg(class_ref)
    sign = jnp.where(sublane_half(), 1.0, -1.0).astype(F32)
    tiles = row_acc.shape[1] // 128

    def body(tile, carry):
        at = lanes(tile)
        for axis in range(2):
            near = [None] * HALF
            far = [None] * GRID
            for a in range(HALF):
                for b in range(HALF):
                    if axis == 0:
                        plus = row_acc[rows8(a * HALF + b), at]
                        minus = row_acc[rows8(81 + a * HALF + b), at]
                        direct, cross = plus + minus, plus - minus
                    else:
                        direct = col_acc[rows8(a * HALF + b), at]
                        cross = sign * direct
                    d, s = abs(a - b), GRID - 1 - a - b
                    near[d] = direct if near[d] is None else near[d] + direct
                    far[s] = cross if far[s] is None else far[s] + cross
            for lag in range(GRID):
                total = None
                for part in ([near[lag]] if lag < HALF else []) + ([far[lag]] if lag else []):
                    total = part if total is None else total + part
                total = 0.5 * total
                for cat, length in enumerate(SIDES):
                    row = axis * LAGS + cat * GRID + lag
                    value = jnp.where(side == length, total, 0.0)
                    dk_ref[row : row + 1, at] = jnp.sum(value, axis=0, keepdims=True)
        return carry

    lax.fori_loop(0, tiles, body, 0)


def bit_orders(size, parts):
    bits = size.bit_length() - 1
    turn = min(3, max(bits, 1))
    base = list(range(bits))
    return [
        [base[(k + part) % turn] if k < turn else base[k] for k in range(bits)]
        for part in range(parts)
    ]


def ring_plan(rows, size):
    parts = 3 if rows % (48 * size) == 0 else 1
    per = -(-rows // (parts * size))
    return parts, -(-per // 16) * 16


class Ring:
    def __init__(self, group, size, plan, acc, send, recv, full, sems):
        self.group, self.size = group, size
        self.parts, self.rows = plan
        self.acc, self.send, self.recv, self.full = acc, send, recv, full
        self.send_sem, self.recv_sem, self.back_send, self.back_recv = sems
        self.orders = bit_orders(size, self.parts)
        self.bits = size.bit_length() - 1
        self.me = lax.axis_index("dp")
        self.place = []
        for order in self.orders:
            place = 0
            for bit in order:
                place = place * 2 + lax.rem(self.me // (1 << bit), 2)
            self.place.append(place)

    def base(self, part):
        return (self.group * self.parts + part) * self.size * self.rows

    def peer(self, bit):
        mine = lax.rem(self.me // (1 << bit), 2)
        return self.me + (1 - 2 * mine) * (1 << bit)

    def span(self, part, step):
        half = self.size >> (step + 1)
        index = self.place[part] // half
        mine = lax.rem(index, 2)
        keep = self.base(part) + index * half * self.rows
        away = self.base(part) + (index + 1 - 2 * mine) * half * self.rows
        return pl.multiple_of(keep, 16), pl.multiple_of(away, 16), half * self.rows

    def slot(self, part, step):
        done = self.size - (self.size >> step)
        return self.base(part) + done * self.rows

    def sem(self, sems, part, step):
        return sems.at[self.group * self.parts + part, step]

    def reduce_copy(self, part, step):
        _, away, length = self.span(part, step)
        return pltpu.make_async_remote_copy(
            src_ref=self.send.at[pl.ds(away, length), :],
            dst_ref=self.recv.at[pl.ds(self.slot(part, step), length), :],
            send_sem=self.sem(self.send_sem, part, step),
            recv_sem=self.sem(self.recv_sem, part, step),
            device_id={"dp": self.peer(self.orders[part][step])},
            device_id_type=pl.DeviceIdType.MESH,
        )

    def gather_copy(self, part, step):
        keep, _, length = self.span(part, step)
        return pltpu.make_async_remote_copy(
            src_ref=self.full.at[pl.ds(keep, length), :],
            dst_ref=self.full.at[pl.ds(keep, length), :],
            send_sem=self.sem(self.back_send, part, step),
            recv_sem=self.sem(self.back_recv, part, step),
            device_id={"dp": self.peer(self.orders[part][step])},
            device_id_type=pl.DeviceIdType.MESH,
        )

    def reduce_start(self, step):
        for part in range(self.parts):
            _, away, length = self.span(part, step)
            copy_rows(self.acc, away, self.send, away, length, lambda v: v.astype(BF16))
            self.reduce_copy(part, step).start()

    def reduce_finish(self, step):
        for part in range(self.parts):
            self.reduce_copy(part, step).wait_recv()
            keep, _, length = self.span(part, step)
            add_rows(self.recv, self.slot(part, step), self.acc, keep, length)

    def gather_first(self):
        for part in range(self.parts):
            own = pl.multiple_of(self.base(part) + self.place[part] * self.rows, 16)
            copy_rows(self.acc, own, self.full, own, self.rows, lambda v: v.astype(BF16))

    def gather_start(self, step):
        for part in range(self.parts):
            self.gather_copy(part, step).start()

    def gather_finish(self, step):
        for part in range(self.parts):
            self.gather_copy(part, step).wait_recv()

    def advance(self, step):
        bits = self.bits
        if step > 2 * bits:
            return
        if 0 < step <= bits:
            self.reduce_finish(step - 1)
        if step > bits:
            self.gather_finish(2 * bits - step)
        if step < bits:
            self.reduce_start(step)
        if step == bits:
            self.gather_first()
        if bits <= step < 2 * bits:
            self.gather_start(2 * bits - 1 - step)

    def close(self):
        for part in range(self.parts):
            for step in range(self.bits):
                self.reduce_copy(part, step).wait_send()
                self.gather_copy(part, step).wait_send()


def row_block(length):
    return next(block for block in (128, 96, 64, 48, 32, 16) if length % block == 0)


def add_rows(source, first, target, where, length):
    block = row_block(length)

    def body(t, carry):
        here = pl.ds(pl.multiple_of(first + t * block, 16), block)
        there = pl.ds(pl.multiple_of(where + t * block, 16), block)
        target[there, :] += source[here, :].astype(F32)
        return carry

    lax.fori_loop(0, length // block, body, 0)


def copy_rows(source, first, target, where, length, change):
    block = row_block(length)

    def body(t, carry):
        here = pl.ds(pl.multiple_of(first + t * block, 16), block)
        there = pl.ds(pl.multiple_of(where + t * block, 16), block)
        target[there, :] = change(source[here, :])
        return carry

    lax.fori_loop(0, length // block, body, 0)


def wide(ref, first, count):
    return jnp.concatenate([ref[first + k : first + k + 1, :] for k in range(count)], axis=1)


def images_in(ref, first, count):
    parts = [ref[micro, pl.ds(first, count), :, :].astype(F32) for micro in range(2)]
    return jnp.concatenate(parts, axis=1).reshape(4 * count, ref.shape[3])


def images_out(ref, first, count, value):
    value = value.reshape(count, 4, ref.shape[3])
    for micro in range(2):
        ref[micro, pl.ds(first, count)] = value[:, 2 * micro : 2 * micro + 2, :].astype(BF16)


def mega_kernel(
    size,
    class_ref,
    extent_ref,
    rate_ref,
    freq_ref,
    coef_ref,
    skip_ref,
    b_in_ref,
    gain_ref,
    shift_ref,
    b_out_ref,
    scale_ref,
    w_in_ref,
    w_out_ref,
    x_ref,
    cot_ref,
    block_out,
    dx_out,
    full_out,
    small_out,
    pack_own,
    pack_oth,
    w_in_oth,
    w_out_oth,
    table_ref,
    skip_all,
    mask_ref,
    lag_ref,
    rowop_ref,
    colop_ref,
    u_ref,
    uh_ref,
    v_ref,
    mh_ref,
    mixed_ref,
    normed_ref,
    gmlp_ref,
    act_ref,
    gpre_ref,
    mlp_ref,
    gn_ref,
    stat_ref,
    gm_ref,
    row_acc,
    col_acc,
    dk_ref,
    db_ref,
    sums_ref,
    acc_ref,
    away_ref,
    landed_ref,
    send_ref,
    recv_ref,
    small_keep,
    small_send,
    small_land,
    small_recv,
    pair_send,
    pair_recv,
    red_send,
    red_recv,
    gat_send,
    gat_recv,
    sc_send,
    sc_recv,
    bc_send,
    bc_recv,
):
    cells, channels = x_ref.shape[1], x_ref.shape[3]
    rows = 4 * cells
    own = pack_own.shape[1]
    half_hidden = w_in_ref.shape[1]
    me = lax.axis_index("dp")
    core = lax.axis_index("mp")
    partner = {"mp": 1 - core}

    barrier = pltpu.get_barrier_semaphore()
    pl.semaphore_signal(barrier, inc=1, device_id=partner, device_id_type=pl.DeviceIdType.MESH)
    for offset in range(1, size):
        pl.semaphore_signal(
            barrier,
            inc=1,
            device_id={"dp": lax.rem(me + offset, size)},
            device_id_type=pl.DeviceIdType.MESH,
        )

    def pair_copy(index, source, target):
        return pltpu.make_async_remote_copy(
            src_ref=source,
            dst_ref=target,
            send_sem=pair_send.at[index],
            recv_sem=pair_recv.at[index],
            device_id=partner,
            device_id_type=pl.DeviceIdType.MESH,
        )

    write_tables(extent_ref, rate_ref, freq_ref, coef_ref, pack_own)
    pack_own[108:109, :] = skip_ref[...].reshape(1, own)
    b_in = b_in_ref[...].reshape(1, half_hidden)
    for k in range(4):
        pack_own[109 + k : 110 + k, :] = b_in[:, k * own : (k + 1) * own]
    pack_own[113:PACK_ROWS, :] = jnp.zeros((PACK_ROWS - 113, own), F32)
    pl.semaphore_wait(barrier, size)
    pack_copy = pair_copy(0, pack_own, pack_oth)
    first_copy = pair_copy(1, w_in_ref, w_in_oth)
    second_copy = pair_copy(2, w_out_ref, w_out_oth)
    pack_copy.start()
    first_copy.start()
    second_copy.start()

    build_masks(class_ref, mask_ref)
    block = 144
    scale = scale_ref[...].reshape(1, channels)

    def load(t, carry):
        at = pl.ds(pl.multiple_of(t * 48, 16), 48)
        u_ref[at, :] = images_in(x_ref, t * 12, 12)
        mask = jnp.tile(mask_ref[at, :], (1, channels // 128))
        gmlp_ref[at, :] = (images_in(cot_ref, t * 12, 12) * scale * mask).astype(BF16)
        return carry

    lax.fori_loop(0, rows // 48, load, 0)
    mirror_in(u_ref, mask_ref, uh_ref)

    pack_copy.wait_recv()
    first = core == 0
    low = jnp.where(first, pack_own[...], pack_oth[...])
    high = jnp.where(first, pack_oth[...], pack_own[...])
    table_ref[...] = jnp.concatenate([low, high], axis=1)
    skip_all[...] = table_ref[108:109, :]
    build_operators(class_ref, table_ref, lag_ref, rowop_ref, colop_ref)
    apply_rows(rowop_ref, uh_ref, v_ref)
    apply_cols(colop_ref, v_ref, mh_ref)
    mirror_out(mh_ref, mask_ref, mixed_ref, u_ref, skip_all)

    gain = gain_ref[...].reshape(1, channels)
    shift = shift_ref[...].reshape(1, channels)

    def norm(t, carry):
        at = pl.ds(pl.multiple_of(t * block, block), block)
        value = mixed_ref[at, :]
        mean = jnp.mean(value, axis=1, keepdims=True)
        centered = value - mean
        variance = jnp.mean(centered * centered, axis=1, keepdims=True)
        rstd = lax.rsqrt(variance + 1e-06)
        hat = centered * rstd
        mixed_ref[at, :] = hat
        stat_ref[at, :] = jnp.broadcast_to(rstd, (block, 128))
        normed_ref[at, :] = (hat * gain + shift).astype(BF16)
        return carry

    lax.fori_loop(0, rows // block, norm, 0)

    chunk = CHUNK
    tile_rows = 432
    mlp_ref[...] = jnp.broadcast_to(b_out_ref[...].reshape(1, channels), mlp_ref.shape)
    gn_ref[...] = jnp.zeros_like(gn_ref)
    first_copy.wait_recv()
    second_copy.wait_recv()

    group_rows = 2 * channels * chunk // 128
    plan = ring_plan(group_rows, size)
    stride = plan[0] * plan[1] * size
    groups = half_hidden // chunk
    rings = [
        Ring(group, size, plan, acc_ref, send_ref, recv_ref, full_out,
             (red_send, red_recv, gat_send, gat_recv))
        for group in range(groups)
    ]
    db_ref[2:3, :] = wide(pack_oth, 109, 4)
    db_ref[3:4, :] = b_in

    def feed(f, w_first_ref, w_second_ref, bias_row, target_ref, target_base, db_row):
        cols = pl.ds(pl.multiple_of(f * chunk, chunk), chunk)
        w_first = w_first_ref[:, cols]
        w_second = w_second_ref[cols, :]
        bias = db_ref[bias_row : bias_row + 1, cols]
        db = jnp.zeros((1, chunk), F32)
        for t in range(rows // tile_rows):
            at = pl.ds(t * tile_rows, tile_rows)
            pre = jnp.dot(normed_ref[at, :], w_first, preferred_element_type=F32) + bias
            inv = 1.0 / (1.0 + ERF_SHIFT * jnp.abs(pre))
            poly = jnp.full_like(inv, 0.5 * ERF_POLY[-1])
            for value in reversed(ERF_POLY[:-1]):
                poly = poly * inv + 0.5 * value
            bell = jnp.exp(-0.5 * pre * pre)
            tail = poly * inv * bell
            cdf = jnp.where(pre >= 0.0, 1.0 - tail, tail)
            act = (pre * cdf).astype(BF16)
            slope = cdf + pre * bell * (1.0 / math.sqrt(2.0 * math.pi))
            g_act = lax.dot_general(
                gmlp_ref[at, :], w_second, (((1,), (1,)), ((), ())), preferred_element_type=F32
            )
            g_pre = (g_act * slope).astype(BF16)
            db = db + jnp.sum(g_pre.astype(F32), axis=0, keepdims=True)
            act_ref[at, :] = act
            gpre_ref[at, :] = g_pre
            mlp_ref[at, :] += jnp.dot(act, w_second, preferred_element_type=F32)
            gn_ref[at, :] += lax.dot_general(
                g_pre, w_first, (((1,), (1,)), ((), ())), preferred_element_type=F32
            )
        db_ref[db_row : db_row + 1, cols] = db
        d_first = lax.dot_general(
            normed_ref[...], gpre_ref[...], (((0,), (0,)), ((), ())), preferred_element_type=F32
        )
        for k in range(chunk // 128):
            at = pl.ds(pl.multiple_of(target_base + k * channels, 128), channels)
            target_ref[at, :] = d_first[:, k * 128 : (k + 1) * 128].astype(target_ref.dtype)
        d_second = lax.dot_general(
            act_ref[...], gmlp_ref[...], (((0,), (0,)), ((), ())), preferred_element_type=F32
        )
        base = target_base + channels * (chunk // 128)
        for k in range(channels // 128):
            at = pl.ds(pl.multiple_of(base + k * chunk, 128), chunk)
            target_ref[at, :] = d_second[:, k * 128 : (k + 1) * 128].astype(target_ref.dtype)

    def grads_copy(group):
        at = pl.ds(pl.multiple_of(group * group_rows, 16), group_rows)
        return pair_copy(4 + group, away_ref.at[at, :], landed_ref.at[at, :])

    def join(group):
        grads_copy(group).wait_recv()
        add_rows(landed_ref, pl.multiple_of(group * group_rows, 16), acc_ref,
                 pl.multiple_of(group * stride, 16), group_rows)
        if stride > group_rows:
            acc_ref[pl.ds(pl.multiple_of(group * stride + group_rows, 16), stride - group_rows), :] = (
                jnp.zeros((stride - group_rows, 128), F32)
            )

    def tick(count):
        for group in reversed(range(groups)):
            step = count - 2 * group
            if 0 <= step <= 2 * rings[group].bits:
                rings[group].advance(step)

    def pair_of_chunks(f, carry):
        feed(f, w_in_oth, w_out_oth, 2, away_ref, f * group_rows, 1)
        grads_copy(f).start()
        for count in range(1, groups):
            pl.when(f == count)(partial(tick, 2 * count - 1))
        feed(f, w_in_ref, w_out_ref, 3, acc_ref, f * stride, 0)
        join(f)
        for count in range(groups):
            pl.when(f == count)(partial(tick, 2 * count))
        return carry

    lax.fori_loop(0, groups, pair_of_chunks, 0)
    last = 2 * rings[0].bits + 2 * (groups - 1)
    ticks = iter(range(2 * groups - 1, last + 1))

    def advance():
        count = next(ticks, None)
        if count is not None:
            tick(count)

    def back(t, carry):
        d_gain, d_bias, d_scale, d_b_out = carry
        at = pl.ds(pl.multiple_of(t * 48, 16), 48)
        mask = jnp.tile(mask_ref[at, :], (1, channels // 128))
        branch = mlp_ref[at, :] * mask
        images_out(block_out, t * 12, 12, u_ref[at, :] + scale * branch)
        d_scale = d_scale + jnp.sum(images_in(cot_ref, t * 12, 12) * branch, axis=0, keepdims=True)
        d_b_out = d_b_out + jnp.sum(gmlp_ref[at, :].astype(F32), axis=0, keepdims=True)
        grad = gn_ref[at, :]
        hat = mixed_ref[at, :]
        d_gain = d_gain + jnp.sum(grad * hat, axis=0, keepdims=True)
        d_bias = d_bias + jnp.sum(grad, axis=0, keepdims=True)
        grad = grad * gain
        mean_g = jnp.mean(grad, axis=1, keepdims=True)
        mean_gh = jnp.mean(grad * hat, axis=1, keepdims=True)
        rstd = jnp.tile(stat_ref[at, :], (1, channels // 128))
        gm_ref[at, :] = (rstd * (grad - mean_g - hat * mean_gh)).astype(BF16).astype(F32)
        return d_gain, d_bias, d_scale, d_b_out

    zero = jnp.zeros((1, channels), F32)
    sums = lax.fori_loop(0, rows // 48, back, (zero, zero, zero, zero))
    for index, value in enumerate(sums):
        sums_ref[index : index + 1, :] = value

    gh_ref, xh_ref = mh_ref, mlp_ref
    advance()
    mirror_in(gm_ref, mask_ref, gh_ref)
    apply_cols(colop_ref, gh_ref, xh_ref)
    advance()
    row_correlate(xh_ref, uh_ref, row_acc)
    advance()
    col_correlate(gh_ref, v_ref, col_acc)
    advance()
    gather_lags(class_ref, row_acc, col_acc, dk_ref)

    def skip_sum(t, total):
        at = pl.ds(pl.multiple_of(t * block, block), block)
        return total + jnp.sum(gm_ref[at, :] * u_ref[at, :], axis=0, keepdims=True)

    dk_ref[108:109, :] = lax.fori_loop(0, rows // block, skip_sum, zero)
    dk_ref[109:112, :] = jnp.zeros((3, channels), F32)
    low = dk_ref[:, :own]
    high = dk_ref[:, own:]
    small_keep[...] = jnp.zeros_like(small_keep)
    small_keep[0:112, :] = jnp.where(first, low, high)
    small_send[0:112, :] = jnp.where(first, high, low)
    for k in range(4):
        small_keep[109 + k : 110 + k, :] = db_ref[0:1, k * own : (k + 1) * own]
        small_send[109 + k : 110 + k, :] = db_ref[1:2, k * own : (k + 1) * own]
    for k in range(8):
        value = sums_ref[k // 2 : k // 2 + 1, (k % 2) * own : (k % 2 + 1) * own]
        small_keep[113 + k : 114 + k, :] = value
        small_send[113 + k : 114 + k, :] = value
    small_send[SMALL_ROWS:128, :] = jnp.zeros((128 - SMALL_ROWS, own), F32)
    small_pair = pair_copy(3, small_send, small_land)
    small_pair.start()
    apply_rows(rowop_ref, xh_ref, gh_ref)
    advance()
    small_pair.wait_recv()
    small_keep[0:128, :] += small_land[...]

    per = small_keep.shape[0] // size
    mine = pl.ds(pl.multiple_of(me * per, 8), per)

    def scatter_copy(offset):
        target = lax.rem(me + offset, size)
        return pltpu.make_async_remote_copy(
            src_ref=small_keep.at[pl.ds(pl.multiple_of(target * per, 8), per), :],
            dst_ref=small_recv.at[offset - 1],
            send_sem=sc_send.at[offset - 1],
            recv_sem=sc_recv.at[offset - 1],
            device_id={"dp": target},
            device_id_type=pl.DeviceIdType.MESH,
        )

    def spread_copy(offset):
        target = lax.rem(me + offset, size)
        return pltpu.make_async_remote_copy(
            src_ref=small_out.at[mine, :],
            dst_ref=small_out.at[mine, :],
            send_sem=bc_send.at[offset - 1],
            recv_sem=bc_recv.at[offset - 1],
            device_id={"dp": target},
            device_id_type=pl.DeviceIdType.MESH,
        )

    for offset in range(1, size):
        scatter_copy(offset).start()
    mirror_out(gh_ref, mask_ref, gn_ref, gm_ref, skip_all)
    advance()
    total = small_keep[mine, :]
    for offset in range(1, size):
        scatter_copy(offset).wait_recv()
        total = total + small_recv[offset - 1]
    small_out[mine, :] = total
    for offset in range(1, size):
        spread_copy(offset).start()

    def finish(t, carry):
        at = pl.ds(pl.multiple_of(t * 48, 16), 48)
        images_out(dx_out, t * 12, 12, images_in(cot_ref, t * 12, 12) + gn_ref[at, :])
        return carry

    lax.fori_loop(0, rows // 48, finish, 0)
    for _ in range(last + 1):
        advance()
    for offset in range(1, size):
        spread_copy(offset).wait_recv()
    for offset in range(1, size):
        scatter_copy(offset).wait_send()
        spread_copy(offset).wait_send()
    for group in range(groups):
        rings[group].close()
        grads_copy(group).wait_send()
    for copy in (pack_copy, first_copy, second_copy, small_pair):
        copy.wait_send()


def final_kernel(
    extent_ref, rate_ref, freq_ref, coef_ref, full_ref, small_ref, rate_out, freq_out, coef_out,
    skip_out, gain_out, bias_out, dw_in_out, db_in_out, dw_out_out, b_out_out, scale_out,
):
    channels, half_hidden = dw_in_out.shape
    groups = half_hidden // CHUNK
    stride = full_ref.shape[0] // groups
    for group in range(groups):
        base = group * stride
        for k in range(CHUNK // 128):
            at = group * CHUNK + k * 128
            dw_in_out[:, at : at + 128] = full_ref[base : base + channels, :].astype(F32)
            base += channels
        for k in range(channels // 128):
            dw_out_out[group * CHUNK : (group + 1) * CHUNK, k * 128 : (k + 1) * 128] = full_ref[
                base : base + CHUNK, :
            ].astype(F32)
            base += CHUNK
    modes_grad(extent_ref, rate_ref, freq_ref, coef_ref, small_ref, rate_out, freq_out, coef_out)
    skip_out[...] = small_ref[108:109, :].reshape(skip_out.shape)
    db_in_out[...] = wide(small_ref, 109, 4).reshape(db_in_out.shape)
    for k, ref in enumerate((gain_out, bias_out, scale_out, b_out_out)):
        ref[...] = wide(small_ref, 113 + 2 * k, 2).reshape(ref.shape)


VM = pl.BlockSpec(memory_space=pltpu.VMEM)
SM = pl.BlockSpec(memory_space=pltpu.SMEM)


def shape(dims, kind=F32):
    return jax.ShapeDtypeStruct(dims, kind)


def on_device(
    size,
    pixels,
    grid_class,
    extent,
    ssm_rate,
    ssm_freq,
    ssm_coef,
    skip_gain,
    norm_gain,
    norm_bias,
    w_in,
    b_in,
    w_out,
    b_out,
    layer_scale,
    cotangent,
):
    micro, count, channels, cells = pixels.shape
    rows = micro * count * cells
    own = ssm_rate.shape[1]
    modes = ssm_rate.shape[2]
    half_hidden = b_in.shape[0]
    x = pixels.transpose(0, 3, 1, 2)
    cot = cotangent.transpose(0, 3, 1, 2)
    rate = ssm_rate.transpose(0, 2, 1)
    freq = ssm_freq.transpose(0, 2, 1)
    coef = ssm_coef.transpose(0, 2, 1)
    field = (rows, channels)
    grad_rows = 2 * channels * half_hidden // 128
    groups = half_hidden // CHUNK
    parts, per = ring_plan(grad_rows // groups, size)
    all_rows = groups * parts * per * size
    small_rows = max(128, 8 * size)
    bits = max(size.bit_length() - 1, 1)
    peers = max(size - 1, 1)
    DMA = pltpu.SemaphoreType.DMA
    block_out, dx, full, small = pl.pallas_call(
        partial(mega_kernel, size),
        out_shape=(
            shape(x.shape, BF16),
            shape(x.shape, BF16),
            shape((all_rows, 128), BF16),
            shape((small_rows, own)),
        ),
        in_specs=[SM] + [VM] * 14,
        out_specs=(VM,) * 4,
        scratch_shapes=[
            pltpu.VMEM((PACK_ROWS, own), F32),
            pltpu.VMEM((PACK_ROWS, own), F32),
            pltpu.VMEM(w_in.shape, BF16),
            pltpu.VMEM(w_out.shape, BF16),
            pltpu.VMEM((PACK_ROWS, channels), F32),
            pltpu.VMEM((1, channels), F32),
            pltpu.VMEM((rows, 128), F32),
            pltpu.VMEM((2 * GRID, 8, channels), F32),
            pltpu.VMEM((90, 8, channels), F32),
            pltpu.VMEM((45, 8, channels), F32),
            pltpu.VMEM(field, F32),
            pltpu.VMEM(field, F32),
            pltpu.VMEM(field, F32),
            pltpu.VMEM(field, F32),
            pltpu.VMEM(field, F32),
            pltpu.VMEM(field, BF16),
            pltpu.VMEM(field, BF16),
            pltpu.VMEM((rows, 256), BF16),
            pltpu.VMEM((rows, 256), BF16),
            pltpu.VMEM(field, F32),
            pltpu.VMEM(field, F32),
            pltpu.VMEM((rows, 128), F32),
            pltpu.VMEM(field, F32),
            pltpu.VMEM((162 * 8, channels), F32),
            pltpu.VMEM((81 * 8, channels), F32),
            pltpu.VMEM((112, channels), F32),
            pltpu.VMEM((4, half_hidden), F32),
            pltpu.VMEM((4, channels), F32),
            pltpu.VMEM((all_rows, 128), F32),
            pltpu.VMEM((grad_rows, 128), BF16),
            pltpu.VMEM((grad_rows, 128), BF16),
            pltpu.VMEM((all_rows, 128), BF16),
            pltpu.VMEM((all_rows, 128), BF16),
            pltpu.VMEM((small_rows, own), F32),
            pltpu.VMEM((128, own), F32),
            pltpu.VMEM((128, own), F32),
            pltpu.VMEM((peers, small_rows // size, own), F32),
            DMA((4 + groups,)),
            DMA((4 + groups,)),
            DMA((groups * parts, bits)),
            DMA((groups * parts, bits)),
            DMA((groups * parts, bits)),
            DMA((groups * parts, bits)),
            DMA((peers,)),
            DMA((peers,)),
            DMA((peers,)),
            DMA((peers,)),
        ],
        compiler_params=pltpu.CompilerParams(
            vmem_limit_bytes=VMEM_LIMIT, collective_id=0, has_side_effects=True
        ),
        name="block",
    )(
        grid_class,
        extent,
        rate,
        freq,
        coef,
        skip_gain,
        b_in,
        norm_gain,
        norm_bias,
        b_out,
        layer_scale,
        w_in,
        w_out,
        x,
        cot,
    )
    g_rate, g_freq, g_coef, g_skip, g_gain, g_bias, dw_in, db_in, dw_out, g_b_out, g_scale = pl.pallas_call(
        final_kernel,
        out_shape=(
            shape((2, modes, own)),
            shape((2, modes, own)),
            shape((2, modes, own)),
            shape((own,)),
            shape((channels,)),
            shape((channels,)),
            shape(w_in.shape),
            shape((half_hidden,)),
            shape(w_out.shape),
            shape((channels,)),
            shape((channels,)),
        ),
        in_specs=[VM] * 6,
        out_specs=(VM,) * 11,
        compiler_params=pltpu.CompilerParams(vmem_limit_bytes=VMEM_LIMIT),
        name="final",
    )(extent, rate, freq, coef, full, small)
    return (
        block_out.transpose(0, 2, 3, 1),
        dx.transpose(0, 2, 3, 1),
        g_rate.transpose(0, 2, 1),
        g_freq.transpose(0, 2, 1),
        g_coef.transpose(0, 2, 1),
        g_skip,
        g_gain,
        g_bias,
        dw_in,
        db_in,
        dw_out,
        g_b_out,
        g_scale,
    )


def solution(mesh):
    placed = (
        P(None, ("dp", "mp"), None, None),
        P(None, "dp"),
        P("mp"),
        P(None, "mp", None),
        P(None, "mp", None),
        P(None, "mp", None),
        P("mp"),
        P(),
        P(),
        P(None, "mp"),
        P("mp"),
        P("mp", None),
        P(),
        P(),
        P(None, ("dp", "mp"), None, None),
    )
    return jax.shard_map(
        partial(on_device, mesh.shape["dp"]),
        mesh=mesh,
        in_specs=placed,
        out_specs=(
            P(None, ("dp", "mp"), None, None),
            P(None, ("dp", "mp"), None, None),
            P(None, "mp", None),
            P(None, "mp", None),
            P(None, "mp", None),
            P("mp"),
            P(),
            P(),
            P(None, "mp"),
            P("mp"),
            P("mp", None),
            P(),
            P(),
        ),
        check_vma=False,
    )
```

```python
import math
from functools import partial

import jax
import jax.numpy as jnp
import numpy as np
from jax import lax
from jax.experimental import pallas as pl
from jax.experimental.pallas import tpu as pltpu
from jax.sharding import PartitionSpec as P

GRID = 18
HALF = 9
SIDES = (10, 14, 18)
LAGS = 3 * GRID
F32 = jnp.float32
BF16 = jnp.bfloat16

ERF_SHIFT = 0.35 / math.sqrt(2.0)
ERF_POLY = (
    0.19396706,
    0.23864529,
    -0.01708609,
    0.69839275,
    -0.6929918,
    0.77818103,
    -0.19910822,
)
CHUNK = 256
VMEM_LIMIT = 60 * 1024 * 1024


def small_sincos(angle):
    sq = angle * angle
    cos = 1.0 + sq * (
        -1 / 2 + sq * (1 / 24 + sq * (-1 / 720 + sq * (1 / 40320 + sq * (-1 / 3628800))))
    )
    sin = angle * (
        1.0
        + sq * (-1 / 6 + sq * (1 / 120 + sq * (-1 / 5040 + sq * (1 / 362880 + sq * (-1 / 39916800)))))
    )
    return sin, cos


def mode_step(rate, freq, side):
    decay = jnp.exp(rate * (-1.0 / side))
    sin, cos = small_sincos(freq * (1.0 / side))
    return decay * cos, decay * sin


PACK_ROWS = 112
SUM_ROWS = 128
WIDE = 512


def write_tables(extent_ref, rate_ref, freq_ref, coef_ref, out_ref):
    extent = extent_ref[...].reshape(1, extent_ref.shape[0])
    for axis in range(2):
        for cat, side in enumerate(SIDES):
            z_re, z_im = mode_step(rate_ref[axis], freq_ref[axis], side)
            w_re = coef_ref[axis]
            w_im = jnp.zeros_like(w_re)
            for lag in range(GRID):
                row = axis * LAGS + cat * GRID + lag
                if lag >= side:
                    out_ref[row : row + 1, :] = jnp.zeros((1, w_re.shape[1]), F32)
                    continue
                total = jnp.sum(w_re, axis=0, keepdims=True)
                out_ref[row : row + 1, :] = jnp.where(extent > lag, total, 0.0)
                if lag < side - 1:
                    w_re, w_im = w_re * z_re - w_im * z_im, w_re * z_im + w_im * z_re


def modes_grad(axis, extent_ref, rate_ref, freq_ref, coef_ref, dk_ref, rate_out, freq_out, coef_out):
    extent = extent_ref[...].reshape(1, extent_ref.shape[0])
    if True:
        coef = coef_ref[axis]
        g_rate = jnp.zeros_like(coef)
        g_freq = jnp.zeros_like(coef)
        g_coef = jnp.zeros_like(coef)
        for cat, side in enumerate(SIDES):
            z_re, z_im = mode_step(rate_ref[axis], freq_ref[axis], side)
            p_re = jnp.zeros_like(coef)
            p_im = jnp.zeros_like(coef)
            q_re = jnp.zeros_like(coef)
            q_im = jnp.zeros_like(coef)
            for lag in reversed(range(side)):
                row = axis * LAGS + cat * GRID + lag
                d = jnp.where(extent > lag, dk_ref[row : row + 1, :], 0.0)
                p_re, p_im = p_re * z_re - p_im * z_im + d, p_re * z_im + p_im * z_re
                q_re, q_im = q_re * z_re - q_im * z_im + float(lag) * d, q_re * z_im + q_im * z_re
            g_coef = g_coef + p_re
            g_rate = g_rate - (1.0 / side) * q_re
            g_freq = g_freq - (1.0 / side) * q_im
        coef_out[axis] = g_coef
        rate_out[axis] = g_rate * coef
        freq_out[axis] = g_freq * coef

def tri(a, b):
    low, high = min(a, b), max(a, b)
    return low * HALF - low * (low - 1) // 2 + (high - low)


def rows8(index):
    if isinstance(index, int):
        return pl.ds(index * 8, 8)
    return pl.ds(pl.multiple_of(index * 8, 8), 8)


def lanes(tile):
    if isinstance(tile, int):
        return pl.ds(tile * 128, 128)
    return pl.ds(pl.multiple_of(tile * 128, 128), 128)


def swap(value):
    return pltpu.roll(value, 4, 0)


def sublane_half():
    return lax.broadcasted_iota(jnp.int32, (8, 128), 0) < 4


def side_vreg(class_ref):
    mine = lax.axis_index("mp")
    image = lax.rem(lax.broadcasted_iota(jnp.int32, (8, 128), 0), 4)
    cls = jnp.zeros((8, 128), jnp.int32)
    own = class_ref.shape[1] // 2
    for micro in range(2):
        for img in range(2):
            cls = jnp.where(image == micro * 2 + img, class_ref[micro, mine * own + img], cls)
    return 10 + 4 * cls


def build_masks(class_ref, mask_ref):
    side = side_vreg(class_ref)
    offset = jnp.where(sublane_half(), 0, 1)

    def row(i, carry):
        for pair in range(HALF):
            ok = (i < side) & (2 * pair + offset < side)
            mask_ref[rows8(i * HALF + pair), :] = jnp.where(ok, 1.0, 0.0).astype(F32)
        return carry

    lax.fori_loop(0, GRID, row, 0)


def build_operators(class_ref, table_ref, lag_ref, rowop_ref, colop_ref):
    side = side_vreg(class_ref)
    sign = jnp.where(sublane_half(), 1.0, -1.0).astype(F32)
    tiles = table_ref.shape[1] // 128

    def tile_body(tile, carry):
        at = lanes(tile)
        for axis in range(2):
            for lag in range(GRID):
                by_side = [
                    jnp.broadcast_to(table_ref[axis * LAGS + cat * GRID + lag : axis * LAGS + cat * GRID + lag + 1, at], (8, 128))
                    for cat in range(3)
                ]
                lag_ref[axis * GRID + lag, :, at] = 0.5 * jnp.where(
                    side == 10, by_side[0], jnp.where(side == 14, by_side[1], by_side[2])
                )
        for a in range(HALF):
            for b in range(a, HALF):
                near = lag_ref[b - a, :, at]
                far = lag_ref[GRID - 1 - a - b, :, at]
                rowop_ref[tri(a, b), :, at] = near + far
                rowop_ref[45 + tri(a, b), :, at] = near - far
                near = lag_ref[GRID + b - a, :, at]
                far = lag_ref[GRID + GRID - 1 - a - b, :, at]
                colop_ref[tri(a, b), :, at] = near + sign * far
        return carry

    lax.fori_loop(0, tiles, tile_body, 0)


def mirror_in(source_ref, mask_ref, out_ref):
    half = sublane_half()
    sign = jnp.where(half, 1.0, -1.0).astype(F32)
    tiles = source_ref.shape[1] // 128

    def body(i, carry):
        for tile in range(tiles):
            at = lanes(tile)

            def mirrored(row, pair):
                near = source_ref[rows8(row * HALF + pair), at] * mask_ref[rows8(row * HALF + pair), :]
                if pair == 4:
                    return swap(near) + sign * near, None
                other = row * HALF + 8 - pair
                far = source_ref[rows8(other), at] * mask_ref[rows8(other), :]
                even = jnp.where(half, near, far)
                odd = jnp.where(half, far, near)
                return swap(even) + sign * even, odd + sign * swap(odd)

            for pair in range(5):
                top = mirrored(i, pair)
                bottom = mirrored(GRID - 1 - i, pair)
                for step in range(2 if pair < 4 else 1):
                    where = i * HALF + 2 * pair + step
                    out_ref[rows8(where), at] = top[step] + bottom[step]
                    out_ref[rows8(81 + where), at] = top[step] - bottom[step]
        return carry

    lax.fori_loop(0, HALF, body, 0)


def mirror_out(source_ref, mask_ref, out_ref, extra_ref, gain_ref):
    half = sublane_half()
    sign = jnp.where(half, 1.0, -1.0).astype(F32)
    tiles = source_ref.shape[1] // 128

    def body(i, carry):
        for tile in range(tiles):
            at = lanes(tile)
            gain = jnp.broadcast_to(gain_ref[:, at], (8, 128))

            def finish(index, value):
                value = value * mask_ref[rows8(index), :] + gain * extra_ref[rows8(index), at]
                out_ref[rows8(index), at] = value.astype(BF16).astype(F32)

            for pair in range(5):
                both = []
                for step in range(2 if pair < 4 else 1):
                    where = i * HALF + 2 * pair + step
                    plus = source_ref[rows8(where), at]
                    minus = source_ref[rows8(81 + where), at]
                    top, bottom = plus + minus, plus - minus
                    both.append(
                        (swap(top) + sign * top, swap(bottom) + sign * bottom)
                        if step == 0
                        else (top - sign * swap(top), bottom - sign * swap(bottom))
                    )
                for part, row in ((0, i), (1, GRID - 1 - i)):
                    if pair == 4:
                        finish(row * HALF + 4, both[0][part])
                        continue
                    if True:
                        even, odd = both[0][part], both[1][part]
                        finish(row * HALF + pair, jnp.where(half, even, odd))
                        finish(row * HALF + 8 - pair, jnp.where(half, odd, even))
        return carry

    lax.fori_loop(0, HALF, body, 0)


def apply_rows(op_ref, source_ref, out_ref):
    tiles = source_ref.shape[1] // 128

    def body(j, carry):
        for tile in range(tiles):
            at = lanes(tile)
            for rho in range(2):
                values = [source_ref[rows8(rho * 81 + p * HALF + j), at] for p in range(HALF)]
                for i in range(HALF):
                    total = None
                    for p in range(HALF):
                        term = op_ref[rho * 45 + tri(i, p), :, at] * values[p]
                        total = term if total is None else total + term
                    out_ref[rows8(rho * 81 + i * HALF + j), at] = total
        return carry

    lax.fori_loop(0, HALF, body, 0)


def apply_cols(op_ref, source_ref, out_ref):
    tiles = source_ref.shape[1] // 128

    def body(i, carry):
        for tile in range(tiles):
            at = lanes(tile)
            values = [source_ref[rows8(i * HALF + q), at] for q in range(HALF)]
            for j in range(HALF):
                total = None
                for q in range(HALF):
                    term = op_ref[tri(j, q), :, at] * values[q]
                    total = term if total is None else total + term
                out_ref[rows8(i * HALF + j), at] = total
        return carry

    lax.fori_loop(0, 2 * HALF, body, 0)


def row_correlate(left_ref, right_ref, acc_ref, cut=3):
    for tile in range(left_ref.shape[1] // 128):
        for rho in range(2):

            def body(step, carry, at=lanes(tile), rho=rho):
                first = step * cut
                sums = [[None] * HALF for _ in range(cut)]
                for j in range(HALF):
                    left = [
                        left_ref[rows8(rho * 81 + (first + k) * HALF + j), at] for k in range(cut)
                    ]
                    for p in range(HALF):
                        right = right_ref[rows8(rho * 81 + p * HALF + j), at]
                        for k in range(cut):
                            term = left[k] * right
                            sums[k][p] = term if sums[k][p] is None else sums[k][p] + term
                for k in range(cut):
                    for p in range(HALF):
                        acc_ref[rows8(rho * 81 + (first + k) * HALF + p), at] = sums[k][p]
                return carry

            lax.fori_loop(0, HALF // cut, body, 0)


def col_correlate(left_ref, right_ref, acc_ref, cut=3):
    for tile in range(left_ref.shape[1] // 128):

        def body(step, carry, at=lanes(tile)):
            first = step * cut
            sums = [[None] * HALF for _ in range(cut)]
            for i in range(2 * HALF):
                left = [left_ref[rows8(i * HALF + first + k), at] for k in range(cut)]
                for q in range(HALF):
                    right = right_ref[rows8(i * HALF + q), at]
                    for k in range(cut):
                        term = left[k] * right
                        sums[k][q] = term if sums[k][q] is None else sums[k][q] + term
            for k in range(cut):
                for q in range(HALF):
                    acc_ref[rows8((first + k) * HALF + q), at] = sums[k][q]
            return carry

        lax.fori_loop(0, HALF // cut, body, 0)


def gather_lags(class_ref, row_acc, col_acc, dk_ref):
    side = side_vreg(class_ref)
    sign = jnp.where(sublane_half(), 1.0, -1.0).astype(F32)
    tiles = row_acc.shape[1] // 128

    def body(tile, carry):
        at = lanes(tile)
        for axis in range(2):
            near = [None] * HALF
            far = [None] * GRID
            for a in range(HALF):
                for b in range(HALF):
                    if axis == 0:
                        plus = row_acc[rows8(a * HALF + b), at]
                        minus = row_acc[rows8(81 + a * HALF + b), at]
                        direct, cross = plus + minus, plus - minus
                    else:
                        direct = col_acc[rows8(a * HALF + b), at]
                        cross = sign * direct
                    d, s = abs(a - b), GRID - 1 - a - b
                    near[d] = direct if near[d] is None else near[d] + direct
                    far[s] = cross if far[s] is None else far[s] + cross
            for lag in range(GRID):
                total = None
                for part in ([near[lag]] if lag < HALF else []) + ([far[lag]] if lag else []):
                    total = part if total is None else total + part
                total = 0.5 * total
                for cat, length in enumerate(SIDES):
                    row = axis * LAGS + cat * GRID + lag
                    value = jnp.where(side == length, total, 0.0)
                    dk_ref[row : row + 1, at] = jnp.sum(value, axis=0, keepdims=True)
        return carry

    lax.fori_loop(0, tiles, body, 0)


def stages_of(size):
    bits = size.bit_length() - 1
    stages, stride = [], 1
    while bits:
        take = bits if bits <= 3 and bits != 2 else 2
        stages.append((stride, 1 << take))
        stride <<= take
        bits -= take
    return stages


def chunk_rows(rows, size):
    return -(-rows // (16 * size)) * 16


class Ring:
    def __init__(self, group, size, rows, acc, send, recv, full, sems):
        self.group, self.size, self.rows = group, size, rows
        self.acc, self.send, self.recv, self.full = acc, send, recv, full
        self.send_sem, self.recv_sem, self.back_send, self.back_recv = sems
        self.stages = stages_of(size)
        self.me = lax.axis_index("dp")
        self.base = group * size * rows
        self.digit, self.start, self.length = [], [], []
        start, length = 0, size
        for stride, members in self.stages:
            digit = lax.rem(self.me // stride, members)
            self.digit.append(digit)
            self.start.append(start)
            self.length.append(length)
            length //= members
            start = start + digit * length
        self.mine = start

    def at(self, chunk, count):
        return pl.ds(pl.multiple_of(self.base + chunk * self.rows, 16), count * self.rows)

    def hop(self, stage, offset):
        stride, members = self.stages[stage]
        digit = self.digit[stage]
        other = lax.rem(digit + offset, members)
        length = self.length[stage] // members
        start = self.start[stage]
        return self.me + (other - digit) * stride, start + other * length, start + digit * length, length

    def slot(self, stage, offset):
        length = self.length[stage] // self.stages[stage][1]
        return self.at(self.size - self.length[stage] + (offset - 1) * length, length)

    def sem(self, sems, stage, offset):
        return sems.at[self.group, stage, offset - 1]

    def reduce_copy(self, stage, offset):
        peer, theirs, _, length = self.hop(stage, offset)
        return pltpu.make_async_remote_copy(
            src_ref=self.send.at[self.at(theirs, length), :],
            dst_ref=self.recv.at[self.slot(stage, offset), :],
            send_sem=self.sem(self.send_sem, stage, offset),
            recv_sem=self.sem(self.recv_sem, stage, offset),
            device_id={"dp": peer},
            device_id_type=pl.DeviceIdType.MESH,
        )

    def gather_copy(self, stage, offset):
        peer, _, ours, length = self.hop(stage, offset)
        return pltpu.make_async_remote_copy(
            src_ref=self.full.at[self.at(ours, length), :],
            dst_ref=self.full.at[self.at(ours, length), :],
            send_sem=self.sem(self.back_send, stage, offset),
            recv_sem=self.sem(self.back_recv, stage, offset),
            device_id={"dp": peer},
            device_id_type=pl.DeviceIdType.MESH,
        )

    def offsets(self, stage):
        return range(1, self.stages[stage][1])

    def reduce_start(self, stage):
        for offset in self.offsets(stage):
            _, theirs, _, length = self.hop(stage, offset)
            first = pl.multiple_of(self.base + theirs * self.rows, 16)
            copy_rows(self.acc, first, self.send, first, length * self.rows, lambda v: v.astype(BF16))
            self.reduce_copy(stage, offset).start()

    def reduce_finish(self, stage):
        for offset in self.offsets(stage):
            self.reduce_copy(stage, offset).wait_recv()
        _, _, ours, length = self.hop(stage, 0)
        shift = length * self.rows
        slot = self.base + (self.size - self.length[stage]) * self.rows
        add_rows(self.recv, slot, shift, self.stages[stage][1] - 1, self.acc,
                 pl.multiple_of(self.base + ours * self.rows, 16), shift)

    def gather_start(self, stage):
        for offset in self.offsets(stage):
            self.gather_copy(stage, offset).start()

    def gather_finish(self, stage):
        for offset in self.offsets(stage):
            self.gather_copy(stage, offset).wait_recv()

    def advance(self, step):
        count = len(self.stages)
        if 0 < step <= count:
            self.reduce_finish(step - 1)
        if step > count:
            self.gather_finish(2 * count - step)
        if step < count:
            self.reduce_start(step)
        if step == count:
            own = pl.multiple_of(self.base + self.mine * self.rows, 16)
            copy_rows(self.acc, own, self.full, own, self.rows, lambda v: v.astype(BF16))
        if count <= step < 2 * count:
            self.gather_start(2 * count - 1 - step)

    def close(self):
        for stage in range(len(self.stages)):
            for offset in self.offsets(stage):
                self.reduce_copy(stage, offset).wait_send()
                self.gather_copy(stage, offset).wait_send()


def row_block(length):
    return next(block for block in (128, 96, 64, 48, 32, 16) if length % block == 0)


def add_rows(source, first, shift, count, target, where, length):
    block = row_block(length)

    def body(t, carry):
        there = pl.ds(pl.multiple_of(where + t * block, 16), block)
        total = target[there, :]
        for n in range(count):
            here = pl.ds(pl.multiple_of(first + n * shift + t * block, 16), block)
            total = total + source[here, :].astype(F32)
        target[there, :] = total
        return carry

    lax.fori_loop(0, length // block, body, 0)


def copy_rows(source, first, target, where, length, change):
    block = row_block(length)

    def body(t, carry):
        here = pl.ds(pl.multiple_of(first + t * block, 16), block)
        there = pl.ds(pl.multiple_of(where + t * block, 16), block)
        target[there, :] = change(source[here, :])
        return carry

    lax.fori_loop(0, length // block, body, 0)


def images_in(ref, first, count):
    parts = [ref[micro, pl.ds(first, count), :, :].astype(F32) for micro in range(2)]
    return jnp.concatenate(parts, axis=1).reshape(4 * count, ref.shape[3])


def images_out(ref, first, count, value):
    value = value.reshape(count, 4, ref.shape[3])
    for micro in range(2):
        ref[micro, pl.ds(first, count)] = value[:, 2 * micro : 2 * micro + 2, :].astype(BF16)


def gelu_and_slope(pre):
    size = 1.0 + ERF_SHIFT * jnp.abs(pre)
    inv = pltpu.reciprocal(size, approx=True)
    inv = inv * (2.0 - size * inv)
    poly = (0.5 * ERF_POLY[-1]) * inv + 0.5 * ERF_POLY[-2]
    for value in reversed(ERF_POLY[:-2]):
        poly = poly * inv + 0.5 * value
    bell = jnp.exp2(pre * pre * (-0.5 * math.log2(math.e)))
    tail = poly * inv * bell
    cdf = jnp.where(pre >= 0.0, 1.0 - tail, tail)
    return (pre * cdf).astype(BF16), cdf + pre * bell * (1.0 / math.sqrt(2.0 * math.pi))


STEPS = (
    ((), (), (), ()),
    ((), (), (), (0,)),
    ((), (), (), ()),
    ((), (), (), (0, 1)),
    ((), (), (), ()),
    ((), (0,), (), (1, 2)),
)
LATER = ((), (), (0, 1), (), (2,), (), (1,), (2, 0), (1, 2))


def mega_kernel(
    size,
    class_ref,
    extent_ref,
    rate_ref,
    freq_ref,
    coef_ref,
    skip_ref,
    b_in_ref,
    gain_ref,
    shift_ref,
    b_out_ref,
    scale_ref,
    w_in_hbm,
    w_out_hbm,
    x_hbm,
    cot_hbm,
    block_out,
    dx_out,
    dw_in_out,
    dw_out_out,
    small_out,
    x_ref,
    cot_ref,
    w_in_ref,
    w_out_ref,
    pack_own,
    pack_oth,
    w_in_oth,
    w_out_oth,
    table_ref,
    skip_all,
    mask_ref,
    lag_ref,
    rowop_ref,
    colop_ref,
    u_ref,
    uh_ref,
    v_ref,
    mh_ref,
    mixed_ref,
    normed_ref,
    gmlp_ref,
    act_ref,
    gpre_ref,
    mlp_ref,
    gn_ref,
    stat_ref,
    gm_ref,
    row_acc,
    col_acc,
    db_ref,
    sums_ref,
    acc_ref,
    away_ref,
    landed_ref,
    send_ref,
    recv_ref,
    full_ref,
    dw_in_ref,
    dw_out_ref,
    block_ref,
    dx_ref,
    small_keep,
    small_land,
    small_recv,
    pair_send,
    pair_recv,
    red_send,
    red_recv,
    gat_send,
    gat_recv,
    sc_send,
    sc_recv,
    bc_send,
    bc_recv,
    out_sem,
    in_sem,
):
    cells, channels = x_ref.shape[1], x_ref.shape[3]
    rows = 4 * cells
    own = pack_own.shape[1]
    half_hidden = w_in_ref.shape[1]
    me = lax.axis_index("dp")
    core = lax.axis_index("mp")
    partner = {"mp": 1 - core}

    barrier = pltpu.get_barrier_semaphore()
    pl.semaphore_signal(barrier, inc=1, device_id=partner, device_id_type=pl.DeviceIdType.MESH)
    for offset in range(1, size):
        pl.semaphore_signal(
            barrier,
            inc=1,
            device_id={"dp": lax.rem(me + offset, size)},
            device_id_type=pl.DeviceIdType.MESH,
        )
    reads = [
        pltpu.make_async_copy(source, target, in_sem.at[index])
        for index, (source, target) in enumerate(
            (
                (w_in_hbm, w_in_ref.at[pl.ds(0, channels), :]),
                (w_out_hbm, w_out_ref),
                (x_hbm, x_ref),
                (cot_hbm, cot_ref),
            )
        )
    ]
    for copy in reads:
        copy.start()

    def pair_copy(index, source, target):
        return pltpu.make_async_remote_copy(
            src_ref=source,
            dst_ref=target,
            send_sem=pair_send.at[index],
            recv_sem=pair_recv.at[index],
            device_id=partner,
            device_id_type=pl.DeviceIdType.MESH,
        )

    write_tables(extent_ref, rate_ref, freq_ref, coef_ref, pack_own)
    pack_own[108:109, :] = skip_ref[...].reshape(1, own)
    pack_own[109:PACK_ROWS, :] = jnp.zeros((PACK_ROWS - 109, own), F32)
    b_in = b_in_ref[...].reshape(1, half_hidden)
    b_high = b_in.astype(BF16).astype(F32)
    b_mid = (b_in - b_high).astype(BF16).astype(F32)
    b_low = b_in - b_high - b_mid
    line = lax.broadcasted_iota(jnp.int32, (16, half_hidden), 0)
    w_in_ref[channels : channels + 16, :] = jnp.where(
        line == 0, b_high, jnp.where(line == 1, b_mid, jnp.where(line == 2, b_low, 0.0))
    ).astype(BF16)
    rest = WIDE - channels - 16
    w_in_ref[channels + 16 : WIDE, :] = jnp.zeros((rest, half_hidden), BF16)
    w_in_oth[channels + 16 : WIDE, :] = jnp.zeros((rest, half_hidden), BF16)
    pl.semaphore_wait(barrier, size)
    pack_copy = pair_copy(0, pack_own, pack_oth)
    first_copy = pair_copy(
        1, w_in_ref.at[pl.ds(0, channels + 16), :], w_in_oth.at[pl.ds(0, channels + 16), :]
    )
    second_copy = pair_copy(2, w_out_ref, w_out_oth)
    pack_copy.start()
    reads[0].wait()
    first_copy.start()
    reads[1].wait()
    second_copy.start()

    build_masks(class_ref, mask_ref)
    block = 144
    scale = scale_ref[...].reshape(1, channels)
    normed_ref[:, channels:] = jnp.where(
        lax.broadcasted_iota(jnp.int32, (rows, WIDE - channels), 1) < 3, 1.0, 0.0
    ).astype(BF16)
    mlp_ref[...] = jnp.broadcast_to(b_out_ref[...].reshape(1, channels), mlp_ref.shape)
    gn_ref[...] = jnp.zeros_like(gn_ref)
    reads[2].wait()
    reads[3].wait()

    def load(t, carry):
        at = pl.ds(pl.multiple_of(t * 48, 16), 48)
        u_ref[at, :] = images_in(x_ref, t * 12, 12)
        mask = jnp.tile(mask_ref[at, :], (1, channels // 128))
        gmlp_ref[at, :] = (images_in(cot_ref, t * 12, 12) * scale * mask).astype(BF16)
        return carry

    lax.fori_loop(0, rows // 48, load, 0)
    mirror_in(u_ref, mask_ref, uh_ref)

    pack_copy.wait_recv()
    first = core == 0
    low = jnp.where(first, pack_own[...], pack_oth[...])
    high = jnp.where(first, pack_oth[...], pack_own[...])
    table_ref[...] = jnp.concatenate([low, high], axis=1)
    skip_all[...] = table_ref[108:109, :]
    build_operators(class_ref, table_ref, lag_ref, rowop_ref, colop_ref)
    apply_rows(rowop_ref, uh_ref, v_ref)
    apply_cols(colop_ref, v_ref, mh_ref)
    mirror_out(mh_ref, mask_ref, mixed_ref, u_ref, skip_all)

    gain = gain_ref[...].reshape(1, channels)
    shift = shift_ref[...].reshape(1, channels)

    def norm(t, carry):
        at = pl.ds(pl.multiple_of(t * block, block), block)
        value = mixed_ref[at, :]
        mean = jnp.mean(value, axis=1, keepdims=True)
        centered = value - mean
        variance = jnp.mean(centered * centered, axis=1, keepdims=True)
        rstd = lax.rsqrt(variance + 1e-06)
        hat = centered * rstd
        mixed_ref[at, :] = hat
        stat_ref[at, :] = jnp.broadcast_to(rstd, (block, 128))
        normed_ref[at, :channels] = (hat * gain + shift).astype(BF16)
        return carry

    lax.fori_loop(0, rows // block, norm, 0)

    chunk = CHUNK
    tile_rows = 432
    first_copy.wait_recv()
    second_copy.wait_recv()

    group_rows = 2 * channels * chunk // 128
    per_chunk = chunk_rows(group_rows, size)
    stride = per_chunk * size
    groups = half_hidden // chunk
    rings = [
        Ring(group, size, per_chunk, acc_ref, send_ref, recv_ref, full_ref,
             (red_send, red_recv, gat_send, gat_recv))
        for group in range(groups)
    ]
    done = [0] * groups

    def advance(*which):
        last = 2 * len(stages_of(size))
        for group in which:
            if done[group] > last:
                continue
            rings[group].advance(done[group])
            if done[group] == last:
                unpack(group)
            done[group] += 1

    def unpack(group):
        base = group * stride
        for k in range(chunk // 128):
            at = group * chunk + k * 128
            dw_in_ref[:, at : at + 128] = full_ref[base : base + channels, :].astype(F32)
            base += channels
        for k in range(channels // 128):
            dw_out_ref[group * chunk : (group + 1) * chunk, k * 128 : (k + 1) * 128] = full_ref[
                base : base + chunk, :
            ].astype(F32)
            base += chunk
        at = pl.ds(group * chunk, chunk)
        first = pltpu.make_async_copy(dw_in_ref.at[:, at], dw_in_out.at[:, at], out_sem.at[2 * group])
        second = pltpu.make_async_copy(dw_out_ref.at[at, :], dw_out_out.at[at, :], out_sem.at[2 * group + 1])
        first.start()
        second.start()
        writes.extend((first, second))

    writes = []
    tiles = rows // tile_rows

    def feed(f, w_first_ref, w_second_ref, target_ref, target_base, db_row, steps):
        cols = pl.ds(f * chunk, chunk)

        def ahead(t):
            at = pl.ds(t * tile_rows, tile_rows)
            pre = jnp.dot(normed_ref[at, :], w_first_ref[:, cols], preferred_element_type=F32)
            g_act = lax.dot_general(
                gmlp_ref[at, :],
                w_second_ref[cols, :],
                (((1,), (1,)), ((), ())),
                preferred_element_type=F32,
            )
            return pre, g_act

        waiting = ahead(0)
        for t in range(tiles):
            pre, g_act = waiting
            if t + 1 < tiles:
                waiting = ahead(t + 1)
            at = pl.ds(t * tile_rows, tile_rows)
            act, slope = gelu_and_slope(pre)
            g_pre = (g_act * slope).astype(BF16)
            act_ref[at, :] = act
            gpre_ref[at, :] = g_pre
            mlp_ref[at, :] += jnp.dot(act, w_second_ref[cols, :], preferred_element_type=F32)
            gn_ref[at, :] += lax.dot_general(
                g_pre,
                w_first_ref[:channels, cols],
                (((1,), (1,)), ((), ())),
                preferred_element_type=F32,
            )
            advance(*steps[t])
        d_first = lax.dot_general(
            normed_ref[...], gpre_ref[...], (((0,), (0,)), ((), ())), preferred_element_type=F32
        )
        for k in range(chunk // 128):
            at = pl.ds(target_base + k * channels, channels)
            target_ref[at, :] = d_first[:channels, k * 128 : (k + 1) * 128].astype(target_ref.dtype)
        db_ref[db_row : db_row + 1, cols] = d_first[channels : channels + 1, :]
        d_second = lax.dot_general(
            act_ref[...], gmlp_ref[...], (((0,), (0,)), ((), ())), preferred_element_type=F32
        )
        base = target_base + channels * (chunk // 128)
        for k in range(channels // 128):
            at = pl.ds(base + k * chunk, chunk)
            target_ref[at, :] = d_second[:, k * 128 : (k + 1) * 128].astype(target_ref.dtype)

    def grads_copy(group):
        at = pl.ds(group * group_rows, group_rows)
        return pair_copy(4 + group, away_ref.at[at, :], landed_ref.at[at, :])

    for group in range(groups):
        feed(group, w_in_oth, w_out_oth, away_ref, group * group_rows, 1, STEPS[2 * group])
        grads_copy(group).start()
        advance(*STEPS[2 * group][3])
        feed(group, w_in_ref, w_out_ref, acc_ref, group * stride, 0, STEPS[2 * group + 1])
        grads_copy(group).wait_recv()
        add_rows(landed_ref, group * group_rows, 0, 1, acc_ref, group * stride, group_rows)
        if stride > group_rows:
            acc_ref[group * stride + group_rows : (group + 1) * stride, :] = jnp.zeros(
                (stride - group_rows, 128), F32
            )
        advance(*STEPS[2 * group + 1][3])

    def back(t, carry):
        d_gain, d_bias, d_scale, d_b_out = carry
        at = pl.ds(pl.multiple_of(t * 48, 16), 48)
        mask = jnp.tile(mask_ref[at, :], (1, channels // 128))
        branch = mlp_ref[at, :] * mask
        d_scale = d_scale + jnp.sum(images_in(cot_ref, t * 12, 12) * branch, axis=0, keepdims=True)
        d_b_out = d_b_out + jnp.sum(gmlp_ref[at, :].astype(F32), axis=0, keepdims=True)
        grad = gn_ref[at, :]
        hat = mixed_ref[at, :]
        d_gain = d_gain + jnp.sum(grad * hat, axis=0, keepdims=True)
        d_bias = d_bias + jnp.sum(grad, axis=0, keepdims=True)
        grad = grad * gain
        mean_g = jnp.mean(grad, axis=1, keepdims=True)
        mean_gh = jnp.mean(grad * hat, axis=1, keepdims=True)
        rstd = jnp.tile(stat_ref[at, :], (1, channels // 128))
        gm_ref[at, :] = (rstd * (grad - mean_g - hat * mean_gh)).astype(BF16).astype(F32)
        return d_gain, d_bias, d_scale, d_b_out

    zero = jnp.zeros((1, channels), F32)
    sums = lax.fori_loop(0, rows // 48, back, (zero, zero, zero, zero))
    mine_only = pl.ds(pl.multiple_of(core * 256, 128), 128)
    theirs_only = pl.ds(pl.multiple_of((1 - core) * 256, 128), 128)
    for index, value in enumerate(sums):
        for k in range(channels // 128):
            row = 115 + index * (channels // 128) + k
            tile = value[:, k * 128 : (k + 1) * 128]
            sums_ref[row : row + 1, mine_only] = tile
            sums_ref[row : row + 1, theirs_only] = tile
    for k in range(half_hidden // 128):
        at = slice(k * 128, (k + 1) * 128)
        sums_ref[109 + k : 110 + k, mine_only] = db_ref[0:1, at]
        sums_ref[109 + k : 110 + k, theirs_only] = db_ref[1:2, at]
    sums_ref[109:127, 128:256] = jnp.zeros((18, 128), F32)
    sums_ref[127:128, :] = zero
    advance(*LATER[0])
    gh_ref, xh_ref = mh_ref, row_acc
    mirror_in(gm_ref, mask_ref, gh_ref)
    col_correlate(gh_ref, v_ref, col_acc)
    advance(*LATER[1])
    apply_cols(colop_ref, gh_ref, xh_ref)
    advance(*LATER[2])
    row_correlate(xh_ref, uh_ref, v_ref)
    advance(*LATER[3])
    gather_lags(class_ref, v_ref, col_acc, sums_ref)

    def skip_sum(t, total):
        at = pl.ds(pl.multiple_of(t * block, block), block)
        return total + jnp.sum(gm_ref[at, :] * u_ref[at, :], axis=0, keepdims=True)

    sums_ref[108:109, :] = lax.fori_loop(0, rows // block, skip_sum, zero)
    mine_slice = pl.ds(pl.multiple_of(core * 128, 128), 256)
    theirs_slice = pl.ds(pl.multiple_of((1 - core) * 128, 128), 256)
    small_pair = pair_copy(3, sums_ref.at[:, theirs_slice], small_land)
    small_pair.start()
    apply_rows(rowop_ref, xh_ref, gh_ref)
    advance(*LATER[4])
    small_pair.wait_recv()
    small_keep[0:SUM_ROWS, :] = sums_ref[:, mine_slice] + small_land[...]
    if small_keep.shape[0] > SUM_ROWS:
        small_keep[SUM_ROWS:, :] = jnp.zeros((small_keep.shape[0] - SUM_ROWS, 256), F32)

    per = small_keep.shape[0] // size
    mine = pl.ds(pl.multiple_of(me * per, 8), per)

    def scatter_copy(offset):
        target = lax.rem(me + offset, size)
        return pltpu.make_async_remote_copy(
            src_ref=small_keep.at[pl.ds(pl.multiple_of(target * per, 8), per), :],
            dst_ref=small_recv.at[offset - 1],
            send_sem=sc_send.at[offset - 1],
            recv_sem=sc_recv.at[offset - 1],
            device_id={"dp": target},
            device_id_type=pl.DeviceIdType.MESH,
        )

    def spread_copy(offset):
        target = lax.rem(me + offset, size)
        return pltpu.make_async_remote_copy(
            src_ref=small_out.at[mine, :],
            dst_ref=small_out.at[mine, :],
            send_sem=bc_send.at[offset - 1],
            recv_sem=bc_recv.at[offset - 1],
            device_id={"dp": target},
            device_id_type=pl.DeviceIdType.MESH,
        )

    for offset in range(1, size):
        scatter_copy(offset).start()
    mirror_out(gh_ref, mask_ref, gn_ref, gm_ref, skip_all)
    advance(*LATER[5])

    def finish(t, carry):
        at = pl.ds(pl.multiple_of(t * 48, 16), 48)
        images_out(dx_ref, t * 12, 12, images_in(cot_ref, t * 12, 12) + gn_ref[at, :])
        branch = mlp_ref[at, :] * jnp.tile(mask_ref[at, :], (1, channels // 128))
        images_out(block_ref, t * 12, 12, u_ref[at, :] + scale * branch)
        return carry

    lax.fori_loop(0, rows // 48, finish, 0)
    for index, (source, target) in enumerate(((dx_ref, dx_out), (block_ref, block_out))):
        copy = pltpu.make_async_copy(source, target, out_sem.at[2 * groups + index])
        copy.start()
        writes.append(copy)
    advance(*LATER[6])
    total = small_keep[mine, :]
    for offset in range(1, size):
        scatter_copy(offset).wait_recv()
        total = total + small_recv[offset - 1]
    small_out[mine, :] = total
    for offset in range(1, size):
        spread_copy(offset).start()

    advance(*LATER[7])
    for _ in range(2 * len(stages_of(size)) + 1):
        advance(*range(groups))
    for offset in range(1, size):
        spread_copy(offset).wait_recv()
    for offset in range(1, size):
        scatter_copy(offset).wait_send()
        spread_copy(offset).wait_send()
    for group in range(groups):
        rings[group].close()
        grads_copy(group).wait_send()
    for copy in (pack_copy, first_copy, second_copy, small_pair):
        copy.wait_send()
    for copy in writes:
        copy.wait()


def final_kernel(
    extent_ref, rate_ref, freq_ref, coef_ref, small_ref, block_ref, dx_ref, dw_in_ref, dw_out_ref,
    block_out, dx_out, rate_out, freq_out, coef_out, skip_out, gain_out, bias_out, dw_in_out,
    db_in_out, dw_out_out, b_out_out, scale_out,
    mine_ref, block_hold, dx_hold, dw_in_hold, dw_out_hold, sems,
):
    held = (block_ref, dx_ref, dw_in_ref, dw_out_ref)
    stage = (block_hold, dx_hold, dw_in_hold, dw_out_hold)
    outs = (block_out, dx_out, dw_in_out, dw_out_out)
    into = [pltpu.make_async_copy(held[k], stage[k], sems.at[k]) for k in range(4)]
    away = [pltpu.make_async_copy(stage[k], outs[k], sems.at[4 + k]) for k in range(4)]
    for copy in into:
        copy.start()
    core = lax.axis_index("mp")
    own = mine_ref.shape[1]
    mine_ref[...] = jnp.where(core == 0, small_ref[0:112, :own], small_ref[0:112, 256 - own :])
    only = pl.ds(pl.multiple_of(core * 128, 128), 128)

    def line(first, count):
        return jnp.concatenate([small_ref[first + k : first + k + 1, only] for k in range(count)], axis=1)

    args = (extent_ref, rate_ref, freq_ref, coef_ref, mine_ref, rate_out, freq_out, coef_out)
    modes_grad(0, *args)
    for k in range(4):
        into[k].wait()
        away[k].start()
    modes_grad(1, *args)
    skip_out[...] = mine_ref[108:109, :].reshape(skip_out.shape)
    db_in_out[...] = line(109, db_in_out.shape[0] // 128).reshape(db_in_out.shape)
    for k, ref in enumerate((gain_out, bias_out, scale_out, b_out_out)):
        ref[...] = line(115 + 3 * k, 3).reshape(ref.shape)
    for copy in away:
        copy.wait()


ANY = pl.BlockSpec(memory_space=pl.ANY)
VM = pl.BlockSpec(memory_space=pltpu.VMEM)
SM = pl.BlockSpec(memory_space=pltpu.SMEM)


def shape(dims, kind=F32):
    return jax.ShapeDtypeStruct(dims, kind)


def on_device(
    size,
    pixels,
    grid_class,
    extent,
    ssm_rate,
    ssm_freq,
    ssm_coef,
    skip_gain,
    norm_gain,
    norm_bias,
    w_in,
    b_in,
    w_out,
    b_out,
    layer_scale,
    cotangent,
):
    micro, count, channels, cells = pixels.shape
    rows = micro * count * cells
    own = ssm_rate.shape[1]
    modes = ssm_rate.shape[2]
    half_hidden = b_in.shape[0]
    x = pixels.transpose(0, 3, 1, 2)
    cot = cotangent.transpose(0, 3, 1, 2)
    rate = ssm_rate.transpose(0, 2, 1)
    freq = ssm_freq.transpose(0, 2, 1)
    coef = ssm_coef.transpose(0, 2, 1)
    field = (rows, channels)
    grad_rows = 2 * channels * half_hidden // 128
    groups = half_hidden // CHUNK
    all_rows = groups * chunk_rows(grad_rows // groups, size) * size
    stages = stages_of(size)
    hops = (groups, max(len(stages), 1), max([members - 1 for _, members in stages] + [1]))
    small_rows = max(128, 8 * size)
    peers = max(size - 1, 1)
    DMA = pltpu.SemaphoreType.DMA
    block_out, dx, dw_in, dw_out, small = pl.pallas_call(
        partial(mega_kernel, size),
        out_shape=(
            shape(x.shape, BF16),
            shape(x.shape, BF16),
            shape(w_in.shape),
            shape(w_out.shape),
            shape((small_rows, 256)),
        ),
        in_specs=[SM] + [VM] * 10 + [ANY] * 4,
        out_specs=(ANY,) * 4 + (VM,),
        scratch_shapes=[
            pltpu.VMEM(x.shape, BF16),
            pltpu.VMEM(x.shape, BF16),
            pltpu.VMEM((WIDE, half_hidden), BF16),
            pltpu.VMEM(w_out.shape, BF16),
            pltpu.VMEM((PACK_ROWS, own), F32),
            pltpu.VMEM((PACK_ROWS, own), F32),
            pltpu.VMEM((WIDE, half_hidden), BF16),
            pltpu.VMEM(w_out.shape, BF16),
            pltpu.VMEM((PACK_ROWS, channels), F32),
            pltpu.VMEM((1, channels), F32),
            pltpu.VMEM((rows, 128), F32),
            pltpu.VMEM((2 * GRID, 8, channels), F32),
            pltpu.VMEM((90, 8, channels), F32),
            pltpu.VMEM((45, 8, channels), F32),
            pltpu.VMEM(field, F32),
            pltpu.VMEM(field, F32),
            pltpu.VMEM(field, F32),
            pltpu.VMEM(field, F32),
            pltpu.VMEM(field, F32),
            pltpu.VMEM((rows, WIDE), BF16),
            pltpu.VMEM(field, BF16),
            pltpu.VMEM((rows, 256), BF16),
            pltpu.VMEM((rows, 256), BF16),
            pltpu.VMEM(field, F32),
            pltpu.VMEM(field, F32),
            pltpu.VMEM((rows, 128), F32),
            pltpu.VMEM(field, F32),
            pltpu.VMEM((162 * 8, channels), F32),
            pltpu.VMEM((81 * 8, channels), F32),
            pltpu.VMEM((2, half_hidden), F32),
            pltpu.VMEM((SUM_ROWS, channels), F32),
            pltpu.VMEM((all_rows, 128), F32),
            pltpu.VMEM((grad_rows, 128), BF16),
            pltpu.VMEM((grad_rows, 128), BF16),
            pltpu.VMEM((all_rows, 128), BF16),
            pltpu.VMEM((all_rows, 128), BF16),
            pltpu.VMEM((all_rows, 128), BF16),
            pltpu.VMEM(w_in.shape, F32),
            pltpu.VMEM(w_out.shape, F32),
            pltpu.VMEM(x.shape, BF16),
            pltpu.VMEM(x.shape, BF16),
            pltpu.VMEM((small_rows, 256), F32),
            pltpu.VMEM((SUM_ROWS, 256), F32),
            pltpu.VMEM((peers, small_rows // size, 256), F32),
            DMA((4 + groups,)),
            DMA((4 + groups,)),
            DMA(hops),
            DMA(hops),
            DMA(hops),
            DMA(hops),
            DMA((peers,)),
            DMA((peers,)),
            DMA((peers,)),
            DMA((peers,)),
            DMA((2 * groups + 2,)),
            DMA((4,)),
        ],
        compiler_params=pltpu.CompilerParams(
            vmem_limit_bytes=VMEM_LIMIT, collective_id=0, has_side_effects=True
        ),
        name="block",
    )(
        grid_class,
        extent,
        rate,
        freq,
        coef,
        skip_gain,
        b_in,
        norm_gain,
        norm_bias,
        b_out,
        layer_scale,
        w_in,
        w_out,
        x,
        cot,
    )
    (
        block_out, dx, g_rate, g_freq, g_coef, g_skip, g_gain, g_bias, dw_in, db_in, dw_out, g_b_out, g_scale,
    ) = pl.pallas_call(
        final_kernel,
        out_shape=(
            shape(x.shape, BF16),
            shape(x.shape, BF16),
            shape((2, modes, own)),
            shape((2, modes, own)),
            shape((2, modes, own)),
            shape((own,)),
            shape((channels,)),
            shape((channels,)),
            shape(w_in.shape),
            shape((half_hidden,)),
            shape(w_out.shape),
            shape((channels,)),
            shape((channels,)),
        ),
        in_specs=[VM] * 5 + [ANY] * 4,
        out_specs=(ANY, ANY) + (VM,) * 6 + (ANY, VM, ANY, VM, VM),
        scratch_shapes=[
            pltpu.VMEM((112, own), F32),
            pltpu.VMEM(x.shape, BF16),
            pltpu.VMEM(x.shape, BF16),
            pltpu.VMEM(w_in.shape, F32),
            pltpu.VMEM(w_out.shape, F32),
            DMA((8,)),
        ],
        compiler_params=pltpu.CompilerParams(vmem_limit_bytes=VMEM_LIMIT),
        name="final",
    )(extent, rate, freq, coef, small, block_out, dx, dw_in, dw_out)
    return (
        block_out.transpose(0, 2, 3, 1),
        dx.transpose(0, 2, 3, 1),
        g_rate.transpose(0, 2, 1),
        g_freq.transpose(0, 2, 1),
        g_coef.transpose(0, 2, 1),
        g_skip,
        g_gain,
        g_bias,
        dw_in,
        db_in,
        dw_out,
        g_b_out,
        g_scale,
    )


def solution(mesh):
    placed = (
        P(None, ("dp", "mp"), None, None),
        P(None, "dp"),
        P("mp"),
        P(None, "mp", None),
        P(None, "mp", None),
        P(None, "mp", None),
        P("mp"),
        P(),
        P(),
        P(None, "mp"),
        P("mp"),
        P("mp", None),
        P(),
        P(),
        P(None, ("dp", "mp"), None, None),
    )
    return jax.shard_map(
        partial(on_device, mesh.shape["dp"]),
        mesh=mesh,
        in_specs=placed,
        out_specs=(
            P(None, ("dp", "mp"), None, None),
            P(None, ("dp", "mp"), None, None),
            P(None, "mp", None),
            P(None, "mp", None),
            P(None, "mp", None),
            P("mp"),
            P(),
            P(),
            P(None, "mp"),
            P("mp"),
            P("mp", None),
            P(),
            P(),
        ),
        check_vma=False,
    )
```

```python
import math
from functools import partial

import jax
import jax.numpy as jnp
import numpy as np
from jax import lax
from jax.experimental import pallas as pl
from jax.experimental.pallas import tpu as pltpu
from jax.sharding import PartitionSpec as P

GRID = 18
HALF = 9
SIDES = (10, 14, 18)
LAGS = 3 * GRID
F32 = jnp.float32
BF16 = jnp.bfloat16

ERF_SHIFT = 0.35 / math.sqrt(2.0)
ERF_POLY = (
    0.19396706,
    0.23864529,
    -0.01708609,
    0.69839275,
    -0.6929918,
    0.77818103,
    -0.19910822,
)
CHUNK = 256
VMEM_LIMIT = 60 * 1024 * 1024


def small_sincos(angle):
    sq = angle * angle
    cos = 1.0 + sq * (
        -1 / 2 + sq * (1 / 24 + sq * (-1 / 720 + sq * (1 / 40320 + sq * (-1 / 3628800))))
    )
    sin = angle * (
        1.0
        + sq * (-1 / 6 + sq * (1 / 120 + sq * (-1 / 5040 + sq * (1 / 362880 + sq * (-1 / 39916800)))))
    )
    return sin, cos


def mode_step(rate, freq, side):
    decay = jnp.exp(rate * (-1.0 / side))
    sin, cos = small_sincos(freq * (1.0 / side))
    return decay * cos, decay * sin


PACK_ROWS = 112
SUM_ROWS = 128
WIDE = 512


def write_tables(extent_ref, rate_ref, freq_ref, coef_ref, out_ref):
    extent = extent_ref[...].reshape(1, extent_ref.shape[0])
    for axis in range(2):
        for cat, side in enumerate(SIDES):
            z_re, z_im = mode_step(rate_ref[axis], freq_ref[axis], side)
            w_re = coef_ref[axis]
            w_im = jnp.zeros_like(w_re)
            for lag in range(GRID):
                row = axis * LAGS + cat * GRID + lag
                if lag >= side:
                    out_ref[row : row + 1, :] = jnp.zeros((1, w_re.shape[1]), F32)
                    continue
                total = jnp.sum(w_re, axis=0, keepdims=True)
                out_ref[row : row + 1, :] = jnp.where(extent > lag, total, 0.0)
                if lag < side - 1:
                    w_re, w_im = w_re * z_re - w_im * z_im, w_re * z_im + w_im * z_re


def modes_grad(axis, extent_ref, rate_ref, freq_ref, coef_ref, dk_ref, rate_out, freq_out, coef_out):
    extent = extent_ref[...].reshape(1, extent_ref.shape[0])
    if True:
        coef = coef_ref[axis]
        g_rate = jnp.zeros_like(coef)
        g_freq = jnp.zeros_like(coef)
        g_coef = jnp.zeros_like(coef)
        for cat, side in enumerate(SIDES):
            z_re, z_im = mode_step(rate_ref[axis], freq_ref[axis], side)
            p_re = jnp.zeros_like(coef)
            p_im = jnp.zeros_like(coef)
            q_re = jnp.zeros_like(coef)
            q_im = jnp.zeros_like(coef)
            for lag in reversed(range(side)):
                row = axis * LAGS + cat * GRID + lag
                d = jnp.where(extent > lag, dk_ref[row : row + 1, :], 0.0)
                p_re, p_im = p_re * z_re - p_im * z_im + d, p_re * z_im + p_im * z_re
                q_re, q_im = q_re * z_re - q_im * z_im + float(lag) * d, q_re * z_im + q_im * z_re
            g_coef = g_coef + p_re
            g_rate = g_rate - (1.0 / side) * q_re
            g_freq = g_freq - (1.0 / side) * q_im
        coef_out[axis] = g_coef
        rate_out[axis] = g_rate * coef
        freq_out[axis] = g_freq * coef

def tri(a, b):
    low, high = min(a, b), max(a, b)
    return low * HALF - low * (low - 1) // 2 + (high - low)


def rows8(index):
    if isinstance(index, int):
        return pl.ds(index * 8, 8)
    return pl.ds(pl.multiple_of(index * 8, 8), 8)


def lanes(tile):
    if isinstance(tile, int):
        return pl.ds(tile * 128, 128)
    return pl.ds(pl.multiple_of(tile * 128, 128), 128)


def swap(value):
    return pltpu.roll(value, 4, 0)


def sublane_half():
    return lax.broadcasted_iota(jnp.int32, (8, 128), 0) < 4


def side_vreg(class_ref):
    mine = lax.axis_index("mp")
    image = lax.rem(lax.broadcasted_iota(jnp.int32, (8, 128), 0), 4)
    cls = jnp.zeros((8, 128), jnp.int32)
    own = class_ref.shape[1] // 2
    for micro in range(2):
        for img in range(2):
            cls = jnp.where(image == micro * 2 + img, class_ref[micro, mine * own + img], cls)
    return 10 + 4 * cls


def build_masks(class_ref, mask_ref):
    side = side_vreg(class_ref)
    offset = jnp.where(sublane_half(), 0, 1)

    def row(i, carry):
        for pair in range(HALF):
            ok = (i < side) & (2 * pair + offset < side)
            mask_ref[rows8(i * HALF + pair), :] = jnp.where(ok, 1.0, 0.0).astype(F32)
        return carry

    lax.fori_loop(0, GRID, row, 0)


def build_operators(class_ref, table_ref, lag_ref, rowop_ref, colop_ref):
    side = side_vreg(class_ref)
    sign = jnp.where(sublane_half(), 1.0, -1.0).astype(F32)
    tiles = table_ref.shape[1] // 128

    def tile_body(tile, carry):
        at = lanes(tile)
        for axis in range(2):
            for lag in range(GRID):
                by_side = [
                    jnp.broadcast_to(table_ref[axis * LAGS + cat * GRID + lag : axis * LAGS + cat * GRID + lag + 1, at], (8, 128))
                    for cat in range(3)
                ]
                lag_ref[axis * GRID + lag, :, at] = 0.5 * jnp.where(
                    side == 10, by_side[0], jnp.where(side == 14, by_side[1], by_side[2])
                )
        for a in range(HALF):
            for b in range(a, HALF):
                near = lag_ref[b - a, :, at]
                far = lag_ref[GRID - 1 - a - b, :, at]
                rowop_ref[tri(a, b), :, at] = near + far
                rowop_ref[45 + tri(a, b), :, at] = near - far
                near = lag_ref[GRID + b - a, :, at]
                far = lag_ref[GRID + GRID - 1 - a - b, :, at]
                colop_ref[tri(a, b), :, at] = near + sign * far
        return carry

    lax.fori_loop(0, tiles, tile_body, 0)


def mirror_in(source_ref, mask_ref, out_ref):
    half = sublane_half()
    sign = jnp.where(half, 1.0, -1.0).astype(F32)
    tiles = source_ref.shape[1] // 128

    def body(i, carry):
        for tile in range(tiles):
            at = lanes(tile)

            def mirrored(row, pair):
                near = source_ref[rows8(row * HALF + pair), at] * mask_ref[rows8(row * HALF + pair), :]
                if pair == 4:
                    return swap(near) + sign * near, None
                other = row * HALF + 8 - pair
                far = source_ref[rows8(other), at] * mask_ref[rows8(other), :]
                even = jnp.where(half, near, far)
                odd = jnp.where(half, far, near)
                return swap(even) + sign * even, odd + sign * swap(odd)

            for pair in range(5):
                top = mirrored(i, pair)
                bottom = mirrored(GRID - 1 - i, pair)
                for step in range(2 if pair < 4 else 1):
                    where = i * HALF + 2 * pair + step
                    out_ref[rows8(where), at] = top[step] + bottom[step]
                    out_ref[rows8(81 + where), at] = top[step] - bottom[step]
        return carry

    lax.fori_loop(0, HALF, body, 0)


def mirror_out(source_ref, mask_ref, out_ref, extra_ref, gain_ref):
    half = sublane_half()
    sign = jnp.where(half, 1.0, -1.0).astype(F32)
    tiles = source_ref.shape[1] // 128

    def body(i, carry):
        for tile in range(tiles):
            at = lanes(tile)
            gain = jnp.broadcast_to(gain_ref[:, at], (8, 128))

            def finish(index, value):
                value = value * mask_ref[rows8(index), :] + gain * extra_ref[rows8(index), at]
                out_ref[rows8(index), at] = value.astype(BF16).astype(F32)

            for pair in range(5):
                both = []
                for step in range(2 if pair < 4 else 1):
                    where = i * HALF + 2 * pair + step
                    plus = source_ref[rows8(where), at]
                    minus = source_ref[rows8(81 + where), at]
                    top, bottom = plus + minus, plus - minus
                    both.append(
                        (swap(top) + sign * top, swap(bottom) + sign * bottom)
                        if step == 0
                        else (top - sign * swap(top), bottom - sign * swap(bottom))
                    )
                for part, row in ((0, i), (1, GRID - 1 - i)):
                    if pair == 4:
                        finish(row * HALF + 4, both[0][part])
                        continue
                    if True:
                        even, odd = both[0][part], both[1][part]
                        finish(row * HALF + pair, jnp.where(half, even, odd))
                        finish(row * HALF + 8 - pair, jnp.where(half, odd, even))
        return carry

    lax.fori_loop(0, HALF, body, 0)


def apply_rows(op_ref, source_ref, out_ref):
    tiles = source_ref.shape[1] // 128

    def body(j, carry):
        for tile in range(tiles):
            at = lanes(tile)
            for rho in range(2):
                values = [source_ref[rows8(rho * 81 + p * HALF + j), at] for p in range(HALF)]
                for i in range(HALF):
                    total = None
                    for p in range(HALF):
                        term = op_ref[rho * 45 + tri(i, p), :, at] * values[p]
                        total = term if total is None else total + term
                    out_ref[rows8(rho * 81 + i * HALF + j), at] = total
        return carry

    lax.fori_loop(0, HALF, body, 0)


def apply_cols(op_ref, source_ref, out_ref):
    tiles = source_ref.shape[1] // 128

    def body(i, carry):
        for tile in range(tiles):
            at = lanes(tile)
            values = [source_ref[rows8(i * HALF + q), at] for q in range(HALF)]
            for j in range(HALF):
                total = None
                for q in range(HALF):
                    term = op_ref[tri(j, q), :, at] * values[q]
                    total = term if total is None else total + term
                out_ref[rows8(i * HALF + j), at] = total
        return carry

    lax.fori_loop(0, 2 * HALF, body, 0)


def row_correlate(left_ref, right_ref, acc_ref, cut=3):
    for tile in range(left_ref.shape[1] // 128):
        for rho in range(2):

            def body(step, carry, at=lanes(tile), rho=rho):
                first = step * cut
                sums = [[None] * HALF for _ in range(cut)]
                for j in range(HALF):
                    left = [
                        left_ref[rows8(rho * 81 + (first + k) * HALF + j), at] for k in range(cut)
                    ]
                    for p in range(HALF):
                        right = right_ref[rows8(rho * 81 + p * HALF + j), at]
                        for k in range(cut):
                            term = left[k] * right
                            sums[k][p] = term if sums[k][p] is None else sums[k][p] + term
                for k in range(cut):
                    for p in range(HALF):
                        acc_ref[rows8(rho * 81 + (first + k) * HALF + p), at] = sums[k][p]
                return carry

            lax.fori_loop(0, HALF // cut, body, 0)


def col_correlate(left_ref, right_ref, acc_ref, cut=3):
    for tile in range(left_ref.shape[1] // 128):

        def body(step, carry, at=lanes(tile)):
            first = step * cut
            sums = [[None] * HALF for _ in range(cut)]
            for i in range(2 * HALF):
                left = [left_ref[rows8(i * HALF + first + k), at] for k in range(cut)]
                for q in range(HALF):
                    right = right_ref[rows8(i * HALF + q), at]
                    for k in range(cut):
                        term = left[k] * right
                        sums[k][q] = term if sums[k][q] is None else sums[k][q] + term
            for k in range(cut):
                for q in range(HALF):
                    acc_ref[rows8((first + k) * HALF + q), at] = sums[k][q]
            return carry

        lax.fori_loop(0, HALF // cut, body, 0)


def gather_lags(class_ref, row_acc, col_acc, dk_ref):
    side = side_vreg(class_ref)
    sign = jnp.where(sublane_half(), 1.0, -1.0).astype(F32)
    tiles = row_acc.shape[1] // 128

    def body(tile, carry):
        at = lanes(tile)
        for axis in range(2):
            near = [None] * HALF
            far = [None] * GRID
            for a in range(HALF):
                for b in range(HALF):
                    if axis == 0:
                        plus = row_acc[rows8(a * HALF + b), at]
                        minus = row_acc[rows8(81 + a * HALF + b), at]
                        direct, cross = plus + minus, plus - minus
                    else:
                        direct = col_acc[rows8(a * HALF + b), at]
                        cross = sign * direct
                    d, s = abs(a - b), GRID - 1 - a - b
                    near[d] = direct if near[d] is None else near[d] + direct
                    far[s] = cross if far[s] is None else far[s] + cross
            for lag in range(GRID):
                total = None
                for part in ([near[lag]] if lag < HALF else []) + ([far[lag]] if lag else []):
                    total = part if total is None else total + part
                total = 0.5 * total
                for cat, length in enumerate(SIDES):
                    row = axis * LAGS + cat * GRID + lag
                    value = jnp.where(side == length, total, 0.0)
                    dk_ref[row : row + 1, at] = jnp.sum(value, axis=0, keepdims=True)
        return carry

    lax.fori_loop(0, tiles, body, 0)


def stages_of(size):
    bits = size.bit_length() - 1
    stages, stride = [], 1
    while bits:
        take = bits if bits <= 3 and bits != 2 else 2
        stages.append((stride, 1 << take))
        stride <<= take
        bits -= take
    return stages


def chunk_rows(rows, size):
    return -(-rows // (16 * size)) * 16


class Ring:
    def __init__(self, group, size, rows, acc, send, recv, full, sems):
        self.group, self.size, self.rows = group, size, rows
        self.acc, self.send, self.recv, self.full = acc, send, recv, full
        self.send_sem, self.recv_sem, self.back_send, self.back_recv = sems
        self.stages = stages_of(size)
        self.me = lax.axis_index("dp")
        self.base = group * size * rows
        self.digit, self.start, self.length = [], [], []
        start, length = 0, size
        for stride, members in self.stages:
            digit = lax.rem(self.me // stride, members)
            self.digit.append(digit)
            self.start.append(start)
            self.length.append(length)
            length //= members
            start = start + digit * length
        self.mine = start

    def at(self, chunk, count):
        return pl.ds(pl.multiple_of(self.base + chunk * self.rows, 16), count * self.rows)

    def hop(self, stage, offset):
        stride, members = self.stages[stage]
        digit = self.digit[stage]
        other = lax.rem(digit + offset, members)
        length = self.length[stage] // members
        start = self.start[stage]
        return self.me + (other - digit) * stride, start + other * length, start + digit * length, length

    def slot(self, stage, offset):
        length = self.length[stage] // self.stages[stage][1]
        return self.at(self.size - self.length[stage] + (offset - 1) * length, length)

    def sem(self, sems, stage, offset):
        return sems.at[self.group, stage, offset - 1]

    def reduce_copy(self, stage, offset):
        peer, theirs, _, length = self.hop(stage, offset)
        return pltpu.make_async_remote_copy(
            src_ref=self.send.at[self.at(theirs, length), :],
            dst_ref=self.recv.at[self.slot(stage, offset), :],
            send_sem=self.sem(self.send_sem, stage, offset),
            recv_sem=self.sem(self.recv_sem, stage, offset),
            device_id={"dp": peer},
            device_id_type=pl.DeviceIdType.MESH,
        )

    def gather_copy(self, stage, offset):
        peer, _, ours, length = self.hop(stage, offset)
        return pltpu.make_async_remote_copy(
            src_ref=self.full.at[self.at(ours, length), :],
            dst_ref=self.full.at[self.at(ours, length), :],
            send_sem=self.sem(self.back_send, stage, offset),
            recv_sem=self.sem(self.back_recv, stage, offset),
            device_id={"dp": peer},
            device_id_type=pl.DeviceIdType.MESH,
        )

    def offsets(self, stage):
        return range(1, self.stages[stage][1])

    def reduce_start(self, stage):
        for offset in self.offsets(stage):
            _, theirs, _, length = self.hop(stage, offset)
            first = pl.multiple_of(self.base + theirs * self.rows, 16)
            copy_rows(self.acc, first, self.send, first, length * self.rows, lambda v: v.astype(BF16))
            self.reduce_copy(stage, offset).start()

    def reduce_finish(self, stage):
        for offset in self.offsets(stage):
            self.reduce_copy(stage, offset).wait_recv()
        _, _, ours, length = self.hop(stage, 0)
        shift = length * self.rows
        slot = self.base + (self.size - self.length[stage]) * self.rows
        add_rows(self.recv, slot, shift, self.stages[stage][1] - 1, self.acc,
                 pl.multiple_of(self.base + ours * self.rows, 16), shift)

    def gather_start(self, stage):
        for offset in self.offsets(stage):
            self.gather_copy(stage, offset).start()

    def gather_finish(self, stage):
        for offset in self.offsets(stage):
            self.gather_copy(stage, offset).wait_recv()

    def advance(self, step):
        count = len(self.stages)
        if 0 < step <= count:
            self.reduce_finish(step - 1)
        if step > count:
            self.gather_finish(2 * count - step)
        if step < count:
            self.reduce_start(step)
        if step == count:
            own = pl.multiple_of(self.base + self.mine * self.rows, 16)
            copy_rows(self.acc, own, self.full, own, self.rows, lambda v: v.astype(BF16))
        if count <= step < 2 * count:
            self.gather_start(2 * count - 1 - step)

    def close(self):
        for stage in range(len(self.stages)):
            for offset in self.offsets(stage):
                self.reduce_copy(stage, offset).wait_send()
                self.gather_copy(stage, offset).wait_send()


def row_block(length):
    return next(block for block in (128, 96, 64, 48, 32, 16) if length % block == 0)


def add_rows(source, first, shift, count, target, where, length):
    block = row_block(length)

    def body(t, carry):
        there = pl.ds(pl.multiple_of(where + t * block, 16), block)
        total = target[there, :]
        for n in range(count):
            here = pl.ds(pl.multiple_of(first + n * shift + t * block, 16), block)
            total = total + source[here, :].astype(F32)
        target[there, :] = total
        return carry

    lax.fori_loop(0, length // block, body, 0)


def copy_rows(source, first, target, where, length, change):
    block = row_block(length)

    def body(t, carry):
        here = pl.ds(pl.multiple_of(first + t * block, 16), block)
        there = pl.ds(pl.multiple_of(where + t * block, 16), block)
        target[there, :] = change(source[here, :])
        return carry

    lax.fori_loop(0, length // block, body, 0)


def images_in(ref, first, count):
    parts = [ref[micro, pl.ds(first, count), :, :].astype(F32) for micro in range(2)]
    return jnp.concatenate(parts, axis=1).reshape(4 * count, ref.shape[3])


def images_out(ref, first, count, value):
    value = value.reshape(count, 4, ref.shape[3])
    for micro in range(2):
        ref[micro, pl.ds(first, count)] = value[:, 2 * micro : 2 * micro + 2, :].astype(BF16)


def gelu_and_slope(pre):
    size = 1.0 + ERF_SHIFT * jnp.abs(pre)
    inv = pltpu.reciprocal(size, approx=True)
    inv = inv * (2.0 - size * inv)
    poly = (0.5 * ERF_POLY[-1]) * inv + 0.5 * ERF_POLY[-2]
    for value in reversed(ERF_POLY[:-2]):
        poly = poly * inv + 0.5 * value
    bell = jnp.exp2(pre * pre * (-0.5 * math.log2(math.e)))
    tail = poly * inv * bell
    cdf = jnp.where(pre >= 0.0, 1.0 - tail, tail)
    return (pre * cdf).astype(BF16), cdf + pre * bell * (1.0 / math.sqrt(2.0 * math.pi))


STEPS = (
    ((), (), (), ()),
    ((), (), (), (0,)),
    ((), (), (), ()),
    ((), (), (), (0, 1)),
    ((), (), (), ()),
    ((), (0,), (), (1, 2)),
)
LATER = ((), (), (0, 1), (2,), (), (1,), (2,), (0, 2, 1))


def mega_kernel(
    size,
    class_ref,
    extent_ref,
    rate_ref,
    freq_ref,
    coef_ref,
    skip_ref,
    b_in_ref,
    gain_ref,
    shift_ref,
    b_out_ref,
    scale_ref,
    w_in_hbm,
    w_out_hbm,
    x_hbm,
    cot_hbm,
    block_ref,
    dx_ref,
    full_ref,
    small_out,
    x_ref,
    cot_ref,
    w_in_ref,
    w_out_ref,
    pack_own,
    pack_oth,
    w_in_oth,
    w_out_oth,
    table_ref,
    skip_all,
    mask_ref,
    lag_ref,
    rowop_ref,
    colop_ref,
    u_ref,
    uh_ref,
    v_ref,
    mh_ref,
    mixed_ref,
    normed_ref,
    gmlp_ref,
    act_ref,
    gpre_ref,
    mlp_ref,
    gn_ref,
    stat_ref,
    gm_ref,
    row_acc,
    col_acc,
    db_ref,
    sums_ref,
    acc_ref,
    away_ref,
    landed_ref,
    send_ref,
    recv_ref,
    small_keep,
    small_land,
    small_recv,
    pair_send,
    pair_recv,
    red_send,
    red_recv,
    gat_send,
    gat_recv,
    sc_send,
    sc_recv,
    bc_send,
    bc_recv,
    in_sem,
):
    cells, channels = x_ref.shape[1], x_ref.shape[3]
    rows = 4 * cells
    own = pack_own.shape[1]
    half_hidden = w_in_ref.shape[1]
    me = lax.axis_index("dp")
    core = lax.axis_index("mp")
    partner = {"mp": 1 - core}

    barrier = pltpu.get_barrier_semaphore()
    pl.semaphore_signal(barrier, inc=1, device_id=partner, device_id_type=pl.DeviceIdType.MESH)
    for offset in range(1, size):
        pl.semaphore_signal(
            barrier,
            inc=1,
            device_id={"dp": lax.rem(me + offset, size)},
            device_id_type=pl.DeviceIdType.MESH,
        )
    reads = [
        pltpu.make_async_copy(source, target, in_sem.at[index])
        for index, (source, target) in enumerate(
            (
                (w_in_hbm, w_in_ref.at[pl.ds(0, channels), :]),
                (w_out_hbm, w_out_ref),
                (x_hbm, x_ref),
                (cot_hbm, cot_ref),
            )
        )
    ]
    for copy in reads:
        copy.start()

    def pair_copy(index, source, target):
        return pltpu.make_async_remote_copy(
            src_ref=source,
            dst_ref=target,
            send_sem=pair_send.at[index],
            recv_sem=pair_recv.at[index],
            device_id=partner,
            device_id_type=pl.DeviceIdType.MESH,
        )

    write_tables(extent_ref, rate_ref, freq_ref, coef_ref, pack_own)
    pack_own[108:109, :] = skip_ref[...].reshape(1, own)
    pack_own[109:PACK_ROWS, :] = jnp.zeros((PACK_ROWS - 109, own), F32)
    b_in = b_in_ref[...].reshape(1, half_hidden)
    b_high = b_in.astype(BF16).astype(F32)
    b_mid = (b_in - b_high).astype(BF16).astype(F32)
    b_low = b_in - b_high - b_mid
    line = lax.broadcasted_iota(jnp.int32, (16, half_hidden), 0)
    w_in_ref[channels : channels + 16, :] = jnp.where(
        line == 0, b_high, jnp.where(line == 1, b_mid, jnp.where(line == 2, b_low, 0.0))
    ).astype(BF16)
    rest = WIDE - channels - 16
    w_in_ref[channels + 16 : WIDE, :] = jnp.zeros((rest, half_hidden), BF16)
    w_in_oth[channels + 16 : WIDE, :] = jnp.zeros((rest, half_hidden), BF16)
    pl.semaphore_wait(barrier, size)
    pack_copy = pair_copy(0, pack_own, pack_oth)
    first_copy = pair_copy(
        1, w_in_ref.at[pl.ds(0, channels + 16), :], w_in_oth.at[pl.ds(0, channels + 16), :]
    )
    second_copy = pair_copy(2, w_out_ref, w_out_oth)
    pack_copy.start()
    reads[0].wait()
    first_copy.start()
    reads[1].wait()
    second_copy.start()

    build_masks(class_ref, mask_ref)
    block = 144
    scale = scale_ref[...].reshape(1, channels)
    normed_ref[:, channels:] = jnp.where(
        lax.broadcasted_iota(jnp.int32, (rows, WIDE - channels), 1) < 3, 1.0, 0.0
    ).astype(BF16)
    gn_ref[...] = jnp.zeros_like(gn_ref)
    reads[2].wait()
    reads[3].wait()

    def load(t, carry):
        at = pl.ds(pl.multiple_of(t * 48, 16), 48)
        u_ref[at, :] = images_in(x_ref, t * 12, 12)
        mask = jnp.tile(mask_ref[at, :], (1, channels // 128))
        gmlp_ref[at, :] = (images_in(cot_ref, t * 12, 12) * scale * mask).astype(BF16)
        return carry

    lax.fori_loop(0, rows // 48, load, 0)
    mirror_in(u_ref, mask_ref, uh_ref)

    pack_copy.wait_recv()
    first = core == 0
    low = jnp.where(first, pack_own[...], pack_oth[...])
    high = jnp.where(first, pack_oth[...], pack_own[...])
    table_ref[...] = jnp.concatenate([low, high], axis=1)
    skip_all[...] = table_ref[108:109, :]
    build_operators(class_ref, table_ref, lag_ref, rowop_ref, colop_ref)
    apply_rows(rowop_ref, uh_ref, v_ref)
    apply_cols(colop_ref, v_ref, mh_ref)
    mirror_out(mh_ref, mask_ref, mixed_ref, u_ref, skip_all)

    gain = gain_ref[...].reshape(1, channels)
    shift = shift_ref[...].reshape(1, channels)

    def norm(t, carry):
        at = pl.ds(pl.multiple_of(t * block, block), block)
        value = mixed_ref[at, :]
        mean = jnp.mean(value, axis=1, keepdims=True)
        centered = value - mean
        variance = jnp.mean(centered * centered, axis=1, keepdims=True)
        rstd = lax.rsqrt(variance + 1e-06)
        hat = centered * rstd
        mixed_ref[at, :] = hat
        stat_ref[at, :] = jnp.broadcast_to(rstd, (block, 128))
        normed_ref[at, :channels] = (hat * gain + shift).astype(BF16)
        return carry

    lax.fori_loop(0, rows // block, norm, 0)

    chunk = CHUNK
    tile_rows = 432
    first_copy.wait_recv()
    second_copy.wait_recv()

    group_rows = 2 * channels * chunk // 128
    per_chunk = chunk_rows(group_rows, size)
    stride = per_chunk * size
    groups = half_hidden // chunk
    rings = [
        Ring(group, size, per_chunk, acc_ref, send_ref, recv_ref, full_ref,
             (red_send, red_recv, gat_send, gat_recv))
        for group in range(groups)
    ]
    done = [0] * groups

    def advance(*which):
        last = 2 * len(stages_of(size))
        for group in which:
            if done[group] > last:
                continue
            rings[group].advance(done[group])
            done[group] += 1

    tiles = rows // tile_rows
    shares = []

    def feed(f, w_first_ref, w_second_ref, target_ref, target_base, db_row, steps, ready):
        cols = pl.ds(f * chunk, chunk)
        act_cols = pl.ds((1 - db_row) * half_hidden + f * chunk, chunk)

        def ahead(t):
            at = pl.ds(t * tile_rows, tile_rows)
            pre = jnp.dot(normed_ref[at, :], w_first_ref[:, cols], preferred_element_type=F32)
            g_act = lax.dot_general(
                gmlp_ref[at, :],
                w_second_ref[cols, :],
                (((1,), (1,)), ((), ())),
                preferred_element_type=F32,
            )
            return pre, g_act

        def outward(t, g_pre):
            at = pl.ds(t * tile_rows, tile_rows)
            gn_ref[at, :] += lax.dot_general(
                g_pre,
                w_first_ref[:channels, cols],
                (((1,), (1,)), ((), ())),
                preferred_element_type=F32,
            )

        late = f == groups - 1 and db_row == 0
        waiting = ahead(0)
        for t in range(tiles):
            pre, g_act = waiting
            if t + 1 < tiles:
                waiting = ahead(t + 1)
            at = pl.ds(t * tile_rows, tile_rows)
            act, slope = gelu_and_slope(pre)
            g_pre = (g_act * slope).astype(BF16)
            act_ref[at, act_cols] = act
            gpre_ref[at, :] = g_pre
            if not late:
                outward(t, g_pre)
            advance(*steps[t])
        d_first = lax.dot_general(
            normed_ref[:, : channels + 16],
            gpre_ref[...],
            (((0,), (0,)), ((), ())),
            preferred_element_type=F32,
        )
        for k in range(chunk // 128):
            at = pl.ds(target_base + k * channels, channels)
            target_ref[at, :] = d_first[:channels, k * 128 : (k + 1) * 128].astype(target_ref.dtype)
        db_ref[db_row : db_row + 1, cols] = d_first[channels : channels + 1, :]
        d_second = lax.dot_general(
            act_ref[:, act_cols], gmlp_ref[...], (((0,), (0,)), ((), ())), preferred_element_type=F32
        )
        base = target_base + channels * (chunk // 128)
        for k in range(channels // 128):
            at = pl.ds(base + k * chunk, chunk)
            target_ref[at, :] = d_second[:, k * 128 : (k + 1) * 128].astype(target_ref.dtype)
        shares.append(
            jnp.sum(d_second * w_second_ref[cols, :].astype(F32), axis=0, keepdims=True)
        )
        ready(f)
        advance(*steps[3])
        if late:
            for t in range(tiles):
                at = pl.ds(t * tile_rows, tile_rows)
                outward(t, gpre_ref[at, :])

    def grads_copy(group):
        at = pl.ds(group * group_rows, group_rows)
        return pair_copy(4 + group, away_ref.at[at, :], landed_ref.at[at, :])

    def join(group):
        grads_copy(group).wait_recv()
        add_rows(landed_ref, group * group_rows, 0, 1, acc_ref, group * stride, group_rows)
        if stride > group_rows:
            acc_ref[group * stride + group_rows : (group + 1) * stride, :] = jnp.zeros(
                (stride - group_rows, 128), F32
            )

    for group in range(groups):
        feed(group, w_in_oth, w_out_oth, away_ref, group * group_rows, 1, STEPS[2 * group],
             lambda g: grads_copy(g).start())
        feed(group, w_in_ref, w_out_ref, acc_ref, group * stride, 0, STEPS[2 * group + 1], join)

    def back(t, carry):
        d_gain, d_bias, d_b_out = carry
        at = pl.ds(pl.multiple_of(t * 48, 16), 48)
        d_b_out = d_b_out + jnp.sum(gmlp_ref[at, :].astype(F32), axis=0, keepdims=True)
        grad = gn_ref[at, :]
        hat = mixed_ref[at, :]
        d_gain = d_gain + jnp.sum(grad * hat, axis=0, keepdims=True)
        d_bias = d_bias + jnp.sum(grad, axis=0, keepdims=True)
        grad = grad * gain
        mean_g = jnp.mean(grad, axis=1, keepdims=True)
        mean_gh = jnp.mean(grad * hat, axis=1, keepdims=True)
        rstd = jnp.tile(stat_ref[at, :], (1, channels // 128))
        gm_ref[at, :] = (rstd * (grad - mean_g - hat * mean_gh)).astype(BF16).astype(F32)
        return d_gain, d_bias, d_b_out

    zero = jnp.zeros((1, channels), F32)
    d_gain, d_bias, d_b_out = lax.fori_loop(0, rows // 48, back, (zero, zero, zero))
    b_out = b_out_ref[...].reshape(1, channels)
    d_scale = (sum(shares) + b_out * d_b_out) / scale
    sums = (d_gain, d_bias, d_scale, d_b_out)
    mine_only = pl.ds(pl.multiple_of(core * 256, 128), 128)
    theirs_only = pl.ds(pl.multiple_of((1 - core) * 256, 128), 128)
    for index, value in enumerate(sums):
        for k in range(channels // 128):
            row = 115 + index * (channels // 128) + k
            tile = value[:, k * 128 : (k + 1) * 128]
            sums_ref[row : row + 1, mine_only] = tile
            sums_ref[row : row + 1, theirs_only] = tile
    for k in range(half_hidden // 128):
        at = slice(k * 128, (k + 1) * 128)
        sums_ref[109 + k : 110 + k, mine_only] = db_ref[0:1, at]
        sums_ref[109 + k : 110 + k, theirs_only] = db_ref[1:2, at]
    sums_ref[109:127, 128:256] = jnp.zeros((18, 128), F32)
    sums_ref[127:128, :] = zero
    advance(*LATER[0])
    gh_ref, xh_ref = mh_ref, row_acc
    mirror_in(gm_ref, mask_ref, gh_ref)
    col_correlate(gh_ref, v_ref, col_acc)
    advance(*LATER[1])
    apply_cols(colop_ref, gh_ref, xh_ref)
    advance(*LATER[2])
    row_correlate(xh_ref, uh_ref, v_ref)
    advance(*LATER[3])
    gather_lags(class_ref, v_ref, col_acc, sums_ref)

    def skip_sum(t, total):
        at = pl.ds(pl.multiple_of(t * block, block), block)
        return total + jnp.sum(gm_ref[at, :] * u_ref[at, :], axis=0, keepdims=True)

    sums_ref[108:109, :] = lax.fori_loop(0, rows // block, skip_sum, zero)
    mine_slice = pl.ds(pl.multiple_of(core * 128, 128), 256)
    theirs_slice = pl.ds(pl.multiple_of((1 - core) * 128, 128), 256)
    small_pair = pair_copy(3, sums_ref.at[:, theirs_slice], small_land)
    small_pair.start()
    apply_rows(rowop_ref, xh_ref, gh_ref)
    advance(*LATER[4])
    small_pair.wait_recv()
    small_keep[0:SUM_ROWS, :] = sums_ref[:, mine_slice] + small_land[...]
    if small_keep.shape[0] > SUM_ROWS:
        small_keep[SUM_ROWS:, :] = jnp.zeros((small_keep.shape[0] - SUM_ROWS, 256), F32)

    per = small_keep.shape[0] // size
    mine = pl.ds(pl.multiple_of(me * per, 8), per)

    def scatter_copy(offset):
        target = lax.rem(me + offset, size)
        return pltpu.make_async_remote_copy(
            src_ref=small_keep.at[pl.ds(pl.multiple_of(target * per, 8), per), :],
            dst_ref=small_recv.at[offset - 1],
            send_sem=sc_send.at[offset - 1],
            recv_sem=sc_recv.at[offset - 1],
            device_id={"dp": target},
            device_id_type=pl.DeviceIdType.MESH,
        )

    def spread_copy(offset):
        target = lax.rem(me + offset, size)
        return pltpu.make_async_remote_copy(
            src_ref=small_out.at[mine, :],
            dst_ref=small_out.at[mine, :],
            send_sem=bc_send.at[offset - 1],
            recv_sem=bc_recv.at[offset - 1],
            device_id={"dp": target},
            device_id_type=pl.DeviceIdType.MESH,
        )

    for offset in range(1, size):
        scatter_copy(offset).start()
    mirror_out(gh_ref, mask_ref, gn_ref, gm_ref, skip_all)
    advance(*LATER[5])
    for t in range(tiles):
        at = pl.ds(t * tile_rows, tile_rows)
        mlp_ref[at, :] = (
            jnp.dot(act_ref[at, :half_hidden], w_out_oth[...], preferred_element_type=F32)
            + jnp.dot(act_ref[at, half_hidden:], w_out_ref[...], preferred_element_type=F32)
            + b_out
        )

    def finish(t, carry):
        at = pl.ds(pl.multiple_of(t * 48, 16), 48)
        images_out(dx_ref, t * 12, 12, images_in(cot_ref, t * 12, 12) + gn_ref[at, :])
        branch = mlp_ref[at, :] * jnp.tile(mask_ref[at, :], (1, channels // 128))
        images_out(block_ref, t * 12, 12, u_ref[at, :] + scale * branch)
        return carry

    lax.fori_loop(0, rows // 48, finish, 0)
    advance(*LATER[6])
    total = small_keep[mine, :]
    for offset in range(1, size):
        scatter_copy(offset).wait_recv()
        total = total + small_recv[offset - 1]
    small_out[mine, :] = total
    for offset in range(1, size):
        spread_copy(offset).start()

    advance(*LATER[7])
    for _ in range(2 * len(stages_of(size)) + 1):
        advance(*range(groups))
    for offset in range(1, size):
        spread_copy(offset).wait_recv()
    for offset in range(1, size):
        scatter_copy(offset).wait_send()
        spread_copy(offset).wait_send()
    for group in range(groups):
        rings[group].close()
        grads_copy(group).wait_send()
    for copy in (pack_copy, first_copy, second_copy, small_pair):
        copy.wait_send()


def final_kernel(
    extent_ref, rate_ref, freq_ref, coef_ref, small_ref, block_hbm, dx_hbm, full_hbm,
    block_out, dx_out, rate_out, freq_out, coef_out, skip_out, gain_out, bias_out, dw_in_out,
    db_in_out, dw_out_out, b_out_out, scale_out,
    mine_ref, dw_in_ref, dw_out_ref, full_ref, block_ref, dx_ref, sems,
):
    channels, half_hidden = dw_in_ref.shape
    groups = half_hidden // CHUNK
    stride = full_ref.shape[0] // groups

    def moves(first, *pairs):
        return [
            pltpu.make_async_copy(source, target, sems.at[first + k])
            for k, (source, target) in enumerate(pairs)
        ]

    reads = moves(0, (full_hbm, full_ref), (block_hbm, block_ref), (dx_hbm, dx_ref))
    writes = moves(3, (dw_in_ref, dw_in_out), (dw_out_ref, dw_out_out), (block_ref, block_out), (dx_ref, dx_out))
    for copy in reads:
        copy.start()
    core = lax.axis_index("mp")
    own = mine_ref.shape[1]
    mine_ref[...] = jnp.where(core == 0, small_ref[0:112, :own], small_ref[0:112, 256 - own :])
    only = pl.ds(pl.multiple_of(core * 128, 128), 128)

    def line(first, count):
        return jnp.concatenate([small_ref[first + k : first + k + 1, only] for k in range(count)], axis=1)

    args = (extent_ref, rate_ref, freq_ref, coef_ref, mine_ref, rate_out, freq_out, coef_out)
    modes_grad(0, *args)
    reads[0].wait()
    for group in range(groups):
        base = group * stride
        for k in range(CHUNK // 128):
            at = group * CHUNK + k * 128
            dw_in_ref[:, at : at + 128] = full_ref[base : base + channels, :].astype(F32)
            base += channels
        for k in range(channels // 128):
            dw_out_ref[group * CHUNK : (group + 1) * CHUNK, k * 128 : (k + 1) * 128] = full_ref[
                base : base + CHUNK, :
            ].astype(F32)
            base += CHUNK
    writes[0].start()
    writes[1].start()
    reads[1].wait()
    writes[2].start()
    reads[2].wait()
    writes[3].start()
    modes_grad(1, *args)
    skip_out[...] = mine_ref[108:109, :].reshape(skip_out.shape)
    db_in_out[...] = line(109, db_in_out.shape[0] // 128).reshape(db_in_out.shape)
    for k, ref in enumerate((gain_out, bias_out, scale_out, b_out_out)):
        ref[...] = line(115 + 3 * k, 3).reshape(ref.shape)
    for copy in writes:
        copy.wait()


ANY = pl.BlockSpec(memory_space=pl.ANY)
VM = pl.BlockSpec(memory_space=pltpu.VMEM)
SM = pl.BlockSpec(memory_space=pltpu.SMEM)


def shape(dims, kind=F32):
    return jax.ShapeDtypeStruct(dims, kind)


def on_device(
    size,
    pixels,
    grid_class,
    extent,
    ssm_rate,
    ssm_freq,
    ssm_coef,
    skip_gain,
    norm_gain,
    norm_bias,
    w_in,
    b_in,
    w_out,
    b_out,
    layer_scale,
    cotangent,
):
    micro, count, channels, cells = pixels.shape
    rows = micro * count * cells
    own = ssm_rate.shape[1]
    modes = ssm_rate.shape[2]
    half_hidden = b_in.shape[0]
    x = pixels.transpose(0, 3, 1, 2)
    cot = cotangent.transpose(0, 3, 1, 2)
    rate = ssm_rate.transpose(0, 2, 1)
    freq = ssm_freq.transpose(0, 2, 1)
    coef = ssm_coef.transpose(0, 2, 1)
    field = (rows, channels)
    grad_rows = 2 * channels * half_hidden // 128
    groups = half_hidden // CHUNK
    all_rows = groups * chunk_rows(grad_rows // groups, size) * size
    stages = stages_of(size)
    hops = (groups, max(len(stages), 1), max([members - 1 for _, members in stages] + [1]))
    small_rows = max(128, 8 * size)
    peers = max(size - 1, 1)
    DMA = pltpu.SemaphoreType.DMA
    block_out, dx, full, small = pl.pallas_call(
        partial(mega_kernel, size),
        out_shape=(
            shape(x.shape, BF16),
            shape(x.shape, BF16),
            shape((all_rows, 128), BF16),
            shape((small_rows, 256)),
        ),
        in_specs=[SM] + [VM] * 10 + [ANY] * 4,
        out_specs=(VM,) * 4,
        scratch_shapes=[
            pltpu.VMEM(x.shape, BF16),
            pltpu.VMEM(x.shape, BF16),
            pltpu.VMEM((WIDE, half_hidden), BF16),
            pltpu.VMEM(w_out.shape, BF16),
            pltpu.VMEM((PACK_ROWS, own), F32),
            pltpu.VMEM((PACK_ROWS, own), F32),
            pltpu.VMEM((WIDE, half_hidden), BF16),
            pltpu.VMEM(w_out.shape, BF16),
            pltpu.VMEM((PACK_ROWS, channels), F32),
            pltpu.VMEM((1, channels), F32),
            pltpu.VMEM((rows, 128), F32),
            pltpu.VMEM((2 * GRID, 8, channels), F32),
            pltpu.VMEM((90, 8, channels), F32),
            pltpu.VMEM((45, 8, channels), F32),
            pltpu.VMEM(field, F32),
            pltpu.VMEM(field, F32),
            pltpu.VMEM(field, F32),
            pltpu.VMEM(field, F32),
            pltpu.VMEM(field, F32),
            pltpu.VMEM((rows, WIDE), BF16),
            pltpu.VMEM(field, BF16),
            pltpu.VMEM((rows, 2 * half_hidden), BF16),
            pltpu.VMEM((rows, CHUNK), BF16),
            pltpu.VMEM(field, F32),
            pltpu.VMEM(field, F32),
            pltpu.VMEM((rows, 128), F32),
            pltpu.VMEM(field, F32),
            pltpu.VMEM((162 * 8, channels), F32),
            pltpu.VMEM((81 * 8, channels), F32),
            pltpu.VMEM((2, half_hidden), F32),
            pltpu.VMEM((SUM_ROWS, channels), F32),
            pltpu.VMEM((all_rows, 128), F32),
            pltpu.VMEM((grad_rows, 128), BF16),
            pltpu.VMEM((grad_rows, 128), BF16),
            pltpu.VMEM((all_rows, 128), BF16),
            pltpu.VMEM((all_rows, 128), BF16),
            pltpu.VMEM((small_rows, 256), F32),
            pltpu.VMEM((SUM_ROWS, 256), F32),
            pltpu.VMEM((peers, small_rows // size, 256), F32),
            DMA((4 + groups,)),
            DMA((4 + groups,)),
            DMA(hops),
            DMA(hops),
            DMA(hops),
            DMA(hops),
            DMA((peers,)),
            DMA((peers,)),
            DMA((peers,)),
            DMA((peers,)),
            DMA((4,)),
        ],
        compiler_params=pltpu.CompilerParams(
            vmem_limit_bytes=VMEM_LIMIT, collective_id=0, has_side_effects=True
        ),
        name="block",
    )(
        grid_class,
        extent,
        rate,
        freq,
        coef,
        skip_gain,
        b_in,
        norm_gain,
        norm_bias,
        b_out,
        layer_scale,
        w_in,
        w_out,
        x,
        cot,
    )
    (
        block_out, dx, g_rate, g_freq, g_coef, g_skip, g_gain, g_bias, dw_in, db_in, dw_out, g_b_out, g_scale,
    ) = pl.pallas_call(
        final_kernel,
        out_shape=(
            shape(x.shape, BF16),
            shape(x.shape, BF16),
            shape((2, modes, own)),
            shape((2, modes, own)),
            shape((2, modes, own)),
            shape((own,)),
            shape((channels,)),
            shape((channels,)),
            shape(w_in.shape),
            shape((half_hidden,)),
            shape(w_out.shape),
            shape((channels,)),
            shape((channels,)),
        ),
        in_specs=[VM] * 5 + [ANY] * 3,
        out_specs=(ANY, ANY) + (VM,) * 6 + (ANY, VM, ANY, VM, VM),
        scratch_shapes=[
            pltpu.VMEM((112, own), F32),
            pltpu.VMEM(w_in.shape, F32),
            pltpu.VMEM(w_out.shape, F32),
            pltpu.VMEM(full.shape, BF16),
            pltpu.VMEM(x.shape, BF16),
            pltpu.VMEM(x.shape, BF16),
            DMA((7,)),
        ],
        compiler_params=pltpu.CompilerParams(vmem_limit_bytes=VMEM_LIMIT),
        name="final",
    )(extent, rate, freq, coef, small, block_out, dx, full)
    return (
        block_out.transpose(0, 2, 3, 1),
        dx.transpose(0, 2, 3, 1),
        g_rate.transpose(0, 2, 1),
        g_freq.transpose(0, 2, 1),
        g_coef.transpose(0, 2, 1),
        g_skip,
        g_gain,
        g_bias,
        dw_in,
        db_in,
        dw_out,
        g_b_out,
        g_scale,
    )


def solution(mesh):
    placed = (
        P(None, ("dp", "mp"), None, None),
        P(None, "dp"),
        P("mp"),
        P(None, "mp", None),
        P(None, "mp", None),
        P(None, "mp", None),
        P("mp"),
        P(),
        P(),
        P(None, "mp"),
        P("mp"),
        P("mp", None),
        P(),
        P(),
        P(None, ("dp", "mp"), None, None),
    )
    return jax.shard_map(
        partial(on_device, mesh.shape["dp"]),
        mesh=mesh,
        in_specs=placed,
        out_specs=(
            P(None, ("dp", "mp"), None, None),
            P(None, ("dp", "mp"), None, None),
            P(None, "mp", None),
            P(None, "mp", None),
            P(None, "mp", None),
            P("mp"),
            P(),
            P(),
            P(None, "mp"),
            P("mp"),
            P("mp", None),
            P(),
            P(),
        ),
        check_vma=False,
    )
```

```python
import math
from functools import partial

import jax
import jax.numpy as jnp
import numpy as np
from jax import lax
from jax.experimental import pallas as pl
from jax.experimental.pallas import tpu as pltpu
from jax.sharding import PartitionSpec as P

GRID = 18
HALF = 9
SIDES = (10, 14, 18)
LAGS = 3 * GRID
F32 = jnp.float32
BF16 = jnp.bfloat16

ERF_SHIFT = 0.35 / math.sqrt(2.0)
ERF_POLY = (
    0.19396706,
    0.23864529,
    -0.01708609,
    0.69839275,
    -0.6929918,
    0.77818103,
    -0.19910822,
)
CHUNK = 256
VMEM_LIMIT = 60 * 1024 * 1024


def small_sincos(angle):
    sq = angle * angle
    cos = 1.0 + sq * (
        -1 / 2 + sq * (1 / 24 + sq * (-1 / 720 + sq * (1 / 40320 + sq * (-1 / 3628800))))
    )
    sin = angle * (
        1.0
        + sq * (-1 / 6 + sq * (1 / 120 + sq * (-1 / 5040 + sq * (1 / 362880 + sq * (-1 / 39916800)))))
    )
    return sin, cos


def mode_step(rate, freq, side):
    decay = jnp.exp(rate * (-1.0 / side))
    sin, cos = small_sincos(freq * (1.0 / side))
    return decay * cos, decay * sin


PACK_ROWS = 112
SUM_ROWS = 128
WIDE = 512


def write_tables(extent_ref, rate_ref, freq_ref, coef_ref, out_ref):
    extent = extent_ref[...].reshape(1, extent_ref.shape[0])
    for axis in range(2):
        for cat, side in enumerate(SIDES):
            z_re, z_im = mode_step(rate_ref[axis], freq_ref[axis], side)
            w_re = coef_ref[axis]
            w_im = jnp.zeros_like(w_re)
            for lag in range(GRID):
                row = axis * LAGS + cat * GRID + lag
                if lag >= side:
                    out_ref[row : row + 1, :] = jnp.zeros((1, w_re.shape[1]), F32)
                    continue
                total = jnp.sum(w_re, axis=0, keepdims=True)
                out_ref[row : row + 1, :] = jnp.where(extent > lag, total, 0.0)
                if lag < side - 1:
                    w_re, w_im = w_re * z_re - w_im * z_im, w_re * z_im + w_im * z_re


def modes_grad(axis, extent_ref, rate_ref, freq_ref, coef_ref, dk_ref, rate_out, freq_out, coef_out):
    extent = extent_ref[...].reshape(1, extent_ref.shape[0])
    if True:
        coef = coef_ref[axis]
        g_rate = jnp.zeros_like(coef)
        g_freq = jnp.zeros_like(coef)
        g_coef = jnp.zeros_like(coef)
        for cat, side in enumerate(SIDES):
            z_re, z_im = mode_step(rate_ref[axis], freq_ref[axis], side)
            p_re = jnp.zeros_like(coef)
            p_im = jnp.zeros_like(coef)
            q_re = jnp.zeros_like(coef)
            q_im = jnp.zeros_like(coef)
            for lag in reversed(range(side)):
                row = axis * LAGS + cat * GRID + lag
                d = jnp.where(extent > lag, dk_ref[row : row + 1, :], 0.0)
                p_re, p_im = p_re * z_re - p_im * z_im + d, p_re * z_im + p_im * z_re
                q_re, q_im = q_re * z_re - q_im * z_im + float(lag) * d, q_re * z_im + q_im * z_re
            g_coef = g_coef + p_re
            g_rate = g_rate - (1.0 / side) * q_re
            g_freq = g_freq - (1.0 / side) * q_im
        coef_out[axis] = g_coef
        rate_out[axis] = g_rate * coef
        freq_out[axis] = g_freq * coef

def tri(a, b):
    low, high = min(a, b), max(a, b)
    return low * HALF - low * (low - 1) // 2 + (high - low)


def rows8(index):
    if isinstance(index, int):
        return pl.ds(index * 8, 8)
    return pl.ds(pl.multiple_of(index * 8, 8), 8)


def lanes(tile):
    if isinstance(tile, int):
        return pl.ds(tile * 128, 128)
    return pl.ds(pl.multiple_of(tile * 128, 128), 128)


def swap(value):
    return pltpu.roll(value, 4, 0)


def sublane_half():
    return lax.broadcasted_iota(jnp.int32, (8, 128), 0) < 4


def side_vreg(class_ref):
    mine = lax.axis_index("mp")
    image = lax.rem(lax.broadcasted_iota(jnp.int32, (8, 128), 0), 4)
    cls = jnp.zeros((8, 128), jnp.int32)
    own = class_ref.shape[1] // 2
    for micro in range(2):
        for img in range(2):
            cls = jnp.where(image == micro * 2 + img, class_ref[micro, mine * own + img], cls)
    return 10 + 4 * cls


def build_masks(class_ref, mask_ref):
    side = side_vreg(class_ref)
    offset = jnp.where(sublane_half(), 0, 1)

    def row(i, carry):
        for pair in range(HALF):
            ok = (i < side) & (2 * pair + offset < side)
            mask_ref[rows8(i * HALF + pair), :] = jnp.where(ok, 1.0, 0.0).astype(F32)
        return carry

    lax.fori_loop(0, GRID, row, 0)


def build_operators(class_ref, table_ref, lag_ref, rowop_ref, colop_ref):
    side = side_vreg(class_ref)
    sign = jnp.where(sublane_half(), 1.0, -1.0).astype(F32)
    tiles = table_ref.shape[1] // 128

    def tile_body(tile, carry):
        at = lanes(tile)
        for axis in range(2):
            for lag in range(GRID):
                by_side = [
                    jnp.broadcast_to(table_ref[axis * LAGS + cat * GRID + lag : axis * LAGS + cat * GRID + lag + 1, at], (8, 128))
                    for cat in range(3)
                ]
                lag_ref[axis * GRID + lag, :, at] = 0.5 * jnp.where(
                    side == 10, by_side[0], jnp.where(side == 14, by_side[1], by_side[2])
                )
        for a in range(HALF):
            for b in range(a, HALF):
                near = lag_ref[b - a, :, at]
                far = lag_ref[GRID - 1 - a - b, :, at]
                rowop_ref[tri(a, b), :, at] = near + far
                rowop_ref[45 + tri(a, b), :, at] = near - far
                near = lag_ref[GRID + b - a, :, at]
                far = lag_ref[GRID + GRID - 1 - a - b, :, at]
                colop_ref[tri(a, b), :, at] = near + sign * far
        return carry

    lax.fori_loop(0, tiles, tile_body, 0)


def mirror_in(source_ref, mask_ref, out_ref):
    half = sublane_half()
    sign = jnp.where(half, 1.0, -1.0).astype(F32)
    tiles = source_ref.shape[1] // 128

    def body(i, carry):
        for tile in range(tiles):
            at = lanes(tile)

            def mirrored(row, pair):
                near = source_ref[rows8(row * HALF + pair), at] * mask_ref[rows8(row * HALF + pair), :]
                if pair == 4:
                    return swap(near) + sign * near, None
                other = row * HALF + 8 - pair
                far = source_ref[rows8(other), at] * mask_ref[rows8(other), :]
                even = jnp.where(half, near, far)
                odd = jnp.where(half, far, near)
                return swap(even) + sign * even, odd + sign * swap(odd)

            for pair in range(5):
                top = mirrored(i, pair)
                bottom = mirrored(GRID - 1 - i, pair)
                for step in range(2 if pair < 4 else 1):
                    where = i * HALF + 2 * pair + step
                    out_ref[rows8(where), at] = top[step] + bottom[step]
                    out_ref[rows8(81 + where), at] = top[step] - bottom[step]
        return carry

    lax.fori_loop(0, HALF, body, 0)


def mirror_out(source_ref, mask_ref, out_ref, extra_ref, gain_ref):
    half = sublane_half()
    sign = jnp.where(half, 1.0, -1.0).astype(F32)
    tiles = source_ref.shape[1] // 128

    def body(i, carry):
        for tile in range(tiles):
            at = lanes(tile)
            gain = jnp.broadcast_to(gain_ref[:, at], (8, 128))

            def finish(index, value):
                value = value * mask_ref[rows8(index), :] + gain * extra_ref[rows8(index), at]
                out_ref[rows8(index), at] = value.astype(BF16).astype(F32)

            for pair in range(5):
                both = []
                for step in range(2 if pair < 4 else 1):
                    where = i * HALF + 2 * pair + step
                    plus = source_ref[rows8(where), at]
                    minus = source_ref[rows8(81 + where), at]
                    top, bottom = plus + minus, plus - minus
                    both.append(
                        (swap(top) + sign * top, swap(bottom) + sign * bottom)
                        if step == 0
                        else (top - sign * swap(top), bottom - sign * swap(bottom))
                    )
                for part, row in ((0, i), (1, GRID - 1 - i)):
                    if pair == 4:
                        finish(row * HALF + 4, both[0][part])
                        continue
                    if True:
                        even, odd = both[0][part], both[1][part]
                        finish(row * HALF + pair, jnp.where(half, even, odd))
                        finish(row * HALF + 8 - pair, jnp.where(half, odd, even))
        return carry

    lax.fori_loop(0, HALF, body, 0)


def apply_rows(op_ref, source_ref, out_ref):
    tiles = source_ref.shape[1] // 128

    def body(j, carry):
        for tile in range(tiles):
            at = lanes(tile)
            for rho in range(2):
                values = [source_ref[rows8(rho * 81 + p * HALF + j), at] for p in range(HALF)]
                for i in range(HALF):
                    total = None
                    for p in range(HALF):
                        term = op_ref[rho * 45 + tri(i, p), :, at] * values[p]
                        total = term if total is None else total + term
                    out_ref[rows8(rho * 81 + i * HALF + j), at] = total
        return carry

    lax.fori_loop(0, HALF, body, 0)


def apply_cols(op_ref, source_ref, out_ref):
    tiles = source_ref.shape[1] // 128

    def body(i, carry):
        for tile in range(tiles):
            at = lanes(tile)
            values = [source_ref[rows8(i * HALF + q), at] for q in range(HALF)]
            for j in range(HALF):
                total = None
                for q in range(HALF):
                    term = op_ref[tri(j, q), :, at] * values[q]
                    total = term if total is None else total + term
                out_ref[rows8(i * HALF + j), at] = total
        return carry

    lax.fori_loop(0, 2 * HALF, body, 0)


def row_correlate(left_ref, right_ref, acc_ref, cut=3):
    for tile in range(left_ref.shape[1] // 128):
        for rho in range(2):

            def body(step, carry, at=lanes(tile), rho=rho):
                first = step * cut
                sums = [[None] * HALF for _ in range(cut)]
                for j in range(HALF):
                    left = [
                        left_ref[rows8(rho * 81 + (first + k) * HALF + j), at] for k in range(cut)
                    ]
                    for p in range(HALF):
                        right = right_ref[rows8(rho * 81 + p * HALF + j), at]
                        for k in range(cut):
                            term = left[k] * right
                            sums[k][p] = term if sums[k][p] is None else sums[k][p] + term
                for k in range(cut):
                    for p in range(HALF):
                        acc_ref[rows8(rho * 81 + (first + k) * HALF + p), at] = sums[k][p]
                return carry

            lax.fori_loop(0, HALF // cut, body, 0)


def col_correlate(left_ref, right_ref, acc_ref, cut=3):
    for tile in range(left_ref.shape[1] // 128):

        def body(step, carry, at=lanes(tile)):
            first = step * cut
            sums = [[None] * HALF for _ in range(cut)]
            for i in range(2 * HALF):
                left = [left_ref[rows8(i * HALF + first + k), at] for k in range(cut)]
                for q in range(HALF):
                    right = right_ref[rows8(i * HALF + q), at]
                    for k in range(cut):
                        term = left[k] * right
                        sums[k][q] = term if sums[k][q] is None else sums[k][q] + term
            for k in range(cut):
                for q in range(HALF):
                    acc_ref[rows8((first + k) * HALF + q), at] = sums[k][q]
            return carry

        lax.fori_loop(0, HALF // cut, body, 0)


def gather_lags(class_ref, row_acc, col_acc, dk_ref):
    side = side_vreg(class_ref)
    sign = jnp.where(sublane_half(), 1.0, -1.0).astype(F32)
    tiles = row_acc.shape[1] // 128

    def body(tile, carry):
        at = lanes(tile)
        for axis in range(2):
            near = [None] * HALF
            far = [None] * GRID
            for a in range(HALF):
                for b in range(HALF):
                    if axis == 0:
                        plus = row_acc[rows8(a * HALF + b), at]
                        minus = row_acc[rows8(81 + a * HALF + b), at]
                        direct, cross = plus + minus, plus - minus
                    else:
                        direct = col_acc[rows8(a * HALF + b), at]
                        cross = sign * direct
                    d, s = abs(a - b), GRID - 1 - a - b
                    near[d] = direct if near[d] is None else near[d] + direct
                    far[s] = cross if far[s] is None else far[s] + cross
            for lag in range(GRID):
                total = None
                for part in ([near[lag]] if lag < HALF else []) + ([far[lag]] if lag else []):
                    total = part if total is None else total + part
                total = 0.5 * total
                for cat, length in enumerate(SIDES):
                    row = axis * LAGS + cat * GRID + lag
                    value = jnp.where(side == length, total, 0.0)
                    dk_ref[row : row + 1, at] = jnp.sum(value, axis=0, keepdims=True)
        return carry

    lax.fori_loop(0, tiles, body, 0)


def stages_of(size):
    bits = size.bit_length() - 1
    stages, stride = [], 1
    while bits:
        take = bits if bits <= 3 and bits != 2 else 2
        stages.append((stride, 1 << take))
        stride <<= take
        bits -= take
    return stages


def chunk_rows(rows, size):
    return -(-rows // (16 * size)) * 16


class Ring:
    def __init__(self, group, size, rows, acc, send, recv, full, sems):
        self.group, self.size, self.rows = group, size, rows
        self.acc, self.send, self.recv, self.full = acc, send, recv, full
        self.send_sem, self.recv_sem, self.back_send, self.back_recv = sems
        self.stages = stages_of(size)
        self.me = lax.axis_index("dp")
        self.base = group * size * rows
        self.digit, self.start, self.length = [], [], []
        start, length = 0, size
        for stride, members in self.stages:
            digit = lax.rem(self.me // stride, members)
            self.digit.append(digit)
            self.start.append(start)
            self.length.append(length)
            length //= members
            start = start + digit * length
        self.mine = start

    def at(self, chunk, count):
        return pl.ds(pl.multiple_of(self.base + chunk * self.rows, 16), count * self.rows)

    def hop(self, stage, offset):
        stride, members = self.stages[stage]
        digit = self.digit[stage]
        other = lax.rem(digit + offset, members)
        length = self.length[stage] // members
        start = self.start[stage]
        return self.me + (other - digit) * stride, start + other * length, start + digit * length, length

    def slot(self, stage, offset):
        length = self.length[stage] // self.stages[stage][1]
        return self.at(self.size - self.length[stage] + (offset - 1) * length, length)

    def sem(self, sems, stage, offset):
        return sems.at[self.group, stage, offset - 1]

    def reduce_copy(self, stage, offset):
        peer, theirs, _, length = self.hop(stage, offset)
        return pltpu.make_async_remote_copy(
            src_ref=self.send.at[self.at(theirs, length), :],
            dst_ref=self.recv.at[self.slot(stage, offset), :],
            send_sem=self.sem(self.send_sem, stage, offset),
            recv_sem=self.sem(self.recv_sem, stage, offset),
            device_id={"dp": peer},
            device_id_type=pl.DeviceIdType.MESH,
        )

    def gather_copy(self, stage, offset):
        peer, _, ours, length = self.hop(stage, offset)
        return pltpu.make_async_remote_copy(
            src_ref=self.full.at[self.at(ours, length), :],
            dst_ref=self.full.at[self.at(ours, length), :],
            send_sem=self.sem(self.back_send, stage, offset),
            recv_sem=self.sem(self.back_recv, stage, offset),
            device_id={"dp": peer},
            device_id_type=pl.DeviceIdType.MESH,
        )

    def offsets(self, stage):
        return range(1, self.stages[stage][1])

    def reduce_start(self, stage):
        for offset in self.offsets(stage):
            _, theirs, _, length = self.hop(stage, offset)
            first = pl.multiple_of(self.base + theirs * self.rows, 16)
            copy_rows(self.acc, first, self.send, first, length * self.rows, lambda v: v.astype(BF16))
            self.reduce_copy(stage, offset).start()

    def reduce_finish(self, stage):
        for offset in self.offsets(stage):
            self.reduce_copy(stage, offset).wait_recv()
        _, _, ours, length = self.hop(stage, 0)
        shift = length * self.rows
        slot = self.base + (self.size - self.length[stage]) * self.rows
        add_rows(self.recv, slot, shift, self.stages[stage][1] - 1, self.acc,
                 pl.multiple_of(self.base + ours * self.rows, 16), shift)

    def gather_start(self, stage):
        for offset in self.offsets(stage):
            self.gather_copy(stage, offset).start()

    def gather_finish(self, stage):
        for offset in self.offsets(stage):
            self.gather_copy(stage, offset).wait_recv()

    def advance(self, step):
        count = len(self.stages)
        if 0 < step <= count:
            self.reduce_finish(step - 1)
        if step > count:
            self.gather_finish(2 * count - step)
        if step < count:
            self.reduce_start(step)
        if step == count:
            own = pl.multiple_of(self.base + self.mine * self.rows, 16)
            copy_rows(self.acc, own, self.full, own, self.rows, lambda v: v.astype(BF16))
        if count <= step < 2 * count:
            self.gather_start(2 * count - 1 - step)

    def close(self):
        for stage in range(len(self.stages)):
            for offset in self.offsets(stage):
                self.reduce_copy(stage, offset).wait_send()
                self.gather_copy(stage, offset).wait_send()


def row_block(length):
    return next(block for block in (128, 96, 64, 48, 32, 16) if length % block == 0)


def add_rows(source, first, shift, count, target, where, length):
    block = row_block(length)

    def body(t, carry):
        there = pl.ds(pl.multiple_of(where + t * block, 16), block)
        total = target[there, :]
        for n in range(count):
            here = pl.ds(pl.multiple_of(first + n * shift + t * block, 16), block)
            total = total + source[here, :].astype(F32)
        target[there, :] = total
        return carry

    lax.fori_loop(0, length // block, body, 0)


def copy_rows(source, first, target, where, length, change):
    block = row_block(length)

    def body(t, carry):
        here = pl.ds(pl.multiple_of(first + t * block, 16), block)
        there = pl.ds(pl.multiple_of(where + t * block, 16), block)
        target[there, :] = change(source[here, :])
        return carry

    lax.fori_loop(0, length // block, body, 0)


def images_in(ref, first, count):
    parts = [ref[micro, pl.ds(first, count), :, :].astype(F32) for micro in range(2)]
    return jnp.concatenate(parts, axis=1).reshape(4 * count, ref.shape[3])


def images_out(ref, first, count, value):
    value = value.reshape(count, 4, ref.shape[3])
    for micro in range(2):
        ref[micro, pl.ds(first, count)] = value[:, 2 * micro : 2 * micro + 2, :].astype(BF16)


def gelu_and_slope(pre):
    size = 1.0 + ERF_SHIFT * jnp.abs(pre)
    inv = pltpu.reciprocal(size, approx=True)
    inv = inv * (2.0 - size * inv)
    poly = (0.5 * ERF_POLY[-1]) * inv + 0.5 * ERF_POLY[-2]
    for value in reversed(ERF_POLY[:-2]):
        poly = poly * inv + 0.5 * value
    bell = jnp.exp2(pre * pre * (-0.5 * math.log2(math.e)))
    tail = poly * inv * bell
    cdf = jnp.where(pre >= 0.0, 1.0 - tail, tail)
    return (pre * cdf).astype(BF16), cdf + pre * bell * (1.0 / math.sqrt(2.0 * math.pi))


STEPS = (
    ((), (), (), ()),
    ((), (), (), (0,)),
    ((), (), (), ()),
    ((), (), (), (0, 1)),
    ((), (), (), ()),
    ((), (0,), (), (1, 2)),
)
LATER = ((), (0,), (1, 2), (), (), (1, 2), (), (), (2, 0, 1))


def mega_kernel(
    size,
    class_ref,
    extent_ref,
    rate_ref,
    freq_ref,
    coef_ref,
    skip_ref,
    b_in_ref,
    gain_ref,
    shift_ref,
    b_out_ref,
    scale_ref,
    w_in_hbm,
    w_out_hbm,
    x_hbm,
    cot_hbm,
    block_ref,
    dx_ref,
    full_ref,
    small_out,
    x_ref,
    cot_ref,
    w_in_ref,
    w_out_ref,
    pack_own,
    pack_oth,
    w_in_oth,
    w_out_oth,
    table_ref,
    skip_all,
    mask_ref,
    lag_ref,
    rowop_ref,
    colop_ref,
    u_ref,
    uh_ref,
    v_ref,
    mh_ref,
    mixed_ref,
    normed_ref,
    gmlp_ref,
    act_ref,
    gpre_ref,
    mlp_ref,
    gn_ref,
    stat_ref,
    gm_ref,
    row_acc,
    col_acc,
    db_ref,
    sums_ref,
    acc_ref,
    away_ref,
    landed_ref,
    send_ref,
    recv_ref,
    small_keep,
    small_land,
    small_recv,
    pair_send,
    pair_recv,
    red_send,
    red_recv,
    gat_send,
    gat_recv,
    sc_send,
    sc_recv,
    bc_send,
    bc_recv,
    in_sem,
):
    cells, channels = x_ref.shape[1], x_ref.shape[3]
    rows = 4 * cells
    own = pack_own.shape[1]
    half_hidden = w_in_ref.shape[1]
    me = lax.axis_index("dp")
    core = lax.axis_index("mp")
    partner = {"mp": 1 - core}

    barrier = pltpu.get_barrier_semaphore()
    pl.semaphore_signal(barrier, inc=1, device_id=partner, device_id_type=pl.DeviceIdType.MESH)
    for offset in range(1, size):
        pl.semaphore_signal(
            barrier,
            inc=1,
            device_id={"dp": lax.rem(me + offset, size)},
            device_id_type=pl.DeviceIdType.MESH,
        )
    reads = [
        pltpu.make_async_copy(source, target, in_sem.at[index])
        for index, (source, target) in enumerate(
            (
                (w_in_hbm, w_in_ref.at[pl.ds(0, channels), :]),
                (w_out_hbm, w_out_ref),
                (x_hbm, x_ref),
                (cot_hbm, cot_ref),
            )
        )
    ]
    for copy in reads:
        copy.start()

    def pair_copy(index, source, target):
        return pltpu.make_async_remote_copy(
            src_ref=source,
            dst_ref=target,
            send_sem=pair_send.at[index],
            recv_sem=pair_recv.at[index],
            device_id=partner,
            device_id_type=pl.DeviceIdType.MESH,
        )

    write_tables(extent_ref, rate_ref, freq_ref, coef_ref, pack_own)
    pack_own[108:109, :] = skip_ref[...].reshape(1, own)
    pack_own[109:PACK_ROWS, :] = jnp.zeros((PACK_ROWS - 109, own), F32)
    b_in = b_in_ref[...].reshape(1, half_hidden)
    b_high = b_in.astype(BF16).astype(F32)
    b_mid = (b_in - b_high).astype(BF16).astype(F32)
    b_low = b_in - b_high - b_mid
    line = lax.broadcasted_iota(jnp.int32, (16, half_hidden), 0)
    w_in_ref[channels : channels + 16, :] = jnp.where(
        line == 0, b_high, jnp.where(line == 1, b_mid, jnp.where(line == 2, b_low, 0.0))
    ).astype(BF16)
    rest = WIDE - channels - 16
    w_in_ref[channels + 16 : WIDE, :] = jnp.zeros((rest, half_hidden), BF16)
    w_in_oth[channels + 16 : WIDE, :] = jnp.zeros((rest, half_hidden), BF16)
    pl.semaphore_wait(barrier, size)
    pack_copy = pair_copy(0, pack_own, pack_oth)
    first_copy = pair_copy(
        1, w_in_ref.at[pl.ds(0, channels + 16), :], w_in_oth.at[pl.ds(0, channels + 16), :]
    )
    second_copy = pair_copy(2, w_out_ref, w_out_oth)
    pack_copy.start()
    reads[0].wait()
    first_copy.start()
    reads[1].wait()
    second_copy.start()

    build_masks(class_ref, mask_ref)
    block = 432
    scale = scale_ref[...].reshape(1, channels)
    normed_ref[:, channels:] = jnp.where(
        lax.broadcasted_iota(jnp.int32, (rows, WIDE - channels), 1) < 3, 1.0, 0.0
    ).astype(BF16)
    gn_ref[...] = jnp.zeros_like(gn_ref)
    reads[2].wait()
    reads[3].wait()

    def load(t, carry):
        at = pl.ds(pl.multiple_of(t * 48, 16), 48)
        u_ref[at, :] = images_in(x_ref, t * 12, 12)
        mask = jnp.tile(mask_ref[at, :], (1, channels // 128))
        gmlp_ref[at, :] = (images_in(cot_ref, t * 12, 12) * scale * mask).astype(BF16)
        return carry

    lax.fori_loop(0, rows // 48, load, 0)
    mirror_in(u_ref, mask_ref, uh_ref)

    pack_copy.wait_recv()
    first = core == 0
    low = jnp.where(first, pack_own[...], pack_oth[...])
    high = jnp.where(first, pack_oth[...], pack_own[...])
    table_ref[...] = jnp.concatenate([low, high], axis=1)
    skip_all[...] = table_ref[108:109, :]
    build_operators(class_ref, table_ref, lag_ref, rowop_ref, colop_ref)
    apply_rows(rowop_ref, uh_ref, v_ref)
    apply_cols(colop_ref, v_ref, mh_ref)
    mirror_out(mh_ref, mask_ref, mixed_ref, u_ref, skip_all)

    gain = gain_ref[...].reshape(1, channels)
    shift = shift_ref[...].reshape(1, channels)

    def norm(t, carry):
        at = pl.ds(pl.multiple_of(t * block, block), block)
        value = mixed_ref[at, :]
        mean = jnp.mean(value, axis=1, keepdims=True)
        centered = value - mean
        variance = jnp.mean(centered * centered, axis=1, keepdims=True)
        rstd = lax.rsqrt(variance + 1e-06)
        hat = centered * rstd
        mixed_ref[at, :] = hat
        stat_ref[at, :] = jnp.broadcast_to(rstd, (block, 128))
        normed_ref[at, :channels] = (hat * gain + shift).astype(BF16)
        return carry

    lax.fori_loop(0, rows // block, norm, 0)

    chunk = CHUNK
    tile_rows = 432
    first_copy.wait_recv()
    second_copy.wait_recv()

    group_rows = 2 * channels * chunk // 128
    per_chunk = chunk_rows(group_rows, size)
    stride = per_chunk * size
    groups = half_hidden // chunk
    rings = [
        Ring(group, size, per_chunk, acc_ref, send_ref, recv_ref, full_ref,
             (red_send, red_recv, gat_send, gat_recv))
        for group in range(groups)
    ]
    done = [0] * groups

    def advance(*which):
        last = 2 * len(stages_of(size))
        for group in which:
            if done[group] > last:
                continue
            rings[group].advance(done[group])
            done[group] += 1

    tiles = rows // tile_rows
    shares = []

    def feed(f, w_first_ref, w_second_ref, target_ref, target_base, db_row, steps, ready):
        cols = pl.ds(f * chunk, chunk)
        pre_cols = pl.ds((1 - db_row) * chunk, chunk)
        act_cols = pl.ds((1 - db_row) * half_hidden + f * chunk, chunk)

        def ahead(t):
            at = pl.ds(t * tile_rows, tile_rows)
            pre = jnp.dot(normed_ref[at, :], w_first_ref[:, cols], preferred_element_type=F32)
            g_act = lax.dot_general(
                gmlp_ref[at, :],
                w_second_ref[cols, :],
                (((1,), (1,)), ((), ())),
                preferred_element_type=F32,
            )
            return pre, g_act

        def outward(t, g_pre):
            at = pl.ds(t * tile_rows, tile_rows)
            gn_ref[at, :] += lax.dot_general(
                g_pre,
                w_first_ref[:channels, cols],
                (((1,), (1,)), ((), ())),
                preferred_element_type=F32,
            )

        late = f == groups - 1 and db_row == 0
        waiting = ahead(0)
        for t in range(tiles):
            pre, g_act = waiting
            if t + 1 < tiles:
                waiting = ahead(t + 1)
            at = pl.ds(t * tile_rows, tile_rows)
            act, slope = gelu_and_slope(pre)
            g_pre = (g_act * slope).astype(BF16)
            act_ref[at, act_cols] = act
            gpre_ref[at, pre_cols] = g_pre
            if not late:
                outward(t, g_pre)
            advance(*steps[t])
        d_first = lax.dot_general(
            normed_ref[:, : channels + 16],
            gpre_ref[:, pre_cols],
            (((0,), (0,)), ((), ())),
            preferred_element_type=F32,
        )
        for k in range(chunk // 128):
            at = pl.ds(target_base + k * channels, channels)
            target_ref[at, :] = d_first[:channels, k * 128 : (k + 1) * 128].astype(target_ref.dtype)
        db_ref[db_row : db_row + 1, cols] = d_first[channels : channels + 1, :]
        d_second = lax.dot_general(
            act_ref[:, act_cols], gmlp_ref[...], (((0,), (0,)), ((), ())), preferred_element_type=F32
        )
        base = target_base + channels * (chunk // 128)
        for k in range(channels // 128):
            at = pl.ds(base + k * chunk, chunk)
            target_ref[at, :] = d_second[:, k * 128 : (k + 1) * 128].astype(target_ref.dtype)
        shares.append(
            jnp.sum(d_second * w_second_ref[cols, :].astype(F32), axis=0, keepdims=True)
        )
        ready(f)
        advance(*steps[3])
        if late:
            for t in range(tiles):
                at = pl.ds(t * tile_rows, tile_rows)
                outward(t, gpre_ref[at, pre_cols])

    def grads_copy(group):
        at = pl.ds(group * group_rows, group_rows)
        return pair_copy(4 + group, away_ref.at[at, :], landed_ref.at[at, :])

    def join(group):
        grads_copy(group).wait_recv()
        add_rows(landed_ref, group * group_rows, 0, 1, acc_ref, group * stride, group_rows)
        if stride > group_rows:
            acc_ref[group * stride + group_rows : (group + 1) * stride, :] = jnp.zeros(
                (stride - group_rows, 128), F32
            )

    for group in range(groups):
        feed(group, w_in_oth, w_out_oth, away_ref, group * group_rows, 1, STEPS[2 * group],
             lambda g: grads_copy(g).start())
        feed(group, w_in_ref, w_out_ref, acc_ref, group * stride, 0, STEPS[2 * group + 1], join)

    def back(t, carry):
        d_gain, d_bias, d_b_out = carry
        at = pl.ds(pl.multiple_of(t * 48, 16), 48)
        d_b_out = d_b_out + jnp.sum(gmlp_ref[at, :].astype(F32), axis=0, keepdims=True)
        grad = gn_ref[at, :]
        hat = mixed_ref[at, :]
        d_gain = d_gain + jnp.sum(grad * hat, axis=0, keepdims=True)
        d_bias = d_bias + jnp.sum(grad, axis=0, keepdims=True)
        grad = grad * gain
        mean_g = jnp.mean(grad, axis=1, keepdims=True)
        mean_gh = jnp.mean(grad * hat, axis=1, keepdims=True)
        rstd = jnp.tile(stat_ref[at, :], (1, channels // 128))
        gm_ref[at, :] = (rstd * (grad - mean_g - hat * mean_gh)).astype(BF16).astype(F32)
        return d_gain, d_bias, d_b_out

    zero = jnp.zeros((1, channels), F32)
    d_gain, d_bias, d_b_out = lax.fori_loop(0, rows // 48, back, (zero, zero, zero))
    b_out = b_out_ref[...].reshape(1, channels)
    d_scale = (sum(shares) + b_out * d_b_out) / scale
    sums = (d_gain, d_bias, d_scale, d_b_out)
    mine_only = pl.ds(pl.multiple_of(core * 256, 128), 128)
    theirs_only = pl.ds(pl.multiple_of((1 - core) * 256, 128), 128)
    for index, value in enumerate(sums):
        for k in range(channels // 128):
            row = 115 + index * (channels // 128) + k
            tile = value[:, k * 128 : (k + 1) * 128]
            sums_ref[row : row + 1, mine_only] = tile
            sums_ref[row : row + 1, theirs_only] = tile
    for k in range(half_hidden // 128):
        at = slice(k * 128, (k + 1) * 128)
        sums_ref[109 + k : 110 + k, mine_only] = db_ref[0:1, at]
        sums_ref[109 + k : 110 + k, theirs_only] = db_ref[1:2, at]
    sums_ref[109:127, 128:256] = jnp.zeros((18, 128), F32)
    sums_ref[127:128, :] = zero
    advance(*LATER[0])
    gh_ref, xh_ref = mh_ref, row_acc
    mirror_in(gm_ref, mask_ref, gh_ref)
    col_correlate(gh_ref, v_ref, col_acc)
    advance(*LATER[1])
    apply_cols(colop_ref, gh_ref, xh_ref)
    advance(*LATER[2])
    row_correlate(xh_ref, uh_ref, v_ref)
    advance(*LATER[3])
    gather_lags(class_ref, v_ref, col_acc, sums_ref)

    def skip_sum(t, total):
        at = pl.ds(pl.multiple_of(t * block, block), block)
        return total + jnp.sum(gm_ref[at, :] * u_ref[at, :], axis=0, keepdims=True)

    sums_ref[108:109, :] = lax.fori_loop(0, rows // block, skip_sum, zero)
    mine_slice = pl.ds(pl.multiple_of(core * 128, 128), 256)
    theirs_slice = pl.ds(pl.multiple_of((1 - core) * 128, 128), 256)
    small_pair = pair_copy(3, sums_ref.at[:, theirs_slice], small_land)
    small_pair.start()
    apply_rows(rowop_ref, xh_ref, gh_ref)
    advance(*LATER[4])
    small_pair.wait_recv()
    small_keep[0:SUM_ROWS, :] = sums_ref[:, mine_slice] + small_land[...]
    if small_keep.shape[0] > SUM_ROWS:
        small_keep[SUM_ROWS:, :] = jnp.zeros((small_keep.shape[0] - SUM_ROWS, 256), F32)

    per = small_keep.shape[0] // size
    mine = pl.ds(pl.multiple_of(me * per, 8), per)

    def scatter_copy(offset):
        target = lax.rem(me + offset, size)
        return pltpu.make_async_remote_copy(
            src_ref=small_keep.at[pl.ds(pl.multiple_of(target * per, 8), per), :],
            dst_ref=small_recv.at[offset - 1],
            send_sem=sc_send.at[offset - 1],
            recv_sem=sc_recv.at[offset - 1],
            device_id={"dp": target},
            device_id_type=pl.DeviceIdType.MESH,
        )

    def spread_copy(offset):
        target = lax.rem(me + offset, size)
        return pltpu.make_async_remote_copy(
            src_ref=small_out.at[mine, :],
            dst_ref=small_out.at[mine, :],
            send_sem=bc_send.at[offset - 1],
            recv_sem=bc_recv.at[offset - 1],
            device_id={"dp": target},
            device_id_type=pl.DeviceIdType.MESH,
        )

    for offset in range(1, size):
        scatter_copy(offset).start()
    mirror_out(gh_ref, mask_ref, gn_ref, gm_ref, skip_all)
    advance(*LATER[5])
    for t in range(tiles):
        at = pl.ds(t * tile_rows, tile_rows)
        mlp_ref[at, :] = (
            jnp.dot(act_ref[at, :half_hidden], w_out_oth[...], preferred_element_type=F32)
            + jnp.dot(act_ref[at, half_hidden:], w_out_ref[...], preferred_element_type=F32)
            + b_out
        )
    advance(*LATER[6])

    def finish(t, carry):
        at = pl.ds(pl.multiple_of(t * 48, 16), 48)
        images_out(dx_ref, t * 12, 12, images_in(cot_ref, t * 12, 12) + gn_ref[at, :])
        branch = mlp_ref[at, :] * jnp.tile(mask_ref[at, :], (1, channels // 128))
        images_out(block_ref, t * 12, 12, u_ref[at, :] + scale * branch)
        return carry

    lax.fori_loop(0, rows // 48, finish, 0)
    advance(*LATER[7])
    total = small_keep[mine, :]
    for offset in range(1, size):
        scatter_copy(offset).wait_recv()
        total = total + small_recv[offset - 1]
    small_out[mine, :] = total
    for offset in range(1, size):
        spread_copy(offset).start()

    advance(*LATER[8])
    for _ in range(2 * len(stages_of(size)) + 1):
        advance(*range(groups))
    for offset in range(1, size):
        spread_copy(offset).wait_recv()
    for offset in range(1, size):
        scatter_copy(offset).wait_send()
        spread_copy(offset).wait_send()
    for group in range(groups):
        rings[group].close()
        grads_copy(group).wait_send()
    for copy in (pack_copy, first_copy, second_copy, small_pair):
        copy.wait_send()


def final_kernel(
    extent_ref, rate_ref, freq_ref, coef_ref, small_ref, block_hbm, dx_hbm, full_hbm,
    block_out, dx_out, rate_out, freq_out, coef_out, skip_out, gain_out, bias_out, dw_in_out,
    db_in_out, dw_out_out, b_out_out, scale_out,
    mine_ref, dw_in_ref, dw_out_ref, full_ref, block_ref, dx_ref, sems,
):
    channels, half_hidden = dw_in_ref.shape
    groups = half_hidden // CHUNK
    stride = full_ref.shape[0] // groups

    def moves(first, *pairs):
        return [
            pltpu.make_async_copy(source, target, sems.at[first + k])
            for k, (source, target) in enumerate(pairs)
        ]

    reads = moves(0, (full_hbm, full_ref), (block_hbm, block_ref), (dx_hbm, dx_ref))
    writes = moves(3, (dw_in_ref, dw_in_out), (dw_out_ref, dw_out_out), (block_ref, block_out), (dx_ref, dx_out))
    for copy in reads:
        copy.start()
    core = lax.axis_index("mp")
    own = mine_ref.shape[1]
    mine_ref[...] = jnp.where(core == 0, small_ref[0:112, :own], small_ref[0:112, 256 - own :])
    only = pl.ds(pl.multiple_of(core * 128, 128), 128)

    def line(first, count):
        return jnp.concatenate([small_ref[first + k : first + k + 1, only] for k in range(count)], axis=1)

    args = (extent_ref, rate_ref, freq_ref, coef_ref, mine_ref, rate_out, freq_out, coef_out)
    modes_grad(0, *args)
    reads[1].wait()
    writes[2].start()
    reads[2].wait()
    writes[3].start()
    reads[0].wait()
    for group in range(groups):
        base = group * stride
        for k in range(CHUNK // 128):
            at = group * CHUNK + k * 128
            dw_in_ref[:, at : at + 128] = full_ref[base : base + channels, :].astype(F32)
            base += channels
        for k in range(channels // 128):
            dw_out_ref[group * CHUNK : (group + 1) * CHUNK, k * 128 : (k + 1) * 128] = full_ref[
                base : base + CHUNK, :
            ].astype(F32)
            base += CHUNK
    writes[0].start()
    writes[1].start()
    modes_grad(1, *args)
    skip_out[...] = mine_ref[108:109, :].reshape(skip_out.shape)
    db_in_out[...] = line(109, db_in_out.shape[0] // 128).reshape(db_in_out.shape)
    for k, ref in enumerate((gain_out, bias_out, scale_out, b_out_out)):
        ref[...] = line(115 + 3 * k, 3).reshape(ref.shape)
    for copy in writes:
        copy.wait()


ANY = pl.BlockSpec(memory_space=pl.ANY)
VM = pl.BlockSpec(memory_space=pltpu.VMEM)
SM = pl.BlockSpec(memory_space=pltpu.SMEM)


def shape(dims, kind=F32):
    return jax.ShapeDtypeStruct(dims, kind)


def on_device(
    size,
    pixels,
    grid_class,
    extent,
    ssm_rate,
    ssm_freq,
    ssm_coef,
    skip_gain,
    norm_gain,
    norm_bias,
    w_in,
    b_in,
    w_out,
    b_out,
    layer_scale,
    cotangent,
):
    micro, count, channels, cells = pixels.shape
    rows = micro * count * cells
    own = ssm_rate.shape[1]
    modes = ssm_rate.shape[2]
    half_hidden = b_in.shape[0]
    x = pixels.transpose(0, 3, 1, 2)
    cot = cotangent.transpose(0, 3, 1, 2)
    rate = ssm_rate.transpose(0, 2, 1)
    freq = ssm_freq.transpose(0, 2, 1)
    coef = ssm_coef.transpose(0, 2, 1)
    field = (rows, channels)
    grad_rows = 2 * channels * half_hidden // 128
    groups = half_hidden // CHUNK
    all_rows = groups * chunk_rows(grad_rows // groups, size) * size
    stages = stages_of(size)
    hops = (groups, max(len(stages), 1), max([members - 1 for _, members in stages] + [1]))
    small_rows = max(128, 8 * size)
    peers = max(size - 1, 1)
    DMA = pltpu.SemaphoreType.DMA
    block_out, dx, full, small = pl.pallas_call(
        partial(mega_kernel, size),
        out_shape=(
            shape(x.shape, BF16),
            shape(x.shape, BF16),
            shape((all_rows, 128), BF16),
            shape((small_rows, 256)),
        ),
        in_specs=[SM] + [VM] * 10 + [ANY] * 4,
        out_specs=(VM,) * 4,
        scratch_shapes=[
            pltpu.VMEM(x.shape, BF16),
            pltpu.VMEM(x.shape, BF16),
            pltpu.VMEM((WIDE, half_hidden), BF16),
            pltpu.VMEM(w_out.shape, BF16),
            pltpu.VMEM((PACK_ROWS, own), F32),
            pltpu.VMEM((PACK_ROWS, own), F32),
            pltpu.VMEM((WIDE, half_hidden), BF16),
            pltpu.VMEM(w_out.shape, BF16),
            pltpu.VMEM((PACK_ROWS, channels), F32),
            pltpu.VMEM((1, channels), F32),
            pltpu.VMEM((rows, 128), F32),
            pltpu.VMEM((2 * GRID, 8, channels), F32),
            pltpu.VMEM((90, 8, channels), F32),
            pltpu.VMEM((45, 8, channels), F32),
            pltpu.VMEM(field, F32),
            pltpu.VMEM(field, F32),
            pltpu.VMEM(field, F32),
            pltpu.VMEM(field, F32),
            pltpu.VMEM(field, F32),
            pltpu.VMEM((rows, WIDE), BF16),
            pltpu.VMEM(field, BF16),
            pltpu.VMEM((rows, 2 * half_hidden), BF16),
            pltpu.VMEM((rows, 2 * CHUNK), BF16),
            pltpu.VMEM(field, F32),
            pltpu.VMEM(field, F32),
            pltpu.VMEM((rows, 128), F32),
            pltpu.VMEM(field, F32),
            pltpu.VMEM((162 * 8, channels), F32),
            pltpu.VMEM((81 * 8, channels), F32),
            pltpu.VMEM((2, half_hidden), F32),
            pltpu.VMEM((SUM_ROWS, channels), F32),
            pltpu.VMEM((all_rows, 128), F32),
            pltpu.VMEM((grad_rows, 128), BF16),
            pltpu.VMEM((grad_rows, 128), BF16),
            pltpu.VMEM((all_rows, 128), BF16),
            pltpu.VMEM((all_rows, 128), BF16),
            pltpu.VMEM((small_rows, 256), F32),
            pltpu.VMEM((SUM_ROWS, 256), F32),
            pltpu.VMEM((peers, small_rows // size, 256), F32),
            DMA((4 + groups,)),
            DMA((4 + groups,)),
            DMA(hops),
            DMA(hops),
            DMA(hops),
            DMA(hops),
            DMA((peers,)),
            DMA((peers,)),
            DMA((peers,)),
            DMA((peers,)),
            DMA((4,)),
        ],
        compiler_params=pltpu.CompilerParams(
            vmem_limit_bytes=VMEM_LIMIT, collective_id=0, has_side_effects=True
        ),
        name="block",
    )(
        grid_class,
        extent,
        rate,
        freq,
        coef,
        skip_gain,
        b_in,
        norm_gain,
        norm_bias,
        b_out,
        layer_scale,
        w_in,
        w_out,
        x,
        cot,
    )
    (
        block_out, dx, g_rate, g_freq, g_coef, g_skip, g_gain, g_bias, dw_in, db_in, dw_out, g_b_out, g_scale,
    ) = pl.pallas_call(
        final_kernel,
        out_shape=(
            shape(x.shape, BF16),
            shape(x.shape, BF16),
            shape((2, modes, own)),
            shape((2, modes, own)),
            shape((2, modes, own)),
            shape((own,)),
            shape((channels,)),
            shape((channels,)),
            shape(w_in.shape),
            shape((half_hidden,)),
            shape(w_out.shape),
            shape((channels,)),
            shape((channels,)),
        ),
        in_specs=[VM] * 5 + [ANY] * 3,
        out_specs=(ANY, ANY) + (VM,) * 6 + (ANY, VM, ANY, VM, VM),
        scratch_shapes=[
            pltpu.VMEM((112, own), F32),
            pltpu.VMEM(w_in.shape, F32),
            pltpu.VMEM(w_out.shape, F32),
            pltpu.VMEM(full.shape, BF16),
            pltpu.VMEM(x.shape, BF16),
            pltpu.VMEM(x.shape, BF16),
            DMA((7,)),
        ],
        compiler_params=pltpu.CompilerParams(vmem_limit_bytes=VMEM_LIMIT),
        name="final",
    )(extent, rate, freq, coef, small, block_out, dx, full)
    return (
        block_out.transpose(0, 2, 3, 1),
        dx.transpose(0, 2, 3, 1),
        g_rate.transpose(0, 2, 1),
        g_freq.transpose(0, 2, 1),
        g_coef.transpose(0, 2, 1),
        g_skip,
        g_gain,
        g_bias,
        dw_in,
        db_in,
        dw_out,
        g_b_out,
        g_scale,
    )


def solution(mesh):
    placed = (
        P(None, ("dp", "mp"), None, None),
        P(None, "dp"),
        P("mp"),
        P(None, "mp", None),
        P(None, "mp", None),
        P(None, "mp", None),
        P("mp"),
        P(),
        P(),
        P(None, "mp"),
        P("mp"),
        P("mp", None),
        P(),
        P(),
        P(None, ("dp", "mp"), None, None),
    )
    return jax.shard_map(
        partial(on_device, mesh.shape["dp"]),
        mesh=mesh,
        in_specs=placed,
        out_specs=(
            P(None, ("dp", "mp"), None, None),
            P(None, ("dp", "mp"), None, None),
            P(None, "mp", None),
            P(None, "mp", None),
            P(None, "mp", None),
            P("mp"),
            P(),
            P(),
            P(None, "mp"),
            P("mp"),
            P("mp", None),
            P(),
            P(),
        ),
        check_vma=False,
    )
```

```python
import math
from functools import partial

import jax
import jax.numpy as jnp
import numpy as np
from jax import lax
from jax.experimental import pallas as pl
from jax.experimental.pallas import tpu as pltpu
from jax.sharding import PartitionSpec as P

GRID = 18
HALF = 9
SIDES = (10, 14, 18)
LAGS = 3 * GRID
F32 = jnp.float32
BF16 = jnp.bfloat16

ERF_SHIFT = 0.35 / math.sqrt(2.0)
ERF_POLY = (
    0.19396706,
    0.23864529,
    -0.01708609,
    0.69839275,
    -0.6929918,
    0.77818103,
    -0.19910822,
)
CHUNK = 256
VMEM_LIMIT = 60 * 1024 * 1024


def small_sincos(angle):
    sq = angle * angle
    cos = 1.0 + sq * (
        -1 / 2 + sq * (1 / 24 + sq * (-1 / 720 + sq * (1 / 40320 + sq * (-1 / 3628800))))
    )
    sin = angle * (
        1.0
        + sq * (-1 / 6 + sq * (1 / 120 + sq * (-1 / 5040 + sq * (1 / 362880 + sq * (-1 / 39916800)))))
    )
    return sin, cos


def mode_step(rate, freq, side):
    decay = jnp.exp(rate * (-1.0 / side))
    sin, cos = small_sincos(freq * (1.0 / side))
    return decay * cos, decay * sin


PACK_ROWS = 112
SUM_ROWS = 128
WIDE = 512


def write_tables(extent_ref, rate_ref, freq_ref, coef_ref, out_ref):
    extent = extent_ref[...].reshape(1, extent_ref.shape[0])
    for axis in range(2):
        for cat, side in enumerate(SIDES):
            z_re, z_im = mode_step(rate_ref[axis], freq_ref[axis], side)
            w_re = coef_ref[axis]
            w_im = jnp.zeros_like(w_re)
            for lag in range(GRID):
                row = axis * LAGS + cat * GRID + lag
                if lag >= side:
                    out_ref[row : row + 1, :] = jnp.zeros((1, w_re.shape[1]), F32)
                    continue
                total = jnp.sum(w_re, axis=0, keepdims=True)
                out_ref[row : row + 1, :] = jnp.where(extent > lag, total, 0.0)
                if lag < side - 1:
                    w_re, w_im = w_re * z_re - w_im * z_im, w_re * z_im + w_im * z_re


def modes_grad(axis, extent_ref, rate_ref, freq_ref, coef_ref, dk_ref, rate_out, freq_out, coef_out):
    extent = extent_ref[...].reshape(1, extent_ref.shape[0])
    if True:
        coef = coef_ref[axis]
        g_rate = jnp.zeros_like(coef)
        g_freq = jnp.zeros_like(coef)
        g_coef = jnp.zeros_like(coef)
        for cat, side in enumerate(SIDES):
            z_re, z_im = mode_step(rate_ref[axis], freq_ref[axis], side)
            p_re = jnp.zeros_like(coef)
            p_im = jnp.zeros_like(coef)
            q_re = jnp.zeros_like(coef)
            q_im = jnp.zeros_like(coef)
            for lag in reversed(range(side)):
                row = axis * LAGS + cat * GRID + lag
                d = jnp.where(extent > lag, dk_ref[row : row + 1, :], 0.0)
                p_re, p_im = p_re * z_re - p_im * z_im + d, p_re * z_im + p_im * z_re
                q_re, q_im = q_re * z_re - q_im * z_im + float(lag) * d, q_re * z_im + q_im * z_re
            g_coef = g_coef + p_re
            g_rate = g_rate - (1.0 / side) * q_re
            g_freq = g_freq - (1.0 / side) * q_im
        coef_out[axis] = g_coef
        rate_out[axis] = g_rate * coef
        freq_out[axis] = g_freq * coef

def tri(a, b):
    low, high = min(a, b), max(a, b)
    return low * HALF - low * (low - 1) // 2 + (high - low)


def rows8(index):
    if isinstance(index, int):
        return pl.ds(index * 8, 8)
    return pl.ds(pl.multiple_of(index * 8, 8), 8)


def lanes(tile):
    if isinstance(tile, int):
        return pl.ds(tile * 128, 128)
    return pl.ds(pl.multiple_of(tile * 128, 128), 128)


def swap(value):
    return pltpu.roll(value, 4, 0)


def sublane_half():
    return lax.broadcasted_iota(jnp.int32, (8, 128), 0) < 4


def side_vreg(class_ref):
    mine = lax.axis_index("mp")
    image = lax.rem(lax.broadcasted_iota(jnp.int32, (8, 128), 0), 4)
    cls = jnp.zeros((8, 128), jnp.int32)
    own = class_ref.shape[1] // 2
    for micro in range(2):
        for img in range(2):
            cls = jnp.where(image == micro * 2 + img, class_ref[micro, mine * own + img], cls)
    return 10 + 4 * cls


def build_masks(class_ref, mask_ref):
    side = side_vreg(class_ref)
    offset = jnp.where(sublane_half(), 0, 1)

    def row(i, carry):
        for pair in range(HALF):
            ok = (i < side) & (2 * pair + offset < side)
            mask_ref[rows8(i * HALF + pair), :] = jnp.where(ok, 1.0, 0.0).astype(F32)
        return carry

    lax.fori_loop(0, GRID, row, 0)


def build_operators(class_ref, table_ref, lag_ref, rowop_ref, colop_ref):
    side = side_vreg(class_ref)
    sign = jnp.where(sublane_half(), 1.0, -1.0).astype(F32)
    tiles = table_ref.shape[1] // 128

    def tile_body(tile, carry):
        at = lanes(tile)
        for axis in range(2):
            for lag in range(GRID):
                by_side = [
                    jnp.broadcast_to(table_ref[axis * LAGS + cat * GRID + lag : axis * LAGS + cat * GRID + lag + 1, at], (8, 128))
                    for cat in range(3)
                ]
                lag_ref[axis * GRID + lag, :, at] = 0.5 * jnp.where(
                    side == 10, by_side[0], jnp.where(side == 14, by_side[1], by_side[2])
                )
        for a in range(HALF):
            for b in range(a, HALF):
                near = lag_ref[b - a, :, at]
                far = lag_ref[GRID - 1 - a - b, :, at]
                rowop_ref[tri(a, b), :, at] = near + far
                rowop_ref[45 + tri(a, b), :, at] = near - far
                near = lag_ref[GRID + b - a, :, at]
                far = lag_ref[GRID + GRID - 1 - a - b, :, at]
                colop_ref[tri(a, b), :, at] = near + sign * far
        return carry

    lax.fori_loop(0, tiles, tile_body, 0)


def mirror_in(source_ref, mask_ref, out_ref):
    half = sublane_half()
    sign = jnp.where(half, 1.0, -1.0).astype(F32)
    tiles = source_ref.shape[1] // 128

    def body(i, carry):
        for tile in range(tiles):
            at = lanes(tile)

            def mirrored(row, pair):
                near = source_ref[rows8(row * HALF + pair), at] * mask_ref[rows8(row * HALF + pair), :]
                if pair == 4:
                    return swap(near) + sign * near, None
                other = row * HALF + 8 - pair
                far = source_ref[rows8(other), at] * mask_ref[rows8(other), :]
                even = jnp.where(half, near, far)
                odd = jnp.where(half, far, near)
                return swap(even) + sign * even, odd + sign * swap(odd)

            for pair in range(5):
                top = mirrored(i, pair)
                bottom = mirrored(GRID - 1 - i, pair)
                for step in range(2 if pair < 4 else 1):
                    where = i * HALF + 2 * pair + step
                    out_ref[rows8(where), at] = top[step] + bottom[step]
                    out_ref[rows8(81 + where), at] = top[step] - bottom[step]
        return carry

    lax.fori_loop(0, HALF, body, 0)


def mirror_out(source_ref, mask_ref, out_ref, extra_ref, gain_ref):
    half = sublane_half()
    sign = jnp.where(half, 1.0, -1.0).astype(F32)
    tiles = source_ref.shape[1] // 128

    def body(i, carry):
        for tile in range(tiles):
            at = lanes(tile)
            gain = jnp.broadcast_to(gain_ref[:, at], (8, 128))

            def finish(index, value):
                value = value * mask_ref[rows8(index), :] + gain * extra_ref[rows8(index), at]
                out_ref[rows8(index), at] = value.astype(BF16).astype(F32)

            for pair in range(5):
                both = []
                for step in range(2 if pair < 4 else 1):
                    where = i * HALF + 2 * pair + step
                    plus = source_ref[rows8(where), at]
                    minus = source_ref[rows8(81 + where), at]
                    top, bottom = plus + minus, plus - minus
                    both.append(
                        (swap(top) + sign * top, swap(bottom) + sign * bottom)
                        if step == 0
                        else (top - sign * swap(top), bottom - sign * swap(bottom))
                    )
                for part, row in ((0, i), (1, GRID - 1 - i)):
                    if pair == 4:
                        finish(row * HALF + 4, both[0][part])
                        continue
                    if True:
                        even, odd = both[0][part], both[1][part]
                        finish(row * HALF + pair, jnp.where(half, even, odd))
                        finish(row * HALF + 8 - pair, jnp.where(half, odd, even))
        return carry

    lax.fori_loop(0, HALF, body, 0)


def apply_rows(op_ref, source_ref, out_ref):
    tiles = source_ref.shape[1] // 128

    def body(j, carry):
        for tile in range(tiles):
            at = lanes(tile)
            for rho in range(2):
                values = [source_ref[rows8(rho * 81 + p * HALF + j), at] for p in range(HALF)]
                for i in range(HALF):
                    total = None
                    for p in range(HALF):
                        term = op_ref[rho * 45 + tri(i, p), :, at] * values[p]
                        total = term if total is None else total + term
                    out_ref[rows8(rho * 81 + i * HALF + j), at] = total
        return carry

    lax.fori_loop(0, HALF, body, 0)


def apply_cols(op_ref, source_ref, out_ref):
    tiles = source_ref.shape[1] // 128

    def body(i, carry):
        for tile in range(tiles):
            at = lanes(tile)
            values = [source_ref[rows8(i * HALF + q), at] for q in range(HALF)]
            for j in range(HALF):
                total = None
                for q in range(HALF):
                    term = op_ref[tri(j, q), :, at] * values[q]
                    total = term if total is None else total + term
                out_ref[rows8(i * HALF + j), at] = total
        return carry

    lax.fori_loop(0, 2 * HALF, body, 0)


def row_correlate(left_ref, right_ref, acc_ref, cut=3):
    for tile in range(left_ref.shape[1] // 128):
        for rho in range(2):

            def body(step, carry, at=lanes(tile), rho=rho):
                first = step * cut
                sums = [[None] * HALF for _ in range(cut)]
                for j in range(HALF):
                    left = [
                        left_ref[rows8(rho * 81 + (first + k) * HALF + j), at] for k in range(cut)
                    ]
                    for p in range(HALF):
                        right = right_ref[rows8(rho * 81 + p * HALF + j), at]
                        for k in range(cut):
                            term = left[k] * right
                            sums[k][p] = term if sums[k][p] is None else sums[k][p] + term
                for k in range(cut):
                    for p in range(HALF):
                        acc_ref[rows8(rho * 81 + (first + k) * HALF + p), at] = sums[k][p]
                return carry

            lax.fori_loop(0, HALF // cut, body, 0)


def col_correlate(left_ref, right_ref, acc_ref, cut=3):
    for tile in range(left_ref.shape[1] // 128):

        def body(step, carry, at=lanes(tile)):
            first = step * cut
            sums = [[None] * HALF for _ in range(cut)]
            for i in range(2 * HALF):
                left = [left_ref[rows8(i * HALF + first + k), at] for k in range(cut)]
                for q in range(HALF):
                    right = right_ref[rows8(i * HALF + q), at]
                    for k in range(cut):
                        term = left[k] * right
                        sums[k][q] = term if sums[k][q] is None else sums[k][q] + term
            for k in range(cut):
                for q in range(HALF):
                    acc_ref[rows8((first + k) * HALF + q), at] = sums[k][q]
            return carry

        lax.fori_loop(0, HALF // cut, body, 0)


def gather_lags(class_ref, row_acc, col_acc, dk_ref):
    side = side_vreg(class_ref)
    sign = jnp.where(sublane_half(), 1.0, -1.0).astype(F32)
    tiles = row_acc.shape[1] // 128

    def body(tile, carry):
        at = lanes(tile)
        for axis in range(2):
            near = [None] * HALF
            far = [None] * GRID
            for a in range(HALF):
                for b in range(HALF):
                    if axis == 0:
                        plus = row_acc[rows8(a * HALF + b), at]
                        minus = row_acc[rows8(81 + a * HALF + b), at]
                        direct, cross = plus + minus, plus - minus
                    else:
                        direct = col_acc[rows8(a * HALF + b), at]
                        cross = sign * direct
                    d, s = abs(a - b), GRID - 1 - a - b
                    near[d] = direct if near[d] is None else near[d] + direct
                    far[s] = cross if far[s] is None else far[s] + cross
            for lag in range(GRID):
                total = None
                for part in ([near[lag]] if lag < HALF else []) + ([far[lag]] if lag else []):
                    total = part if total is None else total + part
                total = 0.5 * total
                for cat, length in enumerate(SIDES):
                    row = axis * LAGS + cat * GRID + lag
                    value = jnp.where(side == length, total, 0.0)
                    dk_ref[row : row + 1, at] = jnp.sum(value, axis=0, keepdims=True)
        return carry

    lax.fori_loop(0, tiles, body, 0)


def stages_of(size):
    bits = size.bit_length() - 1
    stages, stride = [], 1
    while bits:
        take = bits if bits <= 3 and bits != 2 else 2
        stages.append((stride, 1 << take))
        stride <<= take
        bits -= take
    return stages


def chunk_rows(rows, size):
    return -(-rows // (16 * size)) * 16


class Ring:
    def __init__(self, group, size, rows, acc, send, recv, full, sems):
        self.group, self.size, self.rows = group, size, rows
        self.acc, self.send, self.recv, self.full = acc, send, recv, full
        self.send_sem, self.recv_sem, self.back_send, self.back_recv = sems
        self.stages = stages_of(size)
        self.me = lax.axis_index("dp")
        self.base = group * size * rows
        self.digit, self.start, self.length = [], [], []
        start, length = 0, size
        for stride, members in self.stages:
            digit = lax.rem(self.me // stride, members)
            self.digit.append(digit)
            self.start.append(start)
            self.length.append(length)
            length //= members
            start = start + digit * length
        self.mine = start

    def at(self, chunk, count):
        return pl.ds(pl.multiple_of(self.base + chunk * self.rows, 16), count * self.rows)

    def hop(self, stage, offset):
        stride, members = self.stages[stage]
        digit = self.digit[stage]
        other = lax.rem(digit + offset, members)
        length = self.length[stage] // members
        start = self.start[stage]
        return self.me + (other - digit) * stride, start + other * length, start + digit * length, length

    def slot(self, stage, offset):
        length = self.length[stage] // self.stages[stage][1]
        return self.at(self.size - self.length[stage] + (offset - 1) * length, length)

    def sem(self, sems, stage, offset):
        return sems.at[self.group, stage, offset - 1]

    def reduce_copy(self, stage, offset):
        peer, theirs, _, length = self.hop(stage, offset)
        return pltpu.make_async_remote_copy(
            src_ref=self.send.at[self.at(theirs, length), :],
            dst_ref=self.recv.at[self.slot(stage, offset), :],
            send_sem=self.sem(self.send_sem, stage, offset),
            recv_sem=self.sem(self.recv_sem, stage, offset),
            device_id={"dp": peer},
            device_id_type=pl.DeviceIdType.MESH,
        )

    def gather_copy(self, stage, offset):
        peer, _, ours, length = self.hop(stage, offset)
        return pltpu.make_async_remote_copy(
            src_ref=self.full.at[self.at(ours, length), :],
            dst_ref=self.full.at[self.at(ours, length), :],
            send_sem=self.sem(self.back_send, stage, offset),
            recv_sem=self.sem(self.back_recv, stage, offset),
            device_id={"dp": peer},
            device_id_type=pl.DeviceIdType.MESH,
        )

    def offsets(self, stage):
        return range(1, self.stages[stage][1])

    def reduce_start(self, stage):
        for offset in self.offsets(stage):
            _, theirs, _, length = self.hop(stage, offset)
            first = pl.multiple_of(self.base + theirs * self.rows, 16)
            copy_rows(self.acc, first, self.send, first, length * self.rows, lambda v: v.astype(BF16))
            self.reduce_copy(stage, offset).start()

    def reduce_finish(self, stage):
        for offset in self.offsets(stage):
            self.reduce_copy(stage, offset).wait_recv()
        _, _, ours, length = self.hop(stage, 0)
        shift = length * self.rows
        slot = self.base + (self.size - self.length[stage]) * self.rows
        add_rows(self.recv, slot, shift, self.stages[stage][1] - 1, self.acc,
                 pl.multiple_of(self.base + ours * self.rows, 16), shift)

    def gather_start(self, stage):
        for offset in self.offsets(stage):
            self.gather_copy(stage, offset).start()

    def gather_finish(self, stage):
        for offset in self.offsets(stage):
            self.gather_copy(stage, offset).wait_recv()

    def advance(self, step):
        count = len(self.stages)
        if 0 < step <= count:
            self.reduce_finish(step - 1)
        if step > count:
            self.gather_finish(2 * count - step)
        if step < count:
            self.reduce_start(step)
        if step == count:
            own = pl.multiple_of(self.base + self.mine * self.rows, 16)
            copy_rows(self.acc, own, self.full, own, self.rows, lambda v: v.astype(BF16))
        if count <= step < 2 * count:
            self.gather_start(2 * count - 1 - step)

    def close(self):
        for stage in range(len(self.stages)):
            for offset in self.offsets(stage):
                self.reduce_copy(stage, offset).wait_send()
                self.gather_copy(stage, offset).wait_send()


def row_block(length):
    return next(block for block in (128, 96, 64, 48, 32, 16) if length % block == 0)


def add_rows(source, first, shift, count, target, where, length):
    block = row_block(length)

    def body(t, carry):
        there = pl.ds(pl.multiple_of(where + t * block, 16), block)
        total = target[there, :]
        for n in range(count):
            here = pl.ds(pl.multiple_of(first + n * shift + t * block, 16), block)
            total = total + source[here, :].astype(F32)
        target[there, :] = total
        return carry

    lax.fori_loop(0, length // block, body, 0)


def copy_rows(source, first, target, where, length, change):
    block = row_block(length)

    def body(t, carry):
        here = pl.ds(pl.multiple_of(first + t * block, 16), block)
        there = pl.ds(pl.multiple_of(where + t * block, 16), block)
        target[there, :] = change(source[here, :])
        return carry

    lax.fori_loop(0, length // block, body, 0)


def images_in(ref, first, count):
    parts = [ref[micro, pl.ds(first, count), :, :].astype(F32) for micro in range(2)]
    return jnp.concatenate(parts, axis=1).reshape(4 * count, ref.shape[3])


def images_out(ref, first, count, value):
    value = value.reshape(count, 4, ref.shape[3])
    for micro in range(2):
        ref[micro, pl.ds(first, count)] = value[:, 2 * micro : 2 * micro + 2, :].astype(BF16)


def gelu_and_slope(pre):
    size = 1.0 + ERF_SHIFT * jnp.abs(pre)
    inv = pltpu.reciprocal(size, approx=True)
    inv = inv * (2.0 - size * inv)
    poly = (0.5 * ERF_POLY[-1]) * inv + 0.5 * ERF_POLY[-2]
    for value in reversed(ERF_POLY[:-2]):
        poly = poly * inv + 0.5 * value
    bell = jnp.exp2(pre * pre * (-0.5 * math.log2(math.e)))
    tail = poly * inv * bell
    cdf = jnp.where(pre >= 0.0, 1.0 - tail, tail)
    return (pre * cdf).astype(BF16), cdf + pre * bell * (1.0 / math.sqrt(2.0 * math.pi))


STEPS = (
    ((), (), (), ()),
    ((), (), (), (0,)),
    ((), (), (), ()),
    ((), (), (), (0, 1)),
    ((), (), (), ()),
    ((), (0,), (), (1, 2)),
)
LATER = ((), (0,), (1, 2), (), (), (1, 2), (), (), (2, 0, 1))


def mega_kernel(
    size,
    class_ref,
    extent_ref,
    rate_ref,
    freq_ref,
    coef_ref,
    skip_ref,
    b_in_ref,
    gain_ref,
    shift_ref,
    b_out_ref,
    scale_ref,
    w_in_hbm,
    w_out_hbm,
    x_hbm,
    cot_hbm,
    block_ref,
    dx_ref,
    full_ref,
    small_out,
    x_ref,
    cot_ref,
    w_in_ref,
    w_out_ref,
    pack_own,
    pack_oth,
    w_in_oth,
    w_out_oth,
    table_ref,
    skip_all,
    mask_ref,
    lag_ref,
    rowop_ref,
    colop_ref,
    u_ref,
    uh_ref,
    v_ref,
    mh_ref,
    mixed_ref,
    normed_ref,
    gmlp_ref,
    act_ref,
    gpre_ref,
    mlp_ref,
    gn_ref,
    stat_ref,
    gm_ref,
    row_acc,
    col_acc,
    db_ref,
    sums_ref,
    acc_ref,
    away_ref,
    landed_ref,
    send_ref,
    recv_ref,
    small_keep,
    small_land,
    small_recv,
    pair_send,
    pair_recv,
    red_send,
    red_recv,
    gat_send,
    gat_recv,
    sc_send,
    sc_recv,
    bc_send,
    bc_recv,
    in_sem,
):
    cells, channels = x_ref.shape[1], x_ref.shape[3]
    rows = 4 * cells
    own = pack_own.shape[1]
    half_hidden = w_in_ref.shape[1]
    me = lax.axis_index("dp")
    core = lax.axis_index("mp")
    partner = {"mp": 1 - core}

    barrier = pltpu.get_barrier_semaphore()
    pl.semaphore_signal(barrier, inc=1, device_id=partner, device_id_type=pl.DeviceIdType.MESH)
    for offset in range(1, size):
        pl.semaphore_signal(
            barrier,
            inc=1,
            device_id={"dp": lax.rem(me + offset, size)},
            device_id_type=pl.DeviceIdType.MESH,
        )
    reads = [
        pltpu.make_async_copy(source, target, in_sem.at[index])
        for index, (source, target) in enumerate(
            (
                (w_in_hbm, w_in_ref.at[pl.ds(0, channels), :]),
                (w_out_hbm, w_out_ref),
                (x_hbm, x_ref),
                (cot_hbm, cot_ref),
            )
        )
    ]
    for copy in reads:
        copy.start()

    def pair_copy(index, source, target):
        return pltpu.make_async_remote_copy(
            src_ref=source,
            dst_ref=target,
            send_sem=pair_send.at[index],
            recv_sem=pair_recv.at[index],
            device_id=partner,
            device_id_type=pl.DeviceIdType.MESH,
        )

    write_tables(extent_ref, rate_ref, freq_ref, coef_ref, pack_own)
    pack_own[108:109, :] = skip_ref[...].reshape(1, own)
    pack_own[109:PACK_ROWS, :] = jnp.zeros((PACK_ROWS - 109, own), F32)
    b_in = b_in_ref[...].reshape(1, half_hidden)
    b_high = b_in.astype(BF16).astype(F32)
    b_mid = (b_in - b_high).astype(BF16).astype(F32)
    b_low = b_in - b_high - b_mid
    line = lax.broadcasted_iota(jnp.int32, (16, half_hidden), 0)
    w_in_ref[channels : channels + 16, :] = jnp.where(
        line == 0, b_high, jnp.where(line == 1, b_mid, jnp.where(line == 2, b_low, 0.0))
    ).astype(BF16)
    rest = WIDE - channels - 16
    w_in_ref[channels + 16 : WIDE, :] = jnp.zeros((rest, half_hidden), BF16)
    w_in_oth[channels + 16 : WIDE, :] = jnp.zeros((rest, half_hidden), BF16)
    pl.semaphore_wait(barrier, size)
    pack_copy = pair_copy(0, pack_own, pack_oth)
    first_copy = pair_copy(
        1, w_in_ref.at[pl.ds(0, channels + 16), :], w_in_oth.at[pl.ds(0, channels + 16), :]
    )
    second_copy = pair_copy(2, w_out_ref, w_out_oth)
    pack_copy.start()
    reads[0].wait()
    first_copy.start()
    reads[1].wait()
    second_copy.start()

    build_masks(class_ref, mask_ref)
    block = 432
    scale = scale_ref[...].reshape(1, channels)
    normed_ref[:, channels:] = jnp.where(
        lax.broadcasted_iota(jnp.int32, (rows, WIDE - channels), 1) < 3, 1.0, 0.0
    ).astype(BF16)
    gn_ref[...] = jnp.zeros_like(gn_ref)
    reads[2].wait()
    reads[3].wait()

    def load(t, carry):
        at = pl.ds(pl.multiple_of(t * 144, 16), 144)
        u_ref[at, :] = images_in(x_ref, t * 36, 36)
        mask = jnp.tile(mask_ref[at, :], (1, channels // 128))
        gmlp_ref[at, :] = (images_in(cot_ref, t * 36, 36) * scale * mask).astype(BF16)
        return carry

    lax.fori_loop(0, rows // 144, load, 0)
    mirror_in(u_ref, mask_ref, uh_ref)

    pack_copy.wait_recv()
    first = core == 0
    low = jnp.where(first, pack_own[...], pack_oth[...])
    high = jnp.where(first, pack_oth[...], pack_own[...])
    table_ref[...] = jnp.concatenate([low, high], axis=1)
    skip_all[...] = table_ref[108:109, :]
    build_operators(class_ref, table_ref, lag_ref, rowop_ref, colop_ref)
    apply_rows(rowop_ref, uh_ref, v_ref)
    apply_cols(colop_ref, v_ref, mh_ref)
    mirror_out(mh_ref, mask_ref, mixed_ref, u_ref, skip_all)

    gain = gain_ref[...].reshape(1, channels)
    shift = shift_ref[...].reshape(1, channels)

    def norm(t, carry):
        at = pl.ds(pl.multiple_of(t * block, block), block)
        value = mixed_ref[at, :]
        mean = jnp.mean(value, axis=1, keepdims=True)
        centered = value - mean
        variance = jnp.mean(centered * centered, axis=1, keepdims=True)
        rstd = lax.rsqrt(variance + 1e-06)
        hat = centered * rstd
        mixed_ref[at, :] = hat
        stat_ref[at, :] = jnp.broadcast_to(rstd, (block, 128))
        normed_ref[at, :channels] = (hat * gain + shift).astype(BF16)
        return carry

    lax.fori_loop(0, rows // block, norm, 0)

    chunk = CHUNK
    tile_rows = 432
    first_copy.wait_recv()
    second_copy.wait_recv()

    group_rows = 2 * channels * chunk // 128
    per_chunk = chunk_rows(group_rows, size)
    stride = per_chunk * size
    groups = half_hidden // chunk
    rings = [
        Ring(group, size, per_chunk, acc_ref, send_ref, recv_ref, full_ref,
             (red_send, red_recv, gat_send, gat_recv))
        for group in range(groups)
    ]
    done = [0] * groups

    def advance(*which):
        last = 2 * len(stages_of(size))
        for group in which:
            if done[group] > last:
                continue
            rings[group].advance(done[group])
            done[group] += 1

    tiles = rows // tile_rows
    shares = []

    def feed(f, w_first_ref, w_second_ref, target_ref, target_base, db_row, steps, ready):
        cols = pl.ds(f * chunk, chunk)
        pre_cols = pl.ds((1 - db_row) * chunk, chunk)
        act_cols = pl.ds((1 - db_row) * half_hidden + f * chunk, chunk)

        def ahead(t):
            at = pl.ds(t * tile_rows, tile_rows)
            pre = jnp.dot(normed_ref[at, :], w_first_ref[:, cols], preferred_element_type=F32)
            g_act = lax.dot_general(
                gmlp_ref[at, :],
                w_second_ref[cols, :],
                (((1,), (1,)), ((), ())),
                preferred_element_type=F32,
            )
            return pre, g_act

        def outward(t, g_pre):
            at = pl.ds(t * tile_rows, tile_rows)
            gn_ref[at, :] += lax.dot_general(
                g_pre,
                w_first_ref[:channels, cols],
                (((1,), (1,)), ((), ())),
                preferred_element_type=F32,
            )

        late = f == groups - 1 and db_row == 0
        waiting = ahead(0)
        for t in range(tiles):
            pre, g_act = waiting
            if t + 1 < tiles:
                waiting = ahead(t + 1)
            at = pl.ds(t * tile_rows, tile_rows)
            act, slope = gelu_and_slope(pre)
            g_pre = (g_act * slope).astype(BF16)
            act_ref[at, act_cols] = act
            gpre_ref[at, pre_cols] = g_pre
            if not late:
                outward(t, g_pre)
            advance(*steps[t])
        d_first = lax.dot_general(
            normed_ref[:, : channels + 16],
            gpre_ref[:, pre_cols],
            (((0,), (0,)), ((), ())),
            preferred_element_type=F32,
        )
        for k in range(chunk // 128):
            at = pl.ds(target_base + k * channels, channels)
            target_ref[at, :] = d_first[:channels, k * 128 : (k + 1) * 128].astype(target_ref.dtype)
        db_ref[db_row : db_row + 1, cols] = d_first[channels : channels + 1, :]
        d_second = lax.dot_general(
            act_ref[:, act_cols], gmlp_ref[...], (((0,), (0,)), ((), ())), preferred_element_type=F32
        )
        base = target_base + channels * (chunk // 128)
        for k in range(channels // 128):
            at = pl.ds(base + k * chunk, chunk)
            target_ref[at, :] = d_second[:, k * 128 : (k + 1) * 128].astype(target_ref.dtype)
        shares.append(
            jnp.sum(d_second * w_second_ref[cols, :].astype(F32), axis=0, keepdims=True)
        )
        ready(f)
        advance(*steps[3])
        if late:
            for t in range(tiles):
                at = pl.ds(t * tile_rows, tile_rows)
                outward(t, gpre_ref[at, pre_cols])

    def grads_copy(group):
        at = pl.ds(group * group_rows, group_rows)
        return pair_copy(4 + group, away_ref.at[at, :], landed_ref.at[at, :])

    def join(group):
        grads_copy(group).wait_recv()
        add_rows(landed_ref, group * group_rows, 0, 1, acc_ref, group * stride, group_rows)
        if stride > group_rows:
            acc_ref[group * stride + group_rows : (group + 1) * stride, :] = jnp.zeros(
                (stride - group_rows, 128), F32
            )

    for group in range(groups):
        feed(group, w_in_oth, w_out_oth, away_ref, group * group_rows, 1, STEPS[2 * group],
             lambda g: grads_copy(g).start())
        feed(group, w_in_ref, w_out_ref, acc_ref, group * stride, 0, STEPS[2 * group + 1], join)

    def back(t, carry):
        d_gain, d_bias, d_b_out = carry
        at = pl.ds(pl.multiple_of(t * 144, 16), 144)
        d_b_out = d_b_out + jnp.sum(gmlp_ref[at, :].astype(F32), axis=0, keepdims=True)
        grad = gn_ref[at, :]
        hat = mixed_ref[at, :]
        d_gain = d_gain + jnp.sum(grad * hat, axis=0, keepdims=True)
        d_bias = d_bias + jnp.sum(grad, axis=0, keepdims=True)
        grad = grad * gain
        mean_g = jnp.mean(grad, axis=1, keepdims=True)
        mean_gh = jnp.mean(grad * hat, axis=1, keepdims=True)
        rstd = jnp.tile(stat_ref[at, :], (1, channels // 128))
        gm_ref[at, :] = (rstd * (grad - mean_g - hat * mean_gh)).astype(BF16).astype(F32)
        return d_gain, d_bias, d_b_out

    zero = jnp.zeros((1, channels), F32)
    d_gain, d_bias, d_b_out = lax.fori_loop(0, rows // 144, back, (zero, zero, zero))
    b_out = b_out_ref[...].reshape(1, channels)
    d_scale = (sum(shares) + b_out * d_b_out) / scale
    sums = (d_gain, d_bias, d_scale, d_b_out)
    mine_only = pl.ds(pl.multiple_of(core * 256, 128), 128)
    theirs_only = pl.ds(pl.multiple_of((1 - core) * 256, 128), 128)
    for index, value in enumerate(sums):
        for k in range(channels // 128):
            row = 115 + index * (channels // 128) + k
            tile = value[:, k * 128 : (k + 1) * 128]
            sums_ref[row : row + 1, mine_only] = tile
            sums_ref[row : row + 1, theirs_only] = tile
    for k in range(half_hidden // 128):
        at = slice(k * 128, (k + 1) * 128)
        sums_ref[109 + k : 110 + k, mine_only] = db_ref[0:1, at]
        sums_ref[109 + k : 110 + k, theirs_only] = db_ref[1:2, at]
    sums_ref[109:127, 128:256] = jnp.zeros((18, 128), F32)
    sums_ref[127:128, :] = zero
    advance(*LATER[0])
    gh_ref, xh_ref = mh_ref, row_acc
    mirror_in(gm_ref, mask_ref, gh_ref)
    col_correlate(gh_ref, v_ref, col_acc)
    advance(*LATER[1])
    apply_cols(colop_ref, gh_ref, xh_ref)
    advance(*LATER[2])
    row_correlate(xh_ref, uh_ref, v_ref)
    advance(*LATER[3])
    gather_lags(class_ref, v_ref, col_acc, sums_ref)

    def skip_sum(t, total):
        at = pl.ds(pl.multiple_of(t * block, block), block)
        return total + jnp.sum(gm_ref[at, :] * u_ref[at, :], axis=0, keepdims=True)

    sums_ref[108:109, :] = lax.fori_loop(0, rows // block, skip_sum, zero)
    mine_slice = pl.ds(pl.multiple_of(core * 128, 128), 256)
    theirs_slice = pl.ds(pl.multiple_of((1 - core) * 128, 128), 256)
    small_pair = pair_copy(3, sums_ref.at[:, theirs_slice], small_land)
    small_pair.start()
    apply_rows(rowop_ref, xh_ref, gh_ref)
    advance(*LATER[4])
    small_pair.wait_recv()
    small_keep[0:SUM_ROWS, :] = sums_ref[:, mine_slice] + small_land[...]
    if small_keep.shape[0] > SUM_ROWS:
        small_keep[SUM_ROWS:, :] = jnp.zeros((small_keep.shape[0] - SUM_ROWS, 256), F32)

    per = small_keep.shape[0] // size
    mine = pl.ds(pl.multiple_of(me * per, 8), per)

    def scatter_copy(offset):
        target = lax.rem(me + offset, size)
        return pltpu.make_async_remote_copy(
            src_ref=small_keep.at[pl.ds(pl.multiple_of(target * per, 8), per), :],
            dst_ref=small_recv.at[offset - 1],
            send_sem=sc_send.at[offset - 1],
            recv_sem=sc_recv.at[offset - 1],
            device_id={"dp": target},
            device_id_type=pl.DeviceIdType.MESH,
        )

    def spread_copy(offset):
        target = lax.rem(me + offset, size)
        return pltpu.make_async_remote_copy(
            src_ref=small_out.at[mine, :],
            dst_ref=small_out.at[mine, :],
            send_sem=bc_send.at[offset - 1],
            recv_sem=bc_recv.at[offset - 1],
            device_id={"dp": target},
            device_id_type=pl.DeviceIdType.MESH,
        )

    for offset in range(1, size):
        scatter_copy(offset).start()
    mirror_out(gh_ref, mask_ref, gn_ref, gm_ref, skip_all)
    advance(*LATER[5])
    for t in range(tiles):
        at = pl.ds(t * tile_rows, tile_rows)
        mlp_ref[at, :] = (
            jnp.dot(act_ref[at, :half_hidden], w_out_oth[...], preferred_element_type=F32)
            + jnp.dot(act_ref[at, half_hidden:], w_out_ref[...], preferred_element_type=F32)
            + b_out
        )
    advance(*LATER[6])

    def finish(t, carry):
        at = pl.ds(pl.multiple_of(t * 144, 16), 144)
        images_out(dx_ref, t * 36, 36, images_in(cot_ref, t * 36, 36) + gn_ref[at, :])
        branch = mlp_ref[at, :] * jnp.tile(mask_ref[at, :], (1, channels // 128))
        images_out(block_ref, t * 36, 36, u_ref[at, :] + scale * branch)
        return carry

    lax.fori_loop(0, rows // 144, finish, 0)
    advance(*LATER[7])
    total = small_keep[mine, :]
    for offset in range(1, size):
        scatter_copy(offset).wait_recv()
        total = total + small_recv[offset - 1]
    small_out[mine, :] = total
    for offset in range(1, size):
        spread_copy(offset).start()

    advance(*LATER[8])
    for _ in range(2 * len(stages_of(size)) + 1):
        advance(*range(groups))
    for offset in range(1, size):
        spread_copy(offset).wait_recv()
    for offset in range(1, size):
        scatter_copy(offset).wait_send()
        spread_copy(offset).wait_send()
    for group in range(groups):
        rings[group].close()
        grads_copy(group).wait_send()
    for copy in (pack_copy, first_copy, second_copy, small_pair):
        copy.wait_send()


def final_kernel(
    extent_ref, rate_ref, freq_ref, coef_ref, small_ref, block_hbm, dx_hbm, full_hbm,
    block_out, dx_out, rate_out, freq_out, coef_out, skip_out, gain_out, bias_out, dw_in_out,
    db_in_out, dw_out_out, b_out_out, scale_out,
    mine_ref, dw_in_ref, dw_out_ref, full_ref, block_ref, dx_ref, sems,
):
    channels, half_hidden = dw_in_ref.shape
    groups = half_hidden // CHUNK
    stride = full_ref.shape[0] // groups

    def moves(first, *pairs):
        return [
            pltpu.make_async_copy(source, target, sems.at[first + k])
            for k, (source, target) in enumerate(pairs)
        ]

    reads = moves(0, (full_hbm, full_ref), (block_hbm, block_ref), (dx_hbm, dx_ref))
    writes = moves(3, (dw_in_ref, dw_in_out), (dw_out_ref, dw_out_out), (block_ref, block_out), (dx_ref, dx_out))
    for copy in reads:
        copy.start()
    core = lax.axis_index("mp")
    own = mine_ref.shape[1]
    mine_ref[...] = jnp.where(core == 0, small_ref[0:112, :own], small_ref[0:112, 256 - own :])
    only = pl.ds(pl.multiple_of(core * 128, 128), 128)

    def line(first, count):
        return jnp.concatenate([small_ref[first + k : first + k + 1, only] for k in range(count)], axis=1)

    args = (extent_ref, rate_ref, freq_ref, coef_ref, mine_ref, rate_out, freq_out, coef_out)
    modes_grad(0, *args)
    reads[1].wait()
    writes[2].start()
    reads[2].wait()
    writes[3].start()
    reads[0].wait()
    for group in range(groups):
        base = group * stride
        for k in range(CHUNK // 128):
            at = group * CHUNK + k * 128
            dw_in_ref[:, at : at + 128] = full_ref[base : base + channels, :].astype(F32)
            base += channels
        for k in range(channels // 128):
            dw_out_ref[group * CHUNK : (group + 1) * CHUNK, k * 128 : (k + 1) * 128] = full_ref[
                base : base + CHUNK, :
            ].astype(F32)
            base += CHUNK
    writes[0].start()
    writes[1].start()
    modes_grad(1, *args)
    skip_out[...] = mine_ref[108:109, :].reshape(skip_out.shape)
    db_in_out[...] = line(109, db_in_out.shape[0] // 128).reshape(db_in_out.shape)
    for k, ref in enumerate((gain_out, bias_out, scale_out, b_out_out)):
        ref[...] = line(115 + 3 * k, 3).reshape(ref.shape)
    for copy in writes:
        copy.wait()


ANY = pl.BlockSpec(memory_space=pl.ANY)
VM = pl.BlockSpec(memory_space=pltpu.VMEM)
SM = pl.BlockSpec(memory_space=pltpu.SMEM)


def shape(dims, kind=F32):
    return jax.ShapeDtypeStruct(dims, kind)


def on_device(
    size,
    pixels,
    grid_class,
    extent,
    ssm_rate,
    ssm_freq,
    ssm_coef,
    skip_gain,
    norm_gain,
    norm_bias,
    w_in,
    b_in,
    w_out,
    b_out,
    layer_scale,
    cotangent,
):
    micro, count, channels, cells = pixels.shape
    rows = micro * count * cells
    own = ssm_rate.shape[1]
    modes = ssm_rate.shape[2]
    half_hidden = b_in.shape[0]
    x = pixels.transpose(0, 3, 1, 2)
    cot = cotangent.transpose(0, 3, 1, 2)
    rate = ssm_rate.transpose(0, 2, 1)
    freq = ssm_freq.transpose(0, 2, 1)
    coef = ssm_coef.transpose(0, 2, 1)
    field = (rows, channels)
    grad_rows = 2 * channels * half_hidden // 128
    groups = half_hidden // CHUNK
    all_rows = groups * chunk_rows(grad_rows // groups, size) * size
    stages = stages_of(size)
    hops = (groups, max(len(stages), 1), max([members - 1 for _, members in stages] + [1]))
    small_rows = max(128, 8 * size)
    peers = max(size - 1, 1)
    DMA = pltpu.SemaphoreType.DMA
    block_out, dx, full, small = pl.pallas_call(
        partial(mega_kernel, size),
        out_shape=(
            shape(x.shape, BF16),
            shape(x.shape, BF16),
            shape((all_rows, 128), BF16),
            shape((small_rows, 256)),
        ),
        in_specs=[SM] + [VM] * 10 + [ANY] * 4,
        out_specs=(VM,) * 4,
        scratch_shapes=[
            pltpu.VMEM(x.shape, BF16),
            pltpu.VMEM(x.shape, BF16),
            pltpu.VMEM((WIDE, half_hidden), BF16),
            pltpu.VMEM(w_out.shape, BF16),
            pltpu.VMEM((PACK_ROWS, own), F32),
            pltpu.VMEM((PACK_ROWS, own), F32),
            pltpu.VMEM((WIDE, half_hidden), BF16),
            pltpu.VMEM(w_out.shape, BF16),
            pltpu.VMEM((PACK_ROWS, channels), F32),
            pltpu.VMEM((1, channels), F32),
            pltpu.VMEM((rows, 128), F32),
            pltpu.VMEM((2 * GRID, 8, channels), F32),
            pltpu.VMEM((90, 8, channels), F32),
            pltpu.VMEM((45, 8, channels), F32),
            pltpu.VMEM(field, F32),
            pltpu.VMEM(field, F32),
            pltpu.VMEM(field, F32),
            pltpu.VMEM(field, F32),
            pltpu.VMEM(field, F32),
            pltpu.VMEM((rows, WIDE), BF16),
            pltpu.VMEM(field, BF16),
            pltpu.VMEM((rows, 2 * half_hidden), BF16),
            pltpu.VMEM((rows, 2 * CHUNK), BF16),
            pltpu.VMEM(field, F32),
            pltpu.VMEM(field, F32),
            pltpu.VMEM((rows, 128), F32),
            pltpu.VMEM(field, F32),
            pltpu.VMEM((162 * 8, channels), F32),
            pltpu.VMEM((81 * 8, channels), F32),
            pltpu.VMEM((2, half_hidden), F32),
            pltpu.VMEM((SUM_ROWS, channels), F32),
            pltpu.VMEM((all_rows, 128), F32),
            pltpu.VMEM((grad_rows, 128), BF16),
            pltpu.VMEM((grad_rows, 128), BF16),
            pltpu.VMEM((all_rows, 128), BF16),
            pltpu.VMEM((all_rows, 128), BF16),
            pltpu.VMEM((small_rows, 256), F32),
            pltpu.VMEM((SUM_ROWS, 256), F32),
            pltpu.VMEM((peers, small_rows // size, 256), F32),
            DMA((4 + groups,)),
            DMA((4 + groups,)),
            DMA(hops),
            DMA(hops),
            DMA(hops),
            DMA(hops),
            DMA((peers,)),
            DMA((peers,)),
            DMA((peers,)),
            DMA((peers,)),
            DMA((4,)),
        ],
        compiler_params=pltpu.CompilerParams(
            vmem_limit_bytes=VMEM_LIMIT, collective_id=0, has_side_effects=True
        ),
        name="block",
    )(
        grid_class,
        extent,
        rate,
        freq,
        coef,
        skip_gain,
        b_in,
        norm_gain,
        norm_bias,
        b_out,
        layer_scale,
        w_in,
        w_out,
        x,
        cot,
    )
    (
        block_out, dx, g_rate, g_freq, g_coef, g_skip, g_gain, g_bias, dw_in, db_in, dw_out, g_b_out, g_scale,
    ) = pl.pallas_call(
        final_kernel,
        out_shape=(
            shape(x.shape, BF16),
            shape(x.shape, BF16),
            shape((2, modes, own)),
            shape((2, modes, own)),
            shape((2, modes, own)),
            shape((own,)),
            shape((channels,)),
            shape((channels,)),
            shape(w_in.shape),
            shape((half_hidden,)),
            shape(w_out.shape),
            shape((channels,)),
            shape((channels,)),
        ),
        in_specs=[VM] * 5 + [ANY] * 3,
        out_specs=(ANY, ANY) + (VM,) * 6 + (ANY, VM, ANY, VM, VM),
        scratch_shapes=[
            pltpu.VMEM((112, own), F32),
            pltpu.VMEM(w_in.shape, F32),
            pltpu.VMEM(w_out.shape, F32),
            pltpu.VMEM(full.shape, BF16),
            pltpu.VMEM(x.shape, BF16),
            pltpu.VMEM(x.shape, BF16),
            DMA((7,)),
        ],
        compiler_params=pltpu.CompilerParams(vmem_limit_bytes=VMEM_LIMIT),
        name="final",
    )(extent, rate, freq, coef, small, block_out, dx, full)
    return (
        block_out.transpose(0, 2, 3, 1),
        dx.transpose(0, 2, 3, 1),
        g_rate.transpose(0, 2, 1),
        g_freq.transpose(0, 2, 1),
        g_coef.transpose(0, 2, 1),
        g_skip,
        g_gain,
        g_bias,
        dw_in,
        db_in,
        dw_out,
        g_b_out,
        g_scale,
    )


def solution(mesh):
    placed = (
        P(None, ("dp", "mp"), None, None),
        P(None, "dp"),
        P("mp"),
        P(None, "mp", None),
        P(None, "mp", None),
        P(None, "mp", None),
        P("mp"),
        P(),
        P(),
        P(None, "mp"),
        P("mp"),
        P("mp", None),
        P(),
        P(),
        P(None, ("dp", "mp"), None, None),
    )
    return jax.shard_map(
        partial(on_device, mesh.shape["dp"]),
        mesh=mesh,
        in_specs=placed,
        out_specs=(
            P(None, ("dp", "mp"), None, None),
            P(None, ("dp", "mp"), None, None),
            P(None, "mp", None),
            P(None, "mp", None),
            P(None, "mp", None),
            P("mp"),
            P(),
            P(),
            P(None, "mp"),
            P("mp"),
            P("mp", None),
            P(),
            P(),
        ),
        check_vma=False,
    )
```
